512 devices in a mesh: wide: 32 (over x, y), narrow: 16 (over z, core).
Axes of the slice: x: 4, y: 8, z: 8, core: 2. Of those that a mesh axis runs over, the one named last changes fastest.
Arguments:
- residual: float32 [3, 512, 256, 128], P(None, 'wide', 'narrow'), may hold values from -6 to 6
- stiffness: float32 [512, 256, 128], P('wide', 'narrow'), may hold values from 0.5 to 4
- coupling: float32 [3, 3], replicated, may hold values from -0.25 to 1.5, as said below
Outputs:
- correction: float32 [3, 512, 256, 128], P(None, 'wide', 'narrow')
The draws below stay inside these ranges and needn't reach their ends.
Inputs may be any that keep to these rules, and one draw needn't show every extreme that they name: The coupling matrix is symmetric, its diagonal entries lie between 1 and 1.5 and its off-diagonal entries between -0.25 and 0.25.
All inputs are finite; a program needn't handle non-finite values.
Results may differ from the reference program's by a relative error of at most 0.0001.
Values sent between devices are 32-bit elements; how exact they have to be, the bound alone decides.
A program may use at most 128 MiB of HBM per device.

```python
import math
import jax
import jax.numpy as jnp
from jax import lax

LEVELS = 4
NX = 512
NY = 256
NZ = 128


def draw_residual(key, part):
    key = jax.random.fold_in(key, 11)
    values = jax.random.normal(key, (3, NX, NY, NZ), jnp.float32)
    return jnp.clip(values, -6.0, 6.0)


def draw_coupling(key, part):
    key = jax.random.fold_in(key, 23)
    diagonal = jax.random.uniform(jax.random.fold_in(key, 1), (3,), jnp.float32, 1.0, 1.5)
    offdiag = jax.random.uniform(jax.random.fold_in(key, 2), (3, 3), jnp.float32, -0.25, 0.25)
    symmetric = (offdiag + offdiag.T) * 0.5
    identity = jnp.eye(3, dtype=jnp.float32)
    return symmetric * (1.0 - identity) + identity * diagonal[None, :]


def level_of(key, shape, shards, smallest, high):
    loudness = 1.0
    for dim, shards_of in shards:
        draws = jax.random.uniform(jax.random.fold_in(jax.random.fold_in(key, 6), dim), (shards_of,), jnp.float32, smallest / len(shards), high / len(shards))
        loudness = loudness * jnp.repeat(jnp.exp(draws), shape[dim] // shards_of).reshape((-1,) + (1,) * (len(shape) - 1 - dim))
    return loudness


def setup_inputs(seed: int = 0) -> dict:
    seeds = jax.random.split(jax.random.key(seed), 4)
    return {
        "residual": draw_residual(jax.random.fold_in(seeds[3], 71), 0),
        "stiffness": jnp.clip(jnp.exp(math.log(4.0) - 2.0794415 * jax.random.uniform(seeds[1], (NX, NY, NZ), jnp.float32) ** level_of(seeds[1], (NX, NY, NZ), ((0, 32), (1, 16)), -0.2, 0.2)), 0.5, 4.0),
        "coupling": draw_coupling(jax.random.fold_in(seeds[3], 71), 0),
    }


mass_coef = 0.001
ratio_bound = 8.0


def chebyshev_terms(level_idx):
    bound_top = 4.0 * (2.8 / 4.0 ** level_idx + mass_coef)
    bound_low = bound_top / ratio_bound
    mid_value = (bound_top + bound_low) / 2.0
    half_width = (bound_top - bound_low) / 2.0
    return mid_value, half_width, mid_value / half_width


def box_sum(field):
    padded = jnp.pad(field, ((0, 0), (1, 1), (1, 1), (1, 1)))
    summed = padded[:, :-2] + padded[:, 1:-1] + padded[:, 2:]
    summed = summed[:, :, :-2] + summed[:, :, 1:-1] + summed[:, :, 2:]
    return summed[..., :-2] + summed[..., 1:-1] + summed[..., 2:]


def apply_op(field, stiff_now, level_idx, coupling):
    laplace = field - (box_sum(field) - field) / 26.0
    blended = jnp.tensordot(coupling, laplace, axes=1, precision=lax.Precision.HIGHEST)
    return stiff_now[None] * (blended / 4.0 ** level_idx + mass_coef * field)


def smooth(source, stiff_now, level_idx, coupling, want_rest):
    mid_value, half_width, sigma_val = chebyshev_terms(level_idx)
    remains = source
    step_dir = remains / mid_value
    iterate = step_dir
    rho_now = 1.0 / sigma_val
    for sweep in range(3):
        remains = remains - apply_op(step_dir, stiff_now, level_idx, coupling)
        rho_next = 1.0 / (2.0 * sigma_val - rho_now)
        step_dir = (rho_next * rho_now) * step_dir + (2.0 * rho_next / half_width) * remains
        iterate = iterate + step_dir
        rho_now = rho_next
    if want_rest:
        remains = remains - apply_op(step_dir, stiff_now, level_idx, coupling)
    return iterate, remains


def restrict(field):
    shape = field.shape
    lead = shape[:-3]
    blocks = field.reshape(lead + (shape[-3] // 2, 2, shape[-2] // 2, 2, shape[-1] // 2, 2))
    return jnp.mean(blocks, axis=(-5, -3, -1))


def prolong(field):
    for axis_pos in (-3, -2, -1):
        field = jnp.repeat(field, 2, axis=axis_pos)
    return field


def reference(residual, stiffness, coupling):
    stiff_list = [stiffness]
    for level_idx in range(LEVELS):
        stiff_list.append(restrict(stiff_list[-1]))
    source = residual
    iterates = []
    for level_idx in range(LEVELS + 1):
        iterate, remains = smooth(source, stiff_list[level_idx], level_idx, coupling, level_idx < LEVELS)
        iterates.append(iterate)
        if level_idx < LEVELS:
            source = restrict(remains)
    correction = iterates[LEVELS]
    for level_idx in reversed(range(LEVELS)):
        correction = iterates[level_idx] + prolong(correction)
    return correction
```

```python
import functools

import jax
import jax.numpy as jnp
from jax import lax
from jax.experimental import pallas as pl
from jax.experimental.pallas import tpu as pltpu
from jax.sharding import PartitionSpec as P

LEVELS = 4
MASS = 0.001
RATIO = 8.0
MESH = pl.DeviceIdType.MESH
NEIGHBOURS = [(1, 0), (-1, 0), (0, 1), (0, -1), (1, 1), (1, -1), (-1, 1), (-1, -1)]
WINDOW = [o for k in range(1, 6) for o in (k, -k)]
F32 = jnp.float32
BF16 = jnp.bfloat16


def chebyshev(level):
    top = 4.0 * (2.8 / 4.0**level + MASS)
    theta = (top + top / RATIO) / 2.0
    delta = (top - top / RATIO) / 2.0
    sigma = theta / delta
    rho = 1.0 / sigma
    steps = []
    for _ in range(3):
        nxt = 1.0 / (2.0 * sigma - rho)
        steps.append((nxt * rho, 2.0 * nxt / delta))
        rho = nxt
    return theta, steps


def iota(shape, dim):
    return lax.broadcasted_iota(jnp.int32, shape, dim)


def indicator(cond, value=1.0):
    return jnp.where(cond, value, 0.0).astype(BF16)


def mm(v, w):
    hi = v.astype(BF16)
    lo = (v - hi.astype(F32)).astype(BF16)
    return jnp.dot(hi, w, preferred_element_type=F32) + jnp.dot(
        lo, w, preferred_element_type=F32
    )


def mix(coup, scale, mass, u, d, k):
    out = []
    for c in range(3):
        a = (coup[c][0] * scale) * u[0]
        a = a + (coup[c][1] * scale) * u[1]
        a = a + (coup[c][2] * scale) * u[2]
        a = a + mass * d[c]
        out.append(k * a)
    return out


def flat_box(chunks, nz):
    rows = chunks[0].shape[0]
    lane = iota(chunks[0].shape, 1)
    zpos = lane & (nz - 1)
    s = []
    for v in chunks:
        v = v + pltpu.roll(v, 1, 0) + pltpu.roll(v, rows - 1, 0)
        s.append(
            v
            + jnp.where(zpos == 0, 0.0, pltpu.roll(v, 1, 1))
            + jnp.where(zpos == nz - 1, 0.0, pltpu.roll(v, 127, 1))
        )
    up = [pltpu.roll(v, nz, 1) for v in s]
    down = [pltpu.roll(v, 128 - nz, 1) for v in s]
    out = []
    for j, v in enumerate(s):
        before = up[j - 1] if j > 0 else 0.0
        after = down[j + 1] if j + 1 < len(s) else 0.0
        out.append(
            v
            + jnp.where(lane < nz, before, up[j])
            + jnp.where(lane >= 128 - nz, after, down[j])
        )
    return out


def flat_smooth(f, kappa, coup, level, nz, want_rest):
    theta, steps = chebyshev(level)
    scale = 4.0**-level / 26.0
    n = len(kappa)

    def apply(r, d):
        boxes = [flat_box(d[c], nz) for c in range(3)]
        new = [[None] * n for _ in range(3)]
        for j in range(n):
            u = [27.0 * d[c][j] - boxes[c][j] for c in range(3)]
            a = mix(coup, scale, MASS, u, [d[c][j] for c in range(3)], kappa[j])
            for c in range(3):
                new[c][j] = r[c][j] - a[c]
        return new

    r = f
    d = [[v * (1.0 / theta) for v in f[c]] for c in range(3)]
    x = d
    for a, b in steps:
        r = apply(r, d)
        d = [[a * d[c][j] + b * r[c][j] for j in range(n)] for c in range(3)]
        x = [[x[c][j] + d[c][j] for j in range(n)] for c in range(3)]
    if want_rest:
        r = apply(r, d)
    return x, r


def kernel(
    nw,
    nn,
    res,
    stiff,
    coup_ref,
    acc_out,
    tail_out,
    f0,
    k0,
    r0,
    d1,
    d2,
    d3,
    acc,
    t0,
    g1,
    r1,
    e1,
    w1,
    e2,
    w2,
    t1,
    u_lo,
    u_hi,
    g2,
    t2,
    v2,
    h3,
    h3s,
    t3,
    z4,
    m01,
    m12,
    m23,
    m34,
    p1,
    p2,
    p34,
    local_sem,
    s0,
    q0,
    s1,
    q1,
    s2,
    q2,
    s3,
    q3,
    s4,
    q4,
):
    w = lax.axis_index("wide")
    n = lax.axis_index("narrow")

    def there(ow, on):
        ok = None
        for pos, off, size in ((w, ow, nw), (n, on, nn)):
            if off > 0:
                c = pos + off < size
            elif off < 0:
                c = pos + off >= 0
            else:
                continue
            ok = c if ok is None else jnp.logical_and(ok, c)
        return ok

    def remote(src, dst, send, recv, ow, on):
        return pltpu.make_async_remote_copy(
            src_ref=src,
            dst_ref=dst,
            send_sem=send,
            recv_sem=recv,
            device_id={"wide": w + ow, "narrow": n + on},
            device_id_type=MESH,
        )

    own_f = pltpu.make_async_copy(res, f0.at[:, 4:20, 0:16, :], local_sem.at[0])
    own_k = pltpu.make_async_copy(stiff, k0.at[4:20, 0:16, :], local_sem.at[1])
    own_k.start()
    own_f.start()

    g1[...] = jnp.zeros_like(g1)
    g2[...] = jnp.zeros_like(g2)
    h3[...] = jnp.zeros_like(h3)
    h3s[...] = jnp.zeros_like(h3s)

    barrier = pltpu.get_barrier_semaphore()
    partners = NEIGHBOURS + [(o, 0) for o in WINDOW if abs(o) > 1]
    partners += [(0, o) for o in WINDOW if abs(o) > 1]
    count = 0
    for ow, on in partners:
        ok = there(ow, on)
        count = count + jnp.where(ok, 1, 0)

        @pl.when(ok)
        def _(ow=ow, on=on):
            pl.semaphore_signal(
                barrier,
                inc=1,
                device_id={"wide": w + ow, "narrow": n + on},
                device_id_type=MESH,
            )

    pl.semaphore_wait(barrier, count)

    def copies0(i, ow, on):
        sx, dx = {0: ((0, 16), (4, 20)), 1: ((12, 16), (0, 4)), -1: ((0, 4), (20, 24))}[ow]
        sy, dy = {0: ((0, 16), (0, 16)), 1: ((12, 16), (20, 24)), -1: ((0, 4), (16, 20))}[on]
        sx, dx, sy, dy = slice(*sx), slice(*dx), slice(*sy), slice(*dy)
        return (
            remote(res.at[:, sx, sy, :], f0.at[:, dx, dy, :], s0.at[i], q0.at[i], ow, on),
            remote(stiff.at[sx, sy, :], k0.at[dx, dy, :], s0.at[8 + i], q0.at[8 + i], ow, on),
        )

    def copies1(i, ow, on):
        sx, dx = {0: ((2, 6), (2, 6)), 1: ((4, 6), (0, 2)), -1: ((2, 4), (6, 8))}[ow]
        sy, dy = {0: ((0, 8), (0, 8)), 1: ((4, 8), (12, 16)), -1: ((0, 4), (8, 12))}[on]
        sx, dx, sy, dy = slice(*sx), slice(*dx), slice(*sy), slice(*dy)
        return (
            remote(g1.at[:, sx, sy, :], g1.at[:, dx, dy, :], s1.at[i], q1.at[i], ow, on),
        )

    def copies2(i, ow, on):
        dx = slice(4 - 4 * ow, 8 - 4 * ow)
        dy = slice(128 - 128 * on, 256 - 128 * on)
        return (
            remote(g2.at[:, 4:8, 128:256], g2.at[:, dx, dy], s2.at[i], q2.at[i], ow, on),
        )

    def copies3(i, ow, on):
        rows = slice(10 - 2 * ow, 12 - 2 * ow)
        return (remote(h3.at[10:12, :], h3.at[rows, :], s3.at[i], q3.at[i], ow, on),)

    def copies4(i, ow, on):
        return (remote(h3, h3s.at[5 - on], s4.at[i], q4.at[i], ow, on),)

    def start(copies, offsets, chosen=None):
        for i, (ow, on) in enumerate(offsets):
            if chosen is None or i in chosen:

                @pl.when(there(ow, on))
                def _(i=i, ow=ow, on=on):
                    for c in copies(i, ow, on):
                        c.start()

    def arrive(copies, offsets, chosen=None):
        for i, (ow, on) in enumerate(offsets):
            if chosen is None or i in chosen:

                @pl.when(there(-ow, -on))
                def _(i=i, ow=ow, on=on):
                    for c in copies(i, ow, on):
                        c.wait_recv()

    def sent(copies, offsets):
        for i, (ow, on) in enumerate(offsets):

            @pl.when(there(ow, on))
            def _(i=i, ow=ow, on=on):
                for c in copies(i, ow, on):
                    c.wait_send()

    along_wide = [(o, 0) for o in WINDOW]
    along_narrow = [(0, o) for o in WINDOW]

    start(copies0, NEIGHBOURS)

    @pl.when(w == 0)
    def _():
        f0[:, 0:4] = jnp.zeros((3, 4, 24, 128), F32)
        k0[0:4] = jnp.zeros((4, 24, 128), F32)

    @pl.when(w == nw - 1)
    def _():
        f0[:, 20:24] = jnp.zeros((3, 4, 24, 128), F32)
        k0[20:24] = jnp.zeros((4, 24, 128), F32)

    @pl.when(n == 0)
    def _():
        f0[:, :, 20:24, :] = jnp.zeros((3, 24, 4, 128), F32)
        k0[:, 20:24, :] = jnp.zeros((24, 4, 128), F32)

    @pl.when(n == nn - 1)
    def _():
        f0[:, :, 16:20, :] = jnp.zeros((3, 24, 4, 128), F32)
        k0[:, 16:20, :] = jnp.zeros((24, 4, 128), F32)

    r, c = iota((256, 128), 0), iota((256, 128), 1)
    m01[...] = indicator(((r >> 7) == (c >> 6)) & (((r & 127) >> 1) == (c & 63)), 0.125)
    r, c = iota((512, 128), 0), iota((512, 128), 1)
    m12[...] = indicator(((r >> 7) == (c >> 5)) & (((r & 63) >> 1) == (c & 31)), 0.125)
    m23[...] = indicator(
        ((r >> 7) == (c >> 5))
        & (((r >> 6) & 1) == ((c >> 4) & 1))
        & (((r & 31) >> 1) == (c & 15)),
        0.125,
    )
    r, c = iota((384, 128), 0), iota((384, 128), 1)
    m34[...] = indicator(((r >> 5) == (c >> 3)) & (((r & 15) >> 1) == (c & 7)), 0.125)
    r, c = iota((128, 256), 0), iota((128, 256), 1)
    p1[...] = indicator(((r >> 6) == (c >> 7)) & ((r & 63) == ((c & 127) >> 1)))
    r, c = iota((128, 512), 0), iota((128, 512), 1)
    p2[...] = indicator(((r >> 5) == (c >> 7)) & ((r & 31) == ((c & 127) >> 2)))
    r, c = iota((256, 256), 0), iota((256, 256), 1)
    fine = ((r >> 4) == (2 + (c >> 7))) & ((r & 15) == ((c & 127) >> 3))
    coarse = (r >= 128 + 40) & (r < 128 + 48) & ((r & 7) == ((c & 127) >> 4))
    p34[...] = indicator(fine | coarse)

    coup = [[coup_ref[i, j] for j in range(3)] for i in range(3)]

    own_k.wait()
    for i in range(8):
        t0[pl.ds(384 + 16 * i, 16), :] = (
            k0[4 + 2 * i, 0:16, :] + k0[5 + 2 * i, 0:16, :]
        )

    theta0, steps0 = chebyshev(0)
    lane24 = iota((24, 128), 1)

    def plane0(i, d, k_of, scale, mass):
        us, ds_ = [], []
        for c in range(3):
            mid = d[c, i]
            s = d[c, i - 1] + mid + d[c, i + 1]
            s = s + pltpu.roll(s, 1, 0) + pltpu.roll(s, 23, 0)
            s = (
                s
                + jnp.where(lane24 == 0, 0.0, pltpu.roll(s, 1, 1))
                + jnp.where(lane24 == 127, 0.0, pltpu.roll(s, 127, 1))
            )
            us.append(27.0 * mid - s)
            ds_.append(mid)
        return ds_, mix(coup, scale, mass, us, ds_, k_of[i])

    fields = [f0, d1, d2, d3]

    def sweep0(k, lo, pairs):
        d = fields[k]
        over = 1.0 / theta0 if k == 0 else 1.0
        scale, mass = over / 26.0, over * MASS
        rest = f0 if k == 0 else r0

        def body(t, carry):
            both = []
            for u in range(2):
                i = lo + 2 * t + u
                mids, a = plane0(i, d, k0, scale, mass)
                new = [rest[c, i] - a[c] for c in range(3)]
                if k < 3:
                    ca, cb = steps0[k]
                    for c in range(3):
                        r0[c, i] = new[c]
                        fields[k + 1][c, i] = (ca * over) * mids[c] + cb * new[c]
                both.append(new)
            if k == 3:
                half = (lo - 4) // 2 + t
                for c in range(3):
                    rows = pl.multiple_of(128 * c + 16 * half, 16)
                    t0[pl.ds(rows, 16), :] = both[0][c][0:16] + both[1][c][0:16]
            return carry

        lax.fori_loop(0, pairs, body, 0)

    own_f.wait()
    arrive(copies0, NEIGHBOURS, (2, 3))
    for k in range(4):
        sweep0(k, 5 + k, 7 - k) if k < 3 else sweep0(3, 8, 4)
    arrive(copies0, NEIGHBOURS, (0, 1, 4, 5, 6, 7))
    for k in range(4):
        sweep0(k, 1 + k, 2)
        sweep0(k, 19 - k, 2)

    s = t0[pl.ds(0, 256, stride=2), :] + t0[pl.ds(1, 256, stride=2), :]
    s = s.reshape(4, 4, 2, 8, 128)
    pair = jnp.concatenate(
        [s[:, :, 0].reshape(128, 128), s[:, :, 1].reshape(128, 128)], axis=1
    )
    g1[:, 2:6, 0:8, :] = mm(pair, m01[...]).reshape(4, 4, 8, 128)
    start(copies1, NEIGHBOURS)

    def sum0(i, carry):
        for c in range(3):
            acc[c, i] = (
                f0[c, 4 + i, 0:16, :] * (1.0 / theta0)
                + d1[c, 4 + i, 0:16, :]
                + d2[c, 4 + i, 0:16, :]
                + d3[c, 4 + i, 0:16, :]
            )
        return carry

    lax.fori_loop(0, 16, sum0, 0)

    arrive(copies1, NEIGHBOURS)

    theta1, steps1 = chebyshev(1)
    lane16 = iota((16, 128), 1)
    lower = lane16 < 64
    zpos1 = lane16 & 63
    for p in range(8):
        for c in range(3):
            w1[c, p] = pltpu.roll(g1[c, p], 64, 1)

    def plane1(p, d, wd, scale, mass):
        us, mids = [], []
        for c in range(3):
            mid = d[c, p]
            before = wd[c, max(p - 1, 0)]
            after = wd[c, min(p + 1, 7)]
            s = mid + wd[c, p] + jnp.where(lower, before, after)
            s = s + pltpu.roll(s, 1, 0) + pltpu.roll(s, 15, 0)
            s = (
                s
                + jnp.where(zpos1 == 0, 0.0, pltpu.roll(s, 1, 1))
                + jnp.where(zpos1 == 63, 0.0, pltpu.roll(s, 127, 1))
            )
            us.append(27.0 * mid - s)
            mids.append(mid)
        return mids, mix(coup, scale, mass, us, mids, g1[3, p])

    x1 = {}
    pairs1 = [(g1, w1), (e1, w2), (e2, w1), (e1, w2)]
    for k, (lo, hi) in enumerate([(0, 8), (1, 7), (1, 7), (2, 6)]):
        d, wd = pairs1[k]
        over = 1.0 / theta1 if k == 0 else 1.0
        scale, mass = over / (4.0 * 26.0), over * MASS
        for p in range(lo, hi):
            mids, a = plane1(p, d, wd, scale, mass)
            for c in range(3):
                new = (g1 if k == 0 else r1)[c, p] - a[c]
                if k < 3:
                    ca, cb = steps1[k]
                    nd, nwd = pairs1[k + 1]
                    r1[c, p] = new
                    step = (ca * over) * mids[c] + cb * new
                    nd[c, p] = step
                    nwd[c, p] = pltpu.roll(step, 64, 1)
                else:
                    t1[pl.ds(32 * c + 8 * (p - 2), 8), :] = new[0:8]
                if 2 <= p < 6:
                    part = (mids[c] * over)[0:8]
                    x1[c, p] = part if k == 0 else x1[c, p] + part
    for p in range(4):
        t1[pl.ds(96 + 8 * p, 8), :] = g1[3, 2 + p, 0:8, :]

    ys = [t1[pl.ds(y, 16, stride=8), :] for y in range(8)]
    ys = jnp.concatenate([ys[2 * j] + ys[2 * j + 1] for j in range(4)], axis=1)
    blk = mm(ys, m12[...])
    for c in range(4):
        g2[c, 4:8, 128:256] = blk[4 * c : 4 * c + 4]
    start(copies2, NEIGHBOURS)

    rows = jnp.concatenate([x1[c, p] for c in range(3) for p in range(2, 6)], axis=0)
    rep = mm(rows, p1[...])
    u_lo[pl.ds(0, 96, stride=2), :] = rep[:, 0:128]
    u_lo[pl.ds(1, 96, stride=2), :] = rep[:, 0:128]
    u_hi[pl.ds(0, 96, stride=2), :] = rep[:, 128:256]
    u_hi[pl.ds(1, 96, stride=2), :] = rep[:, 128:256]
    for c in range(3):
        for p in range(4):
            rows_cp = pl.ds(16 * (4 * c + p), 16)
            for j in range(4):
                acc[c, 4 * p + j] += (u_lo if j < 2 else u_hi)[rows_cp, :]

    arrive(copies2, NEIGHBOURS)
    f2 = [[g2[c, :, 128 * j : 128 * j + 128] for j in range(3)] for c in range(4)]
    x2, r2 = flat_smooth(f2[:3], f2[3], coup, 2, 32, True)

    t2[...] = mm(
        jnp.concatenate([r2[0][1], r2[1][1], r2[2][1], f2[3][1]], axis=1), m23[...]
    )
    h3[10:12, :] = t2[pl.ds(4, 2, stride=2), :] + t2[pl.ds(5, 2, stride=2), :]
    start(copies3, along_wide)

    for c in range(3):
        t3[4 * c : 4 * c + 4, 0:128] = x2[c][1][4:8]
    rep = mm(t3[0:16, 0:128], p2[...])
    for y in range(16):
        j = y // 4
        v2[pl.ds(y, 16, stride=16), :] = rep[:, 128 * j : 128 * j + 128]
    for c in range(3):
        for k in range(4):
            part = v2[pl.ds(16 * (4 * c + k), 16), :]
            for j in range(4):
                acc[c, 4 * k + j] += part
    whole = pltpu.make_async_copy(acc, acc_out, local_sem.at[2])
    whole.start()

    arrive(copies3, along_wide)
    start(copies4, along_narrow)
    arrive(copies4, along_narrow)

    lane3 = iota((24, 128), 1)
    slots = [h3s[j] if j != 5 else h3[...] for j in range(11)]
    f3 = [[None] * 3 for _ in range(4)]
    for c in range(4):
        for v in range(3):
            out = jnp.zeros((24, 128), F32)
            for q in range(4):
                j = 4 * v + q
                if j < 11:
                    turn = 32 * ((q - c) % 4)
                    part = pltpu.roll(slots[j], turn, 1) if turn else slots[j]
                    out = jnp.where((lane3 >> 5) == q, part, out)
            f3[c][v] = out
    x3, r3 = flat_smooth(f3[:3], f3[3], coup, 3, 16, True)

    for c in range(4):
        src = jnp.concatenate(r3[c] if c < 3 else f3[3], axis=1)
        t3[24 * c : 24 * c + 24, :] = src
    s = mm(t3[...], m34[...])
    z4[...] = s
    s = z4[pl.ds(0, 48, stride=2), :] + z4[pl.ds(1, 48, stride=2), :]
    pad = jnp.zeros((4, 128), F32)
    f4 = [[jnp.concatenate([s[12 * c : 12 * c + 12], pad], axis=0)] for c in range(4)]
    x4, _ = flat_smooth(f4[:3], f4[3], coup, 4, 8, False)

    for c in range(3):
        t3[2 * c : 2 * c + 2, 0:128] = x3[c][1][10:12]
        t3[2 * c : 2 * c + 2, 128:256] = jnp.broadcast_to(x4[c][0][5:6], (2, 128))
    tail_out[...] = mm(t3[0:16, 0:256], p34[...])[0:8]

    whole.wait()
    sent(copies0, NEIGHBOURS)
    sent(copies1, NEIGHBOURS)
    sent(copies2, NEIGHBOURS)
    sent(copies3, along_wide)
    sent(copies4, along_narrow)


def solution(mesh):
    nw, nn = mesh.shape["wide"], mesh.shape["narrow"]

    def vm(*shape):
        return pltpu.VMEM(shape, F32)

    def mat(*shape):
        return pltpu.VMEM(shape, BF16)

    dma = pltpu.SemaphoreType.DMA
    scratch = [
        vm(3, 24, 24, 128),
        vm(24, 24, 128),
        vm(3, 24, 24, 128),
        vm(3, 24, 24, 128),
        vm(3, 24, 24, 128),
        vm(3, 24, 24, 128),
        vm(3, 16, 16, 128),
        vm(512, 128),
        vm(4, 8, 16, 128),
        vm(3, 8, 16, 128),
        vm(3, 8, 16, 128),
        vm(3, 8, 16, 128),
        vm(3, 8, 16, 128),
        vm(3, 8, 16, 128),
        vm(128, 128),
        vm(192, 128),
        vm(192, 128),
        vm(4, 16, 384),
        vm(16, 128),
        vm(256, 128),
        vm(24, 128),
        vm(11, 24, 128),
        vm(96, 384),
        vm(96, 128),
        mat(256, 128),
        mat(512, 128),
        mat(512, 128),
        mat(384, 128),
        mat(128, 256),
        mat(128, 512),
        mat(256, 256),
        dma((3,)),
        dma((16,)),
        dma((16,)),
        dma((8,)),
        dma((8,)),
        dma((8,)),
        dma((8,)),
        dma((10,)),
        dma((10,)),
        dma((10,)),
        dma((10,)),
    ]

    def per_device(residual, stiffness, coupling):
        any_space = pl.BlockSpec(memory_space=pl.ANY)
        acc, tail = pl.pallas_call(
            functools.partial(kernel, nw, nn),
            out_shape=(
                jax.ShapeDtypeStruct((3, 16, 16, 128), F32),
                jax.ShapeDtypeStruct((8, 256), F32),
            ),
            in_specs=[any_space, any_space, pl.BlockSpec(memory_space=pltpu.SMEM)],
            out_specs=(any_space, pl.BlockSpec(memory_space=pltpu.VMEM)),
            scratch_shapes=scratch,
            compiler_params=pltpu.CompilerParams(
                collective_id=0,
                has_side_effects=True,
                vmem_limit_bytes=32 * 1024 * 1024,
            ),
        )(residual, stiffness, coupling)
        tail = tail[0:6].reshape(3, 2, 1, 2, 1, 128)
        return (acc.reshape(3, 2, 8, 2, 8, 128) + tail).reshape(3, 16, 16, 128)

    return jax.shard_map(
        per_device,
        mesh=mesh,
        in_specs=(P(None, "wide", "narrow", None), P("wide", "narrow", None), P()),
        out_specs=P(None, "wide", "narrow", None),
        check_vma=False,
    )
```

```python
import functools

import jax
import jax.numpy as jnp
from jax import lax
from jax.experimental import pallas as pl
from jax.experimental.pallas import tpu as pltpu
from jax.sharding import PartitionSpec as P

LEVELS = 4
MASS = 0.001
RATIO = 8.0
MESH = pl.DeviceIdType.MESH
NEIGHBOURS = [(1, 1), (1, -1), (-1, 1), (-1, -1), (1, 0), (-1, 0), (0, 1), (0, -1)]
WINDOW = [o for k in range(5, 0, -1) for o in (k, -k)]
F32 = jnp.float32
BF16 = jnp.bfloat16


def chebyshev(level):
    top = 4.0 * (2.8 / 4.0**level + MASS)
    theta = (top + top / RATIO) / 2.0
    delta = (top - top / RATIO) / 2.0
    sigma = theta / delta
    rho = 1.0 / sigma
    steps = []
    for _ in range(3):
        nxt = 1.0 / (2.0 * sigma - rho)
        steps.append((nxt * rho, 2.0 * nxt / delta))
        rho = nxt
    return theta, steps


def iota(shape, dim):
    return lax.broadcasted_iota(jnp.int32, shape, dim)


def indicator(cond, value=1.0):
    return jnp.where(cond, value, 0.0).astype(BF16)


def mm(v, w):
    hi = v.astype(BF16)
    lo = (v - hi.astype(F32)).astype(BF16)
    return jnp.dot(hi, w, preferred_element_type=F32) + jnp.dot(
        lo, w, preferred_element_type=F32
    )


def mix(coup, scale, mass, u, d, k):
    out = []
    for c in range(3):
        a = (coup[c][0] * scale) * u[0]
        a = a + (coup[c][1] * scale) * u[1]
        a = a + (coup[c][2] * scale) * u[2]
        a = a + mass * d[c]
        out.append(k * a)
    return out


def flat_box(chunks, nz):
    rows = chunks[0].shape[0]
    lane = iota(chunks[0].shape, 1)
    zpos = lane & (nz - 1)
    s = []
    for v in chunks:
        v = v + pltpu.roll(v, 1, 0) + pltpu.roll(v, rows - 1, 0)
        s.append(
            v
            + jnp.where(zpos == 0, 0.0, pltpu.roll(v, 1, 1))
            + jnp.where(zpos == nz - 1, 0.0, pltpu.roll(v, 127, 1))
        )
    up = [pltpu.roll(v, nz, 1) for v in s]
    down = [pltpu.roll(v, 128 - nz, 1) for v in s]
    out = []
    for j, v in enumerate(s):
        before = up[j - 1] if j > 0 else 0.0
        after = down[j + 1] if j + 1 < len(s) else 0.0
        out.append(
            v
            + jnp.where(lane < nz, before, up[j])
            + jnp.where(lane >= 128 - nz, after, down[j])
        )
    return out


def flat_smooth(f, kappa, coup, level, nz, want_rest):
    theta, steps = chebyshev(level)
    scale = 4.0**-level / 26.0
    n = len(kappa)

    def apply(r, d):
        boxes = [flat_box(d[c], nz) for c in range(3)]
        new = [[None] * n for _ in range(3)]
        for j in range(n):
            u = [27.0 * d[c][j] - boxes[c][j] for c in range(3)]
            a = mix(coup, scale, MASS, u, [d[c][j] for c in range(3)], kappa[j])
            for c in range(3):
                new[c][j] = r[c][j] - a[c]
        return new

    r = f
    d = [[v * (1.0 / theta) for v in f[c]] for c in range(3)]
    x = d
    for a, b in steps:
        r = apply(r, d)
        d = [[a * d[c][j] + b * r[c][j] for j in range(n)] for c in range(3)]
        x = [[x[c][j] + d[c][j] for j in range(n)] for c in range(3)]
    if want_rest:
        r = apply(r, d)
    return x, r


def kernel(
    nw,
    nn,
    res,
    stiff,
    coup_hbm,
    acc,
    tail_out,
    f0b,
    k0b,
    r0,
    d1,
    d2,
    d3,
    t0,
    g1b,
    r1,
    e1,
    w1,
    e2,
    w2,
    t1,
    u_lo,
    u_hi,
    g2b,
    t2,
    v2,
    h3b,
    h3sb,
    t3,
    z4,
    m01,
    m12,
    m23,
    m34,
    p1,
    p2,
    p34,
    coup_ref,
    local_sem,
    s0,
    q0,
    s1,
    q1,
    s2,
    q2,
    s3,
    q3,
    s4,
    q4,
):
    w = lax.axis_index("wide")
    n = lax.axis_index("narrow")
    f0, k0, g1, g2, h3, h3s = (b.at[0] for b in (f0b, k0b, g1b, g2b, h3b, h3sb))

    def pair_of(i):
        return i + 1 - 2 * lax.rem(i, 2)

    def out_of(pos, off, size):
        if off == 0:
            return jnp.bool_(False)
        return pos + off >= size if off > 0 else pos + off < 0

    targets = {}

    def target(ow, on):
        if (ow, on) in targets:
            return targets[ow, on]
        w_out, n_out = out_of(w, ow, nw), out_of(n, on, nn)
        if on == 0:
            tw = jnp.where(w_out, w, w + ow)
            tn = jnp.where(w_out, pair_of(n), n)
            away = w_out
        elif ow == 0:
            tw = jnp.where(n_out, pair_of(w), w)
            tn = jnp.where(n_out, n, n + on)
            away = n_out
        else:
            w_end, n_end = (nw - 1 if ow > 0 else 0), (nn - 1 if on > 0 else 0)
            both = jnp.logical_and(w_out, n_out)
            away = jnp.logical_or(w_out, n_out)
            w_near, n_near = w == w_end - ow, n == n_end - on
            tw = jnp.where(
                both,
                w - ow,
                jnp.where(
                    w_out,
                    w,
                    jnp.where(n_out, jnp.where(w_near, w + ow, pair_of(w)), w + ow),
                ),
            )
            tn = jnp.where(
                both,
                n,
                jnp.where(
                    w_out,
                    jnp.where(n_near, n + on, pair_of(n)),
                    jnp.where(n_out, jnp.where(w_near, n - on, n), n + on),
                ),
            )
        targets[ow, on] = tw, tn, jnp.where(away, 1, 0)
        return targets[ow, on]

    def remote(src, dst, where, send, recv, sems, ow, on):
        tw, tn, away = target(ow, on)
        mine, other = sems
        return pltpu.make_async_remote_copy(
            src_ref=src,
            dst_ref=dst.at[(away,) + where],
            send_sem=send.at[mine],
            recv_sem=recv.at[mine + (other - mine) * away],
            device_id={"wide": tw, "narrow": tn},
            device_id_type=MESH,
        )

    def landed(buf, where, send, recv, mine):
        return pltpu.make_async_remote_copy(
            src_ref=buf.at[(0,) + where],
            dst_ref=buf.at[(0,) + where],
            send_sem=send.at[mine],
            recv_sem=recv.at[mine],
            device_id={"wide": w, "narrow": n},
            device_id_type=MESH,
        )

    g1[...] = jnp.zeros_like(g1)
    g2[...] = jnp.zeros_like(g2)
    h3[...] = jnp.zeros_like(h3)
    h3s[...] = jnp.zeros_like(h3s)

    barrier = pltpu.get_barrier_semaphore()
    near = NEIGHBOURS + [(2, 0), (-2, 0), (0, 2), (0, -2)]
    for ow, on in near:
        tw, tn, _ = target(ow, on)
        pl.semaphore_signal(
            barrier,
            inc=1,
            device_id={"wide": tw, "narrow": tn},
            device_id_type=MESH,
        )

    own_f = pltpu.make_async_copy(res, f0.at[:, 4:20, 0:16, :], local_sem.at[0])
    own_k = pltpu.make_async_copy(stiff, k0.at[4:20, 0:16, :], local_sem.at[1])
    own_c = pltpu.make_async_copy(coup_hbm, coup_ref, local_sem.at[2])
    own_k.start()
    own_f.start()
    own_c.start()

    pl.semaphore_wait(barrier, len(near))

    def copies0(i, ow, on):
        sx, dx = {0: (0, 4), 1: (12, 0), -1: (0, 20)}[ow]
        sy, dy = {0: (0, 0), 1: (12, 20), -1: (0, 16)}[on]
        nx, ny = (16 if ow == 0 else 4), (16 if on == 0 else 4)
        fs = (slice(None), slice(sx, sx + nx), slice(sy, sy + ny))
        fd = (slice(None), slice(dx, dx + nx), slice(dy, dy + ny))
        if ow > 0:
            sx, dx = sx + 1, dx + 1
        if on > 0:
            sy, dy = sy + 1, dy + 1
        nx, ny = (16 if ow == 0 else 3), (16 if on == 0 else 3)
        ks = (slice(sx, sx + nx), slice(sy, sy + ny))
        kd = (slice(dx, dx + nx), slice(dy, dy + ny))
        return [
            (res.at[fs], f0b, fd, s0, q0, i),
            (stiff.at[ks], k0b, kd, s0, q0, 8 + i),
        ]

    def copies1(i, ow, on):
        sx, dx = {0: ((2, 6), (2, 6)), 1: ((4, 6), (0, 2)), -1: ((2, 4), (6, 8))}[ow]
        sy, dy = {0: ((0, 8), (0, 8)), 1: ((4, 8), (12, 16)), -1: ((0, 4), (8, 12))}[on]
        src = g1.at[:, slice(*sx), slice(*sy), :]
        return [(src, g1b, (slice(None), slice(*dx), slice(*dy)), s1, q1, i)]

    def copies2(i, ow, on):
        dx = slice(4 - 4 * ow, 8 - 4 * ow)
        dy = slice(128 - 128 * on, 256 - 128 * on)
        return [(g2.at[:, 4:8, 128:256], g2b, (slice(None), dx, dy), s2, q2, i)]

    def copies3(i, ow, on):
        rows = slice(10 - 2 * ow, 12 - 2 * ow)
        return [(h3.at[10:12, :], h3b, (rows,), s3, q3, i)]

    def copies4(i, ow, on):
        return [(h3, h3sb, (5 - on,), s4, q4, i)]

    def start(copies, offsets):
        for i, (ow, on) in enumerate(offsets):
            opposite = offsets.index((-ow, -on))
            for src, dst, where, send, recv, mine in copies(i, ow, on):
                sems = mine, mine + opposite - i
                remote(src, dst, where, send, recv, sems, ow, on).start()

    def arrive(copies, offsets, chosen=None):
        for i, (ow, on) in enumerate(offsets):
            if chosen is None or i in chosen:
                for src, dst, where, send, recv, mine in copies(i, ow, on):
                    landed(dst, where, send, recv, mine).wait_recv()

    def sent(copies, offsets):
        for i, (ow, on) in enumerate(offsets):
            for src, dst, where, send, recv, mine in copies(i, ow, on):
                landed(dst, where, send, recv, mine).wait_send()

    along_wide = [(o, 0) for o in WINDOW]
    along_narrow = [(0, o) for o in WINDOW]

    start(copies0, NEIGHBOURS)

    @pl.when(w == 0)
    def _():
        f0[:, 0:4] = jnp.zeros((3, 4, 24, 128), F32)
        k0[0:4] = jnp.zeros((4, 24, 128), F32)

    @pl.when(w == nw - 1)
    def _():
        f0[:, 20:24] = jnp.zeros((3, 4, 24, 128), F32)
        k0[20:24] = jnp.zeros((4, 24, 128), F32)

    @pl.when(n == 0)
    def _():
        f0[:, :, 20:24, :] = jnp.zeros((3, 24, 4, 128), F32)
        k0[:, 20:24, :] = jnp.zeros((24, 4, 128), F32)

    @pl.when(n == nn - 1)
    def _():
        f0[:, :, 16:20, :] = jnp.zeros((3, 24, 4, 128), F32)
        k0[:, 16:20, :] = jnp.zeros((24, 4, 128), F32)

    r, c = iota((256, 128), 0), iota((256, 128), 1)
    m01[...] = indicator(((r >> 7) == (c >> 6)) & (((r & 127) >> 1) == (c & 63)), 0.125)
    r, c = iota((512, 128), 0), iota((512, 128), 1)
    m12[...] = indicator(((r >> 7) == (c >> 5)) & (((r & 63) >> 1) == (c & 31)), 0.125)
    m23[...] = indicator(
        ((r >> 7) == (c >> 5))
        & (((r >> 6) & 1) == ((c >> 4) & 1))
        & (((r & 31) >> 1) == (c & 15)),
        0.125,
    )
    r, c = iota((384, 128), 0), iota((384, 128), 1)
    m34[...] = indicator(((r >> 5) == (c >> 3)) & (((r & 15) >> 1) == (c & 7)), 0.125)
    r, c = iota((128, 256), 0), iota((128, 256), 1)
    p1[...] = indicator(((r >> 6) == (c >> 7)) & ((r & 63) == ((c & 127) >> 1)))
    r, c = iota((128, 512), 0), iota((128, 512), 1)
    p2[...] = indicator(((r >> 5) == (c >> 7)) & ((r & 31) == ((c & 127) >> 2)))
    r, c = iota((256, 256), 0), iota((256, 256), 1)
    fine = ((r >> 4) == (2 + (c >> 7))) & ((r & 15) == ((c & 127) >> 3))
    coarse = (r >= 128 + 40) & (r < 128 + 48) & ((r & 7) == ((c & 127) >> 4))
    p34[...] = indicator(fine | coarse)

    own_c.wait()
    coup = [[coup_ref[i, j] for j in range(3)] for i in range(3)]

    own_k.wait()
    for i in range(8):
        t0[pl.ds(384 + 16 * i, 16), :] = (
            k0[4 + 2 * i, 0:16, :] + k0[5 + 2 * i, 0:16, :]
        )

    theta0, steps0 = chebyshev(0)
    lane24 = iota((24, 128), 1)

    def plane0(i, d, k_of, scale, mass):
        us, ds_ = [], []
        for c in range(3):
            mid = d[c, i]
            s = d[c, i - 1] + mid + d[c, i + 1]
            s = s + pltpu.roll(s, 1, 0) + pltpu.roll(s, 23, 0)
            s = (
                s
                + jnp.where(lane24 == 0, 0.0, pltpu.roll(s, 1, 1))
                + jnp.where(lane24 == 127, 0.0, pltpu.roll(s, 127, 1))
            )
            us.append(27.0 * mid - s)
            ds_.append(mid)
        return ds_, mix(coup, scale, mass, us, ds_, k_of[i])

    fields = [f0, d1, d2, d3]

    def sweep0(k, lo, pairs):
        d = fields[k]
        over = 1.0 / theta0 if k == 0 else 1.0
        scale, mass = over / 26.0, over * MASS
        rest = f0 if k == 0 else r0

        def body(t, carry):
            both = []
            for u in range(2):
                i = lo + 2 * t + u
                mids, a = plane0(i, d, k0, scale, mass)
                new = [rest[c, i] - a[c] for c in range(3)]
                if k < 3:
                    ca, cb = steps0[k]
                    for c in range(3):
                        r0[c, i] = new[c]
                        fields[k + 1][c, i] = (ca * over) * mids[c] + cb * new[c]
                both.append(new)
            if k == 3:
                half = (lo - 4) // 2 + t
                for c in range(3):
                    rows = pl.multiple_of(128 * c + 16 * half, 16)
                    t0[pl.ds(rows, 16), :] = both[0][c][0:16] + both[1][c][0:16]
            return carry

        lax.fori_loop(0, pairs, body, 0)

    own_f.wait()
    arrive(copies0, NEIGHBOURS, (6, 7))
    for k in range(4):
        sweep0(k, 5 + k, 7 - k) if k < 3 else sweep0(3, 8, 4)
    arrive(copies0, NEIGHBOURS, (0, 1, 2, 3, 4, 5))
    for k in range(4):
        sweep0(k, 1 + k, 2)
        sweep0(k, 19 - k, 2)

    s = t0[pl.ds(0, 256, stride=2), :] + t0[pl.ds(1, 256, stride=2), :]
    s = s.reshape(4, 4, 2, 8, 128)
    pair = jnp.concatenate(
        [s[:, :, 0].reshape(128, 128), s[:, :, 1].reshape(128, 128)], axis=1
    )
    g1[:, 2:6, 0:8, :] = mm(pair, m01[...]).reshape(4, 4, 8, 128)
    start(copies1, NEIGHBOURS)
    sent(copies0, NEIGHBOURS)

    def sum0(i, carry):
        for c in range(3):
            acc[c, i] = (
                f0[c, 4 + i, 0:16, :] * (1.0 / theta0)
                + d1[c, 4 + i, 0:16, :]
                + d2[c, 4 + i, 0:16, :]
                + d3[c, 4 + i, 0:16, :]
            )
        return carry

    lax.fori_loop(0, 16, sum0, 0)

    arrive(copies1, NEIGHBOURS)

    theta1, steps1 = chebyshev(1)
    lane16 = iota((16, 128), 1)
    lower = lane16 < 64
    zpos1 = lane16 & 63
    for p in range(8):
        for c in range(3):
            w1[c, p] = pltpu.roll(g1[c, p], 64, 1)

    def plane1(p, d, wd, scale, mass):
        us, mids = [], []
        for c in range(3):
            mid = d[c, p]
            before = wd[c, max(p - 1, 0)]
            after = wd[c, min(p + 1, 7)]
            s = mid + wd[c, p] + jnp.where(lower, before, after)
            s = s + pltpu.roll(s, 1, 0) + pltpu.roll(s, 15, 0)
            s = (
                s
                + jnp.where(zpos1 == 0, 0.0, pltpu.roll(s, 1, 1))
                + jnp.where(zpos1 == 63, 0.0, pltpu.roll(s, 127, 1))
            )
            us.append(27.0 * mid - s)
            mids.append(mid)
        return mids, mix(coup, scale, mass, us, mids, g1[3, p])

    x1 = {}
    pairs1 = [(g1, w1), (e1, w2), (e2, w1), (e1, w2)]
    for k, (lo, hi) in enumerate([(0, 8), (1, 7), (1, 7), (2, 6)]):
        d, wd = pairs1[k]
        over = 1.0 / theta1 if k == 0 else 1.0
        scale, mass = over / (4.0 * 26.0), over * MASS
        for p in range(lo, hi):
            mids, a = plane1(p, d, wd, scale, mass)
            for c in range(3):
                new = (g1 if k == 0 else r1)[c, p] - a[c]
                if k < 3:
                    ca, cb = steps1[k]
                    nd, nwd = pairs1[k + 1]
                    r1[c, p] = new
                    step = (ca * over) * mids[c] + cb * new
                    nd[c, p] = step
                    nwd[c, p] = pltpu.roll(step, 64, 1)
                else:
                    t1[pl.ds(32 * c + 8 * (p - 2), 8), :] = new[0:8]
                if 2 <= p < 6:
                    part = (mids[c] * over)[0:8]
                    x1[c, p] = part if k == 0 else x1[c, p] + part
    for p in range(4):
        t1[pl.ds(96 + 8 * p, 8), :] = g1[3, 2 + p, 0:8, :]

    ys = [t1[pl.ds(y, 16, stride=8), :] for y in range(8)]
    ys = jnp.concatenate([ys[2 * j] + ys[2 * j + 1] for j in range(4)], axis=1)
    blk = mm(ys, m12[...])
    for c in range(4):
        g2[c, 4:8, 128:256] = blk[4 * c : 4 * c + 4]
    start(copies2, NEIGHBOURS)
    sent(copies1, NEIGHBOURS)

    rows = jnp.concatenate([x1[c, p] for c in range(3) for p in range(2, 6)], axis=0)
    rep = mm(rows, p1[...])
    u_lo[pl.ds(0, 96, stride=2), :] = rep[:, 0:128]
    u_lo[pl.ds(1, 96, stride=2), :] = rep[:, 0:128]
    u_hi[pl.ds(0, 96, stride=2), :] = rep[:, 128:256]
    u_hi[pl.ds(1, 96, stride=2), :] = rep[:, 128:256]
    for c in range(3):
        for p in range(4):
            rows_cp = pl.ds(16 * (4 * c + p), 16)
            for j in range(4):
                acc[c, 4 * p + j] += (u_lo if j < 2 else u_hi)[rows_cp, :]

    arrive(copies2, NEIGHBOURS)

    f2 = [[g2[c, :, 128 * j : 128 * j + 128] for j in range(3)] for c in range(4)]
    x2, r2 = flat_smooth(f2[:3], f2[3], coup, 2, 32, True)

    t2[...] = mm(
        jnp.concatenate([r2[0][1], r2[1][1], r2[2][1], f2[3][1]], axis=1), m23[...]
    )
    h3[10:12, :] = t2[pl.ds(4, 2, stride=2), :] + t2[pl.ds(5, 2, stride=2), :]
    start(copies3, along_wide)
    sent(copies2, NEIGHBOURS)

    for c in range(3):
        t3[4 * c : 4 * c + 4, 0:128] = x2[c][1][4:8]
    rep = mm(t3[0:16, 0:128], p2[...])
    for y in range(16):
        j = y // 4
        v2[pl.ds(y, 16, stride=16), :] = rep[:, 128 * j : 128 * j + 128]
    for c in range(3):
        for k in range(4):
            part = v2[pl.ds(16 * (4 * c + k), 16), :]
            for j in range(4):
                acc[c, 4 * k + j] += part

    arrive(copies3, along_wide)
    start(copies4, along_narrow)
    sent(copies3, along_wide)
    arrive(copies4, along_narrow)
    sent(copies4, along_narrow)

    lane3 = iota((24, 128), 1)
    slots = [h3s[j] if j != 5 else h3[...] for j in range(11)]
    f3 = [[None] * 3 for _ in range(4)]
    for c in range(4):
        for v in range(3):
            out = jnp.zeros((24, 128), F32)
            for q in range(4):
                j = 4 * v + q
                if j < 11:
                    turn = 32 * ((q - c) % 4)
                    part = pltpu.roll(slots[j], turn, 1) if turn else slots[j]
                    out = jnp.where((lane3 >> 5) == q, part, out)
            f3[c][v] = out
    x3, r3 = flat_smooth(f3[:3], f3[3], coup, 3, 16, True)

    for c in range(4):
        src = jnp.concatenate(r3[c] if c < 3 else f3[3], axis=1)
        t3[24 * c : 24 * c + 24, :] = src
    s = mm(t3[...], m34[...])
    z4[...] = s
    s = z4[pl.ds(0, 48, stride=2), :] + z4[pl.ds(1, 48, stride=2), :]
    pad = jnp.zeros((4, 128), F32)
    f4 = [[jnp.concatenate([s[12 * c : 12 * c + 12], pad], axis=0)] for c in range(4)]
    x4, _ = flat_smooth(f4[:3], f4[3], coup, 4, 8, False)

    for c in range(3):
        t3[2 * c : 2 * c + 2, 0:128] = x3[c][1][10:12]
        t3[2 * c : 2 * c + 2, 128:256] = jnp.broadcast_to(x4[c][0][5:6], (2, 128))
    tail_out[...] = mm(t3[0:16, 0:256], p34[...])[0:8]


def solution(mesh):
    nw, nn = mesh.shape["wide"], mesh.shape["narrow"]

    def vm(*shape):
        return pltpu.VMEM(shape, F32)

    def mat(*shape):
        return pltpu.VMEM(shape, BF16)

    dma = pltpu.SemaphoreType.DMA
    scratch = [
        vm(2, 3, 24, 24, 128),
        vm(2, 24, 24, 128),
        vm(3, 24, 24, 128),
        vm(3, 24, 24, 128),
        vm(3, 24, 24, 128),
        vm(3, 24, 24, 128),
        vm(512, 128),
        vm(2, 4, 8, 16, 128),
        vm(3, 8, 16, 128),
        vm(3, 8, 16, 128),
        vm(3, 8, 16, 128),
        vm(3, 8, 16, 128),
        vm(3, 8, 16, 128),
        vm(128, 128),
        vm(192, 128),
        vm(192, 128),
        vm(2, 4, 16, 384),
        vm(16, 128),
        vm(256, 128),
        vm(2, 24, 128),
        vm(2, 11, 24, 128),
        vm(96, 384),
        vm(96, 128),
        mat(256, 128),
        mat(512, 128),
        mat(512, 128),
        mat(384, 128),
        mat(128, 256),
        mat(128, 512),
        mat(256, 256),
        pltpu.SMEM((3, 3), F32),
        dma((3,)),
        dma((16,)),
        dma((16,)),
        dma((8,)),
        dma((8,)),
        dma((8,)),
        dma((8,)),
        dma((10,)),
        dma((10,)),
        dma((10,)),
        dma((10,)),
    ]

    def per_device(residual, stiffness, coupling):
        hbm = pl.BlockSpec(memory_space=pltpu.HBM)
        vmem = pl.BlockSpec(memory_space=pltpu.VMEM)
        acc, tail = pl.pallas_call(
            functools.partial(kernel, nw, nn),
            out_shape=(
                jax.ShapeDtypeStruct((3, 16, 16, 128), F32),
                jax.ShapeDtypeStruct((8, 256), F32),
            ),
            in_specs=[hbm, hbm, hbm],
            out_specs=(vmem, vmem),
            scratch_shapes=scratch,
            compiler_params=pltpu.CompilerParams(
                collective_id=0,
                has_side_effects=True,
                vmem_limit_bytes=(53 * 1024 + 300) * 1024,
            ),
        )(residual, stiffness, coupling)
        tail = tail[0:6].reshape(3, 2, 1, 2, 1, 128)
        return (acc.reshape(3, 2, 8, 2, 8, 128) + tail).reshape(3, 16, 16, 128)

    return jax.shard_map(
        per_device,
        mesh=mesh,
        in_specs=(P(None, "wide", "narrow", None), P("wide", "narrow", None), P()),
        out_specs=P(None, "wide", "narrow", None),
        check_vma=False,
    )
```

```python
import functools

import jax
import jax.numpy as jnp
from jax import lax
from jax.experimental import pallas as pl
from jax.experimental.pallas import tpu as pltpu
from jax.sharding import PartitionSpec as P

LEVELS = 4
MASS = 0.001
RATIO = 8.0
MESH = pl.DeviceIdType.MESH
NEIGHBOURS = [(1, 1), (1, -1), (-1, 1), (-1, -1), (1, 0), (-1, 0), (0, 1), (0, -1)]
AXIAL = NEIGHBOURS[4:]
WINDOW = [o for k in range(5, 0, -1) for o in (k, -k)]
F32 = jnp.float32
BF16 = jnp.bfloat16


def chebyshev(level):
    top = 4.0 * (2.8 / 4.0**level + MASS)
    theta = (top + top / RATIO) / 2.0
    delta = (top - top / RATIO) / 2.0
    sigma = theta / delta
    rho = 1.0 / sigma
    steps = []
    for _ in range(3):
        nxt = 1.0 / (2.0 * sigma - rho)
        steps.append((nxt * rho, 2.0 * nxt / delta))
        rho = nxt
    return theta, steps


def iota(shape, dim):
    return lax.broadcasted_iota(jnp.int32, shape, dim)


def indicator(cond, value=1.0):
    return jnp.where(cond, value, 0.0).astype(BF16)


def mm(v, w):
    hi = v.astype(BF16)
    lo = (v - hi.astype(F32)).astype(BF16)
    return jnp.dot(hi, w, preferred_element_type=F32) + jnp.dot(
        lo, w, preferred_element_type=F32
    )


def mix(coup, scale, mass, u, d, k):
    out = []
    for c in range(3):
        a = (coup[c][0] * scale) * u[0]
        a = a + (coup[c][1] * scale) * u[1]
        a = a + (coup[c][2] * scale) * u[2]
        a = a + mass * d[c]
        out.append(k * a)
    return out


def flat_box(chunks, nz):
    rows = chunks[0].shape[0]
    lane = iota(chunks[0].shape, 1)
    zpos = lane & (nz - 1)
    s = []
    for v in chunks:
        v = v + pltpu.roll(v, 1, 0) + pltpu.roll(v, rows - 1, 0)
        s.append(
            v
            + jnp.where(zpos == 0, 0.0, pltpu.roll(v, 1, 1))
            + jnp.where(zpos == nz - 1, 0.0, pltpu.roll(v, 127, 1))
        )
    up = [pltpu.roll(v, nz, 1) for v in s]
    down = [pltpu.roll(v, 128 - nz, 1) for v in s]
    out = []
    for j, v in enumerate(s):
        before = up[j - 1] if j > 0 else 0.0
        after = down[j + 1] if j + 1 < len(s) else 0.0
        out.append(
            v
            + jnp.where(lane < nz, before, up[j])
            + jnp.where(lane >= 128 - nz, after, down[j])
        )
    return out


def flat_smooth(f, kappa, coup, level, nz, want_rest):
    theta, steps = chebyshev(level)
    scale = 4.0**-level / 26.0
    n = len(kappa)

    def apply(r, d):
        boxes = [flat_box(d[c], nz) for c in range(3)]
        new = [[None] * n for _ in range(3)]
        for j in range(n):
            u = [27.0 * d[c][j] - boxes[c][j] for c in range(3)]
            a = mix(coup, scale, MASS, u, [d[c][j] for c in range(3)], kappa[j])
            for c in range(3):
                new[c][j] = r[c][j] - a[c]
        return new

    r = f
    d = [[v * (1.0 / theta) for v in f[c]] for c in range(3)]
    x = d
    for a, b in steps:
        r = apply(r, d)
        d = [[a * d[c][j] + b * r[c][j] for j in range(n)] for c in range(3)]
        x = [[x[c][j] + d[c][j] for j in range(n)] for c in range(3)]
    if want_rest:
        r = apply(r, d)
    return x, r


def kernel(
    nw,
    nn,
    res,
    stiff,
    coup_hbm,
    acc0,
    acc1,
    acc2,
    tail_out,
    f0b,
    k0b,
    r0,
    d1,
    d2,
    d3,
    t0,
    g1b,
    r1,
    e1,
    w1,
    e2,
    w2,
    t1,
    u_lo,
    u_hi,
    g2b,
    t2,
    v2,
    h3b,
    h3sb,
    t3,
    z4,
    m01,
    m12,
    m23,
    m34,
    p1,
    p2,
    p34,
    coup_ref,
    local_sem,
    ready_sem,
    s0,
    q0,
    s1,
    q1,
    s2,
    q2,
    s3,
    q3,
    s4,
    q4,
):
    w = lax.axis_index("wide")
    n = lax.axis_index("narrow")
    acc = [acc0, acc1, acc2]
    f0, k0, g1, g2, h3, h3s = (b.at[0] for b in (f0b, k0b, g1b, g2b, h3b, h3sb))

    def pair_of(i):
        return i + 1 - 2 * lax.rem(i, 2)

    def out_of(pos, off, size):
        if off == 0:
            return jnp.bool_(False)
        return pos + off >= size if off > 0 else pos + off < 0

    targets = {}

    def target(ow, on):
        if (ow, on) in targets:
            return targets[ow, on]
        w_out, n_out = out_of(w, ow, nw), out_of(n, on, nn)
        if on == 0:
            tw = jnp.where(w_out, w, w + ow)
            tn = jnp.where(w_out, pair_of(n), n)
            away = w_out
        elif ow == 0:
            tw = jnp.where(n_out, pair_of(w), w)
            tn = jnp.where(n_out, n, n + on)
            away = n_out
        else:
            w_end, n_end = (nw - 1 if ow > 0 else 0), (nn - 1 if on > 0 else 0)
            both = jnp.logical_and(w_out, n_out)
            away = jnp.logical_or(w_out, n_out)
            w_near, n_near = w == w_end - ow, n == n_end - on
            tw = jnp.where(
                both,
                w - ow,
                jnp.where(
                    w_out,
                    w,
                    jnp.where(n_out, jnp.where(w_near, w + ow, pair_of(w)), w + ow),
                ),
            )
            tn = jnp.where(
                both,
                n,
                jnp.where(
                    w_out,
                    jnp.where(n_near, n + on, pair_of(n)),
                    jnp.where(n_out, jnp.where(w_near, n - on, n), n + on),
                ),
            )
        targets[ow, on] = tw, tn, jnp.where(away, 1, 0)
        return targets[ow, on]

    def remote(src, dst, where, send, recv, sems, ow, on):
        tw, tn, away = target(ow, on)
        mine, other = sems
        return pltpu.make_async_remote_copy(
            src_ref=src,
            dst_ref=dst.at[(away,) + where],
            send_sem=send.at[mine],
            recv_sem=recv.at[mine + (other - mine) * away],
            device_id={"wide": tw, "narrow": tn},
            device_id_type=MESH,
        )

    def landed(buf, where, send, recv, mine):
        return pltpu.make_async_remote_copy(
            src_ref=buf.at[(0,) + where],
            dst_ref=buf.at[(0,) + where],
            send_sem=send.at[mine],
            recv_sem=recv.at[mine],
            device_id={"wide": w, "narrow": n},
            device_id_type=MESH,
        )

    own_f = pltpu.make_async_copy(res, f0.at[:, 4:20, 0:16, :], local_sem.at[0])
    own_k = pltpu.make_async_copy(stiff, k0.at[4:20, 0:16, :], local_sem.at[1])
    own_c = pltpu.make_async_copy(coup_hbm, coup_ref, local_sem.at[2])
    own_f.start()
    own_k.start()
    own_c.start()

    h3[...] = jnp.zeros_like(h3)
    h3s[...] = jnp.zeros_like(h3s)

    def tell(sem, offsets):
        for ow, on in offsets:
            tw, tn, _ = target(ow, on)
            pl.semaphore_signal(
                sem,
                inc=1,
                device_id={"wide": tw, "narrow": tn},
                device_id_type=MESH,
            )

    barrier = pltpu.get_barrier_semaphore()
    tell(barrier, AXIAL)
    g1[...] = jnp.zeros_like(g1)
    g2[...] = jnp.zeros_like(g2)
    own_f.wait()
    own_k.wait()
    pl.semaphore_wait(barrier, len(AXIAL))

    def copies0(i, ow, on):
        sx, dx = {0: (0, 4), 1: (12, 0), -1: (0, 20)}[ow]
        sy, dy = {0: (0, 0), 1: (12, 20), -1: (0, 16)}[on]
        nx, ny = (16 if ow == 0 else 4), (16 if on == 0 else 4)
        fs = (slice(None), slice(4 + sx, 4 + sx + nx), slice(sy, sy + ny))
        fd = (slice(None), slice(dx, dx + nx), slice(dy, dy + ny))
        if ow > 0:
            sx, dx = sx + 1, dx + 1
        if on > 0:
            sy, dy = sy + 1, dy + 1
        nx, ny = (16 if ow == 0 else 3), (16 if on == 0 else 3)
        ks = (slice(4 + sx, 4 + sx + nx), slice(sy, sy + ny))
        kd = (slice(dx, dx + nx), slice(dy, dy + ny))
        return [
            (f0.at[fs], f0b, fd, s0, q0, i),
            (k0.at[ks], k0b, kd, s0, q0, 8 + i),
        ]

    def copies1(i, ow, on):
        sx, dx = {0: ((2, 6), (2, 6)), 1: ((4, 6), (0, 2)), -1: ((2, 4), (6, 8))}[ow]
        sy, dy = {0: ((0, 8), (0, 8)), 1: ((4, 8), (12, 16)), -1: ((0, 4), (8, 12))}[on]
        src = g1.at[:, slice(*sx), slice(*sy), :]
        return [(src, g1b, (slice(None), slice(*dx), slice(*dy)), s1, q1, i)]

    def copies2(i, ow, on):
        dx = slice(4 - 4 * ow, 8 - 4 * ow)
        dy = slice(128 - 128 * on, 256 - 128 * on)
        return [(g2.at[:, 4:8, 128:256], g2b, (slice(None), dx, dy), s2, q2, i)]

    def copies3(i, ow, on):
        rows = slice(10 - 2 * ow, 12 - 2 * ow)
        return [(h3.at[10:12, :], h3b, (rows,), s3, q3, i)]

    def copies4(i, ow, on):
        return [(h3, h3sb, (5 - on,), s4, q4, i)]

    def start(copies, offsets, chosen=None, part=slice(None)):
        for i, (ow, on) in enumerate(offsets):
            if chosen is None or i in chosen:
                opposite = offsets.index((-ow, -on))
                for src, dst, where, send, recv, mine in copies(i, ow, on)[part]:
                    sems = mine, mine + opposite - i
                    remote(src, dst, where, send, recv, sems, ow, on).start()

    def arrive(copies, offsets, chosen=None):
        for i, (ow, on) in enumerate(offsets):
            if chosen is None or i in chosen:
                for src, dst, where, send, recv, mine in copies(i, ow, on):
                    landed(dst, where, send, recv, mine).wait_recv()

    def sent(copies, offsets):
        for i, (ow, on) in enumerate(offsets):
            for src, dst, where, send, recv, mine in copies(i, ow, on):
                landed(dst, where, send, recv, mine).wait_send()

    along_wide = [(o, 0) for o in WINDOW]
    along_narrow = [(0, o) for o in WINDOW]

    start(copies0, NEIGHBOURS, (4, 5), slice(0, 1))
    start(copies0, NEIGHBOURS, (6, 7))
    tell(ready_sem, AXIAL)
    pl.semaphore_wait(ready_sem, len(AXIAL))
    start(copies0, NEIGHBOURS, (0, 1, 2, 3))
    start(copies0, NEIGHBOURS, (4, 5), slice(1, 2))

    @pl.when(w == 0)
    def _():
        f0[:, 0:4] = jnp.zeros((3, 4, 24, 128), F32)
        k0[0:4] = jnp.zeros((4, 24, 128), F32)

    @pl.when(w == nw - 1)
    def _():
        f0[:, 20:24] = jnp.zeros((3, 4, 24, 128), F32)
        k0[20:24] = jnp.zeros((4, 24, 128), F32)

    @pl.when(n == 0)
    def _():
        f0[:, :, 20:24, :] = jnp.zeros((3, 24, 4, 128), F32)
        k0[:, 20:24, :] = jnp.zeros((24, 4, 128), F32)

    @pl.when(n == nn - 1)
    def _():
        f0[:, :, 16:20, :] = jnp.zeros((3, 24, 4, 128), F32)
        k0[:, 16:20, :] = jnp.zeros((24, 4, 128), F32)

    r, c = iota((256, 128), 0), iota((256, 128), 1)
    m01[...] = indicator(((r >> 7) == (c >> 6)) & (((r & 127) >> 1) == (c & 63)), 0.125)
    r, c = iota((512, 128), 0), iota((512, 128), 1)
    m12[...] = indicator(((r >> 7) == (c >> 5)) & (((r & 63) >> 1) == (c & 31)), 0.125)
    m23[...] = indicator(
        ((r >> 7) == (c >> 5))
        & (((r >> 6) & 1) == ((c >> 4) & 1))
        & (((r & 31) >> 1) == (c & 15)),
        0.125,
    )
    r, c = iota((384, 128), 0), iota((384, 128), 1)
    m34[...] = indicator(((r >> 5) == (c >> 3)) & (((r & 15) >> 1) == (c & 7)), 0.125)
    r, c = iota((128, 256), 0), iota((128, 256), 1)
    p1[...] = indicator(((r >> 6) == (c >> 7)) & ((r & 63) == ((c & 127) >> 1)))
    r, c = iota((128, 512), 0), iota((128, 512), 1)
    p2[...] = indicator(((r >> 5) == (c >> 7)) & ((r & 31) == ((c & 127) >> 2)))
    r, c = iota((256, 256), 0), iota((256, 256), 1)
    fine = ((r >> 4) == (2 + (c >> 7))) & ((r & 15) == ((c & 127) >> 3))
    coarse = (r >= 128 + 40) & (r < 128 + 48) & ((r & 7) == ((c & 127) >> 4))
    p34[...] = indicator(fine | coarse)

    own_c.wait()
    coup = [[coup_ref[i, j] for j in range(3)] for i in range(3)]

    for i in range(8):
        t0[pl.ds(384 + 16 * i, 16), :] = (
            k0[4 + 2 * i, 0:16, :] + k0[5 + 2 * i, 0:16, :]
        )

    theta0, steps0 = chebyshev(0)
    lane24 = iota((24, 128), 1)
    lane16 = iota((16, 128), 1)
    fields = [f0, d1, d2, d3]

    def sweep0(k, starts, count):
        d = fields[k]
        over = 1.0 / theta0 if k == 0 else 1.0
        scale, mass = over / 26.0, over * MASS
        rest = f0 if k == 0 else r0
        rows, lane = (24, lane24) if k < 3 else (16, lane16)
        for lo in starts:
            for i in range(lo, lo + count, 2):
                mids, boxes = [[], []], [[], []]
                for c in range(3):
                    a, b = d[c, i], d[c, i + 1]
                    both = a + b
                    for u, (mid, x) in enumerate(((a, d[c, i - 1]), (b, d[c, i + 2]))):
                        s = both + x
                        s = s + pltpu.roll(s, 1, 0) + pltpu.roll(s, 23, 0)
                        s = s[0:rows]
                        s = (
                            s
                            + jnp.where(lane == 0, 0.0, pltpu.roll(s, 1, 1))
                            + jnp.where(lane == 127, 0.0, pltpu.roll(s, 127, 1))
                        )
                        mids[u].append(mid[0:rows])
                        boxes[u].append(s)
                new = []
                for u in range(2):
                    us = [27.0 * mids[u][c] - boxes[u][c] for c in range(3)]
                    a = mix(coup, scale, mass, us, mids[u], k0[i + u, 0:rows])
                    new.append([rest[c, i + u, 0:rows] - a[c] for c in range(3)])
                    if k < 3:
                        ca, cb = steps0[k]
                        for c in range(3):
                            r0[c, i + u] = new[u][c]
                            fields[k + 1][c, i + u] = (ca * over) * mids[u][c] + cb * new[u][c]
                if k == 3:
                    for c in range(3):
                        t0[pl.ds(128 * c + 8 * (i - 4), 16), :] = new[0][c] + new[1][c]

    arrive(copies0, NEIGHBOURS, (6, 7))
    for k in range(4):
        sweep0(k, (5 + k,), 14 - 2 * k)
    arrive(copies0, NEIGHBOURS, (0, 1, 2, 3, 4, 5))
    for k in range(4):
        sweep0(k, (1 + k, 19 - k), 4)
    s = t0[pl.ds(0, 256, stride=2), :] + t0[pl.ds(1, 256, stride=2), :]
    s = s.reshape(4, 4, 2, 8, 128)
    pair = jnp.concatenate(
        [s[:, :, 0].reshape(128, 128), s[:, :, 1].reshape(128, 128)], axis=1
    )
    g1[:, 2:6, 0:8, :] = mm(pair, m01[...]).reshape(4, 4, 8, 128)
    start(copies1, NEIGHBOURS)
    sent(copies0, NEIGHBOURS)

    def sum0(i, carry):
        for c in range(3):
            acc[c][i] = (
                f0[c, 4 + i, 0:16, :] * (1.0 / theta0)
                + d1[c, 4 + i, 0:16, :]
                + d2[c, 4 + i, 0:16, :]
                + d3[c, 4 + i, 0:16, :]
            )
        return carry

    lax.fori_loop(0, 16, sum0, 0)

    arrive(copies1, NEIGHBOURS)

    theta1, steps1 = chebyshev(1)
    lower = lane16 < 64
    zpos1 = lane16 & 63
    for p in range(8):
        for c in range(3):
            w1[c, p] = pltpu.roll(g1[c, p], 64, 1)

    def plane1(p, d, wd, scale, mass):
        us, mids = [], []
        for c in range(3):
            mid = d[c, p]
            before = wd[c, max(p - 1, 0)]
            after = wd[c, min(p + 1, 7)]
            s = mid + wd[c, p] + jnp.where(lower, before, after)
            s = s + pltpu.roll(s, 1, 0) + pltpu.roll(s, 15, 0)
            s = (
                s
                + jnp.where(zpos1 == 0, 0.0, pltpu.roll(s, 1, 1))
                + jnp.where(zpos1 == 63, 0.0, pltpu.roll(s, 127, 1))
            )
            us.append(27.0 * mid - s)
            mids.append(mid)
        return mids, mix(coup, scale, mass, us, mids, g1[3, p])

    x1 = {}
    pairs1 = [(g1, w1), (e1, w2), (e2, w1), (e1, w2)]
    for k, (lo, hi) in enumerate([(0, 8), (1, 7), (1, 7), (2, 6)]):
        d, wd = pairs1[k]
        over = 1.0 / theta1 if k == 0 else 1.0
        scale, mass = over / (4.0 * 26.0), over * MASS
        for p in range(lo, hi):
            mids, a = plane1(p, d, wd, scale, mass)
            for c in range(3):
                new = (g1 if k == 0 else r1)[c, p] - a[c]
                if k < 3:
                    ca, cb = steps1[k]
                    nd, nwd = pairs1[k + 1]
                    r1[c, p] = new
                    step = (ca * over) * mids[c] + cb * new
                    nd[c, p] = step
                    nwd[c, p] = pltpu.roll(step, 64, 1)
                else:
                    t1[pl.ds(32 * c + 8 * (p - 2), 8), :] = new[0:8]
                if 2 <= p < 6:
                    part = (mids[c] * over)[0:8]
                    x1[c, p] = part if k == 0 else x1[c, p] + part
    for p in range(4):
        t1[pl.ds(96 + 8 * p, 8), :] = g1[3, 2 + p, 0:8, :]

    ys = [t1[pl.ds(y, 16, stride=8), :] for y in range(8)]
    ys = jnp.concatenate([ys[2 * j] + ys[2 * j + 1] for j in range(4)], axis=1)
    blk = mm(ys, m12[...])
    for c in range(4):
        g2[c, 4:8, 128:256] = blk[4 * c : 4 * c + 4]
    start(copies2, NEIGHBOURS)
    sent(copies1, NEIGHBOURS)

    rows = jnp.concatenate([x1[c, p] for c in range(3) for p in range(2, 6)], axis=0)
    rep = mm(rows, p1[...])
    u_lo[pl.ds(0, 96, stride=2), :] = rep[:, 0:128]
    u_lo[pl.ds(1, 96, stride=2), :] = rep[:, 0:128]
    u_hi[pl.ds(0, 96, stride=2), :] = rep[:, 128:256]
    u_hi[pl.ds(1, 96, stride=2), :] = rep[:, 128:256]
    for c in range(3):
        for p in range(4):
            rows_cp = pl.ds(16 * (4 * c + p), 16)
            for j in range(4):
                acc[c][4 * p + j] += (u_lo if j < 2 else u_hi)[rows_cp, :]

    arrive(copies2, NEIGHBOURS)

    f2 = [[g2[c, :, 128 * j : 128 * j + 128] for j in range(3)] for c in range(4)]
    x2, r2 = flat_smooth(f2[:3], f2[3], coup, 2, 32, True)

    t2[...] = mm(
        jnp.concatenate([r2[0][1], r2[1][1], r2[2][1], f2[3][1]], axis=1), m23[...]
    )
    h3[10:12, :] = t2[pl.ds(4, 2, stride=2), :] + t2[pl.ds(5, 2, stride=2), :]
    start(copies3, along_wide)
    sent(copies2, NEIGHBOURS)

    for c in range(3):
        t3[4 * c : 4 * c + 4, 0:128] = x2[c][1][4:8]
    rep = mm(t3[0:16, 0:128], p2[...])
    for y in range(16):
        j = y // 4
        v2[pl.ds(y, 16, stride=16), :] = rep[:, 128 * j : 128 * j + 128]
    for c in range(3):
        for k in range(4):
            part = v2[pl.ds(16 * (4 * c + k), 16), :]
            for j in range(4):
                acc[c][4 * k + j] += part

    arrive(copies3, along_wide)
    start(copies4, along_narrow)
    sent(copies3, along_wide)
    arrive(copies4, along_narrow)
    sent(copies4, along_narrow)

    lane3 = iota((24, 128), 1)
    slots = [h3s[j] if j != 5 else h3[...] for j in range(11)]
    f3 = [[None] * 3 for _ in range(4)]
    for c in range(4):
        for v in range(3):
            out = jnp.zeros((24, 128), F32)
            for q in range(4):
                j = 4 * v + q
                if j < 11:
                    turn = 32 * ((q - c) % 4)
                    part = pltpu.roll(slots[j], turn, 1) if turn else slots[j]
                    out = jnp.where((lane3 >> 5) == q, part, out)
            f3[c][v] = out
    x3, r3 = flat_smooth(f3[:3], f3[3], coup, 3, 16, True)

    for c in range(4):
        src = jnp.concatenate(r3[c] if c < 3 else f3[3], axis=1)
        t3[24 * c : 24 * c + 24, :] = src
    s = mm(t3[...], m34[...])
    z4[...] = s
    s = z4[pl.ds(0, 48, stride=2), :] + z4[pl.ds(1, 48, stride=2), :]
    pad = jnp.zeros((4, 128), F32)
    f4 = [[jnp.concatenate([s[12 * c : 12 * c + 12], pad], axis=0)] for c in range(4)]
    x4, _ = flat_smooth(f4[:3], f4[3], coup, 4, 8, False)

    for c in range(3):
        t3[2 * c : 2 * c + 2, 0:128] = x3[c][1][10:12]
        t3[2 * c : 2 * c + 2, 128:256] = jnp.broadcast_to(x4[c][0][5:6], (2, 128))
    tail_out[...] = mm(t3[0:16, 0:256], p34[...])[0:8]


def solution(mesh):
    nw, nn = mesh.shape["wide"], mesh.shape["narrow"]

    def vm(*shape):
        return pltpu.VMEM(shape, F32)

    def mat(*shape):
        return pltpu.VMEM(shape, BF16)

    dma = pltpu.SemaphoreType.DMA
    scratch = [
        vm(2, 3, 24, 24, 128),
        vm(2, 24, 24, 128),
        vm(3, 24, 24, 128),
        vm(3, 24, 24, 128),
        vm(3, 24, 24, 128),
        vm(3, 24, 24, 128),
        vm(512, 128),
        vm(2, 4, 8, 16, 128),
        vm(3, 8, 16, 128),
        vm(3, 8, 16, 128),
        vm(3, 8, 16, 128),
        vm(3, 8, 16, 128),
        vm(3, 8, 16, 128),
        vm(128, 128),
        vm(192, 128),
        vm(192, 128),
        vm(2, 4, 16, 384),
        vm(16, 128),
        vm(256, 128),
        vm(2, 24, 128),
        vm(2, 11, 24, 128),
        vm(96, 384),
        vm(96, 128),
        mat(256, 128),
        mat(512, 128),
        mat(512, 128),
        mat(384, 128),
        mat(128, 256),
        mat(128, 512),
        mat(256, 256),
        pltpu.SMEM((3, 3), F32),
        dma((3,)),
        pltpu.SemaphoreType.REGULAR,
        dma((16,)),
        dma((16,)),
        dma((8,)),
        dma((8,)),
        dma((8,)),
        dma((8,)),
        dma((10,)),
        dma((10,)),
        dma((10,)),
        dma((10,)),
    ]

    def per_device(residual, stiffness, coupling):
        hbm = pl.BlockSpec(memory_space=pltpu.HBM)
        vmem = pl.BlockSpec(memory_space=pltpu.VMEM)
        *acc, tail = pl.pallas_call(
            functools.partial(kernel, nw, nn),
            out_shape=(
                *[jax.ShapeDtypeStruct((16, 16, 128), F32)] * 3,
                jax.ShapeDtypeStruct((8, 256), F32),
            ),
            in_specs=[hbm, hbm, hbm],
            out_specs=(vmem,) * 4,
            scratch_shapes=scratch,
            compiler_params=pltpu.CompilerParams(
                collective_id=0,
                has_side_effects=True,
                vmem_limit_bytes=(53 * 1024 + 450) * 1024,
            ),
        )(residual, stiffness, coupling)
        tail = tail[0:6].reshape(3, 2, 1, 2, 1, 128)
        return (jnp.stack(acc).reshape(3, 2, 8, 2, 8, 128) + tail).reshape(3, 16, 16, 128)

    return jax.shard_map(
        per_device,
        mesh=mesh,
        in_specs=(P(None, "wide", "narrow", None), P("wide", "narrow", None), P()),
        out_specs=P(None, "wide", "narrow", None),
        check_vma=False,
    )
```

```python
import functools

import jax
import jax.numpy as jnp
from jax import lax
from jax.experimental import pallas as pl
from jax.experimental.pallas import tpu as pltpu
from jax.sharding import PartitionSpec as P

LEVELS = 4
MASS = 0.001
RATIO = 8.0
MESH = pl.DeviceIdType.MESH
NEIGHBOURS = [(1, 1), (1, -1), (-1, 1), (-1, -1), (1, 0), (-1, 0), (0, 1), (0, -1)]
AXIAL = NEIGHBOURS[4:]
WINDOW = [o for k in range(5, 0, -1) for o in (k, -k)]
F32 = jnp.float32
BF16 = jnp.bfloat16


def chebyshev(level):
    top = 4.0 * (2.8 / 4.0**level + MASS)
    theta = (top + top / RATIO) / 2.0
    delta = (top - top / RATIO) / 2.0
    sigma = theta / delta
    rho = 1.0 / sigma
    steps = []
    for _ in range(3):
        nxt = 1.0 / (2.0 * sigma - rho)
        steps.append((nxt * rho, 2.0 * nxt / delta))
        rho = nxt
    return theta, steps


def iota(shape, dim):
    return lax.broadcasted_iota(jnp.int32, shape, dim)


def indicator(cond, value=1.0):
    return jnp.where(cond, value, 0.0).astype(BF16)


def mm(v, w):
    hi = v.astype(BF16)
    lo = (v - hi.astype(F32)).astype(BF16)
    return jnp.dot(hi, w, preferred_element_type=F32) + jnp.dot(
        lo, w, preferred_element_type=F32
    )


def mix(coup, scale, mass, u, d, k):
    out = []
    for c in range(3):
        a = (coup[c][0] * scale) * u[0]
        a = a + (coup[c][1] * scale) * u[1]
        a = a + (coup[c][2] * scale) * u[2]
        a = a + mass * d[c]
        out.append(k * a)
    return out


def flat_box(chunks, nz):
    rows = chunks[0].shape[0]
    lane = iota(chunks[0].shape, 1)
    zpos = lane & (nz - 1)
    s = []
    for v in chunks:
        v = v + pltpu.roll(v, 1, 0) + pltpu.roll(v, rows - 1, 0)
        s.append(
            v
            + jnp.where(zpos == 0, 0.0, pltpu.roll(v, 1, 1))
            + jnp.where(zpos == nz - 1, 0.0, pltpu.roll(v, 127, 1))
        )
    up = [pltpu.roll(v, nz, 1) for v in s]
    down = [pltpu.roll(v, 128 - nz, 1) for v in s]
    out = []
    for j, v in enumerate(s):
        before = up[j - 1] if j > 0 else 0.0
        after = down[j + 1] if j + 1 < len(s) else 0.0
        out.append(
            v
            + jnp.where(lane < nz, before, up[j])
            + jnp.where(lane >= 128 - nz, after, down[j])
        )
    return out


def flat_box_wide(chunks, nz):
    rows = chunks[0].shape[0]
    lane = iota(chunks[0].shape, 1)
    zpos = lane & (nz - 1)

    def shifted(v, y):
        mid = pltpu.roll(v, y % 128, 1) if y else v
        return (
            mid
            + jnp.where(zpos == 0, 0.0, pltpu.roll(v, (y + 1) % 128, 1))
            + jnp.where(zpos == nz - 1, 0.0, pltpu.roll(v, (y - 1) % 128, 1))
        )

    xs = [v + pltpu.roll(v, 1, 0) + pltpu.roll(v, rows - 1, 0) for v in chunks]
    up = [shifted(v, nz) for v in xs]
    down = [shifted(v, -nz) for v in xs]
    out = []
    for j, v in enumerate(xs):
        before = up[j - 1] if j > 0 else 0.0
        after = down[j + 1] if j + 1 < len(xs) else 0.0
        out.append(
            shifted(v, 0)
            + jnp.where(lane < nz, before, up[j])
            + jnp.where(lane >= 128 - nz, after, down[j])
        )
    return out


def flat_smooth(f, kappa, coup, level, nz, want_rest):
    theta, steps = chebyshev(level)
    scale = 4.0**-level / 26.0
    n = len(kappa)

    def apply(r, d):
        box = flat_box if n > 1 else flat_box_wide
        boxes = [box(d[c], nz) for c in range(3)]
        new = [[None] * n for _ in range(3)]
        for j in range(n):
            u = [27.0 * d[c][j] - boxes[c][j] for c in range(3)]
            a = mix(coup, scale, MASS, u, [d[c][j] for c in range(3)], kappa[j])
            for c in range(3):
                new[c][j] = r[c][j] - a[c]
        return new

    r = f
    d = [[v * (1.0 / theta) for v in f[c]] for c in range(3)]
    x = d
    for a, b in steps:
        r = apply(r, d)
        d = [[a * d[c][j] + b * r[c][j] for j in range(n)] for c in range(3)]
        x = [[x[c][j] + d[c][j] for j in range(n)] for c in range(3)]
    if want_rest:
        r = apply(r, d)
    return x, r


def kernel(
    nw,
    nn,
    res,
    stiff,
    coup_hbm,
    acc0,
    acc1,
    acc2,
    tail_out,
    f0b,
    k0b,
    r0,
    d1,
    d2,
    d3,
    t0,
    g1b,
    r1,
    e1,
    e2,
    t1,
    u_lo,
    u_hi,
    g2b,
    t2,
    v2,
    h3b,
    h3sb,
    t3,
    z4,
    m01,
    m12,
    m23,
    m34,
    p1,
    p2,
    p34,
    coup_ref,
    local_sem,
    ready_sem,
    s0,
    q0,
    s1,
    q1,
    s2,
    q2,
    s3,
    q3,
    s4,
    q4,
):
    w = lax.axis_index("wide")
    n = lax.axis_index("narrow")
    acc = [acc0, acc1, acc2]
    f0, k0, g1, g2, h3, h3s = (b.at[0] for b in (f0b, k0b, g1b, g2b, h3b, h3sb))

    def pair_of(i):
        return i + 1 - 2 * lax.rem(i, 2)

    def out_of(pos, off, size):
        if off == 0:
            return jnp.bool_(False)
        return pos + off >= size if off > 0 else pos + off < 0

    targets = {}

    def target(ow, on):
        if (ow, on) in targets:
            return targets[ow, on]
        w_out, n_out = out_of(w, ow, nw), out_of(n, on, nn)
        if on == 0:
            tw = jnp.where(w_out, w, w + ow)
            tn = jnp.where(w_out, pair_of(n), n)
            away = w_out
        elif ow == 0:
            tw = jnp.where(n_out, pair_of(w), w)
            tn = jnp.where(n_out, n, n + on)
            away = n_out
        else:
            w_end, n_end = (nw - 1 if ow > 0 else 0), (nn - 1 if on > 0 else 0)
            both = jnp.logical_and(w_out, n_out)
            away = jnp.logical_or(w_out, n_out)
            w_near, n_near = w == w_end - ow, n == n_end - on
            tw = jnp.where(
                both,
                w - ow,
                jnp.where(
                    w_out,
                    w,
                    jnp.where(n_out, jnp.where(w_near, w + ow, pair_of(w)), w + ow),
                ),
            )
            tn = jnp.where(
                both,
                n,
                jnp.where(
                    w_out,
                    jnp.where(n_near, n + on, pair_of(n)),
                    jnp.where(n_out, jnp.where(w_near, n - on, n), n + on),
                ),
            )
        targets[ow, on] = tw, tn, jnp.where(away, 1, 0)
        return targets[ow, on]

    def remote(src, dst, where, send, recv, sems, ow, on):
        tw, tn, away = target(ow, on)
        mine, other = sems
        return pltpu.make_async_remote_copy(
            src_ref=src,
            dst_ref=dst.at[(away,) + where],
            send_sem=send.at[mine],
            recv_sem=recv.at[mine + (other - mine) * away],
            device_id={"wide": tw, "narrow": tn},
            device_id_type=MESH,
        )

    def landed(buf, where, send, recv, mine):
        return pltpu.make_async_remote_copy(
            src_ref=buf.at[(0,) + where],
            dst_ref=buf.at[(0,) + where],
            send_sem=send.at[mine],
            recv_sem=recv.at[mine],
            device_id={"wide": w, "narrow": n},
            device_id_type=MESH,
        )

    own_f = pltpu.make_async_copy(res, f0.at[:, 4:20, 0:16, :], local_sem.at[0])
    own_k = pltpu.make_async_copy(stiff, k0.at[4:20, 0:16, :], local_sem.at[1])
    own_c = pltpu.make_async_copy(coup_hbm, coup_ref, local_sem.at[2])
    own_f.start()
    own_k.start()
    own_c.start()

    h3[...] = jnp.zeros_like(h3)
    h3s[...] = jnp.zeros_like(h3s)

    def tell(sem, offsets):
        for ow, on in offsets:
            tw, tn, _ = target(ow, on)
            pl.semaphore_signal(
                sem,
                inc=1,
                device_id={"wide": tw, "narrow": tn},
                device_id_type=MESH,
            )

    barrier = pltpu.get_barrier_semaphore()
    tell(barrier, AXIAL)
    g1[...] = jnp.zeros_like(g1)
    g2[...] = jnp.zeros_like(g2)
    own_f.wait()
    own_k.wait()
    pl.semaphore_wait(barrier, len(AXIAL))

    def copies0(i, ow, on):
        sx, dx = {0: (0, 4), 1: (12, 0), -1: (0, 20)}[ow]
        sy, dy = {0: (0, 0), 1: (12, 20), -1: (0, 16)}[on]
        nx, ny = (16 if ow == 0 else 4), (16 if on == 0 else 4)
        fs = (slice(None), slice(4 + sx, 4 + sx + nx), slice(sy, sy + ny))
        fd = (slice(None), slice(dx, dx + nx), slice(dy, dy + ny))
        if ow > 0:
            sx, dx = sx + 1, dx + 1
        if on > 0:
            sy, dy = sy + 1, dy + 1
        nx, ny = (16 if ow == 0 else 3), (16 if on == 0 else 3)
        ks = (slice(4 + sx, 4 + sx + nx), slice(sy, sy + ny))
        kd = (slice(dx, dx + nx), slice(dy, dy + ny))
        return [
            (f0.at[fs], f0b, fd, s0, q0, i),
            (k0.at[ks], k0b, kd, s0, q0, 8 + i),
        ]

    def copies1(i, ow, on):
        sx, dx = {0: ((2, 6), (2, 6)), 1: ((4, 6), (0, 2)), -1: ((2, 4), (6, 8))}[ow]
        sy, dy = {0: ((0, 8), (0, 8)), 1: ((4, 8), (12, 16)), -1: ((0, 4), (8, 12))}[on]
        sx, dx, sy, dy = slice(*sx), slice(*dx), slice(*sy), slice(*dy)
        return [
            (g1.at[0:3, sx, sy], g1b, (slice(0, 3), dx, dy), s1, q1, i),
            (g1.at[3, sx, sy], g1b, (3, dx, dy), s1, q1, 8 + i),
        ]

    def copies2(i, ow, on):
        dx = slice(4 - 4 * ow, 8 - 4 * ow)
        dy = slice(128 - 128 * on, 256 - 128 * on)
        return [(g2.at[:, 4:8, 128:256], g2b, (slice(None), dx, dy), s2, q2, i)]

    def copies3(i, ow, on):
        rows = slice(10 - 2 * ow, 12 - 2 * ow)
        return [(h3.at[10:12, :], h3b, (rows,), s3, q3, i)]

    def copies4(i, ow, on):
        rows = slice(0, 22)
        return [(h3.at[rows], h3sb, (5 - on, rows), s4, q4, i)]

    def start(copies, offsets, chosen=None, part=slice(None)):
        for i, (ow, on) in enumerate(offsets):
            if chosen is None or i in chosen:
                opposite = offsets.index((-ow, -on))
                for src, dst, where, send, recv, mine in copies(i, ow, on)[part]:
                    sems = mine, mine + opposite - i
                    remote(src, dst, where, send, recv, sems, ow, on).start()

    def arrive(copies, offsets, chosen=None):
        for i, (ow, on) in enumerate(offsets):
            if chosen is None or i in chosen:
                for src, dst, where, send, recv, mine in copies(i, ow, on):
                    landed(dst, where, send, recv, mine).wait_recv()

    def sent(copies, offsets):
        for i, (ow, on) in enumerate(offsets):
            for src, dst, where, send, recv, mine in copies(i, ow, on):
                landed(dst, where, send, recv, mine).wait_send()

    along_wide = [(o, 0) for o in WINDOW]
    along_narrow = [(0, o) for o in WINDOW]

    start(copies0, NEIGHBOURS, (4, 5), slice(0, 1))
    start(copies0, NEIGHBOURS, (6, 7))
    tell(ready_sem, AXIAL)
    pl.semaphore_wait(ready_sem, len(AXIAL))
    start(copies0, NEIGHBOURS, (0, 1, 2, 3))
    start(copies0, NEIGHBOURS, (4, 5), slice(1, 2))

    @pl.when(w == 0)
    def _():
        f0[:, 0:4] = jnp.zeros((3, 4, 24, 128), F32)
        k0[0:4] = jnp.zeros((4, 24, 128), F32)

    @pl.when(w == nw - 1)
    def _():
        f0[:, 20:24] = jnp.zeros((3, 4, 24, 128), F32)
        k0[20:24] = jnp.zeros((4, 24, 128), F32)

    @pl.when(n == 0)
    def _():
        f0[:, :, 20:24, :] = jnp.zeros((3, 24, 4, 128), F32)
        k0[:, 20:24, :] = jnp.zeros((24, 4, 128), F32)

    @pl.when(n == nn - 1)
    def _():
        f0[:, :, 16:20, :] = jnp.zeros((3, 24, 4, 128), F32)
        k0[:, 16:20, :] = jnp.zeros((24, 4, 128), F32)

    r, c = iota((256, 128), 0), iota((256, 128), 1)
    m01[...] = indicator(((r >> 7) == (c >> 6)) & (((r & 127) >> 1) == (c & 63)), 0.125)
    r, c = iota((512, 128), 0), iota((512, 128), 1)
    m12[...] = indicator(((r >> 7) == (c >> 5)) & (((r & 63) >> 1) == (c & 31)), 0.125)
    m23[...] = indicator(
        ((r >> 7) == (c >> 5))
        & (((r >> 6) & 1) == ((c >> 4) & 1))
        & (((r & 31) >> 1) == (c & 15)),
        0.125,
    )
    r, c = iota((384, 128), 0), iota((384, 128), 1)
    m34[...] = indicator(((r >> 5) == (c >> 3)) & (((r & 15) >> 1) == (c & 7)), 0.125)
    r, c = iota((128, 256), 0), iota((128, 256), 1)
    p1[...] = indicator(((r >> 6) == (c >> 7)) & ((r & 63) == ((c & 127) >> 1)))
    r, c = iota((128, 512), 0), iota((128, 512), 1)
    p2[...] = indicator(((r >> 5) == (c >> 7)) & ((r & 31) == ((c & 127) >> 2)))
    r, c = iota((256, 256), 0), iota((256, 256), 1)
    fine = ((r >> 4) == (2 + (c >> 7))) & ((r & 15) == ((c & 127) >> 3))
    coarse = (r >= 128 + 40) & (r < 128 + 48) & ((r & 7) == ((c & 127) >> 4))
    p34[...] = indicator(fine | coarse)

    own_c.wait()
    coup = [[coup_ref[i, j] for j in range(3)] for i in range(3)]

    for i in range(8):
        t0[pl.ds(384 + 16 * i, 16), :] = (
            k0[4 + 2 * i, 0:16, :] + k0[5 + 2 * i, 0:16, :]
        )

    def halved(first, count):
        s = t0[pl.ds(first, count, stride=2), :] + t0[pl.ds(first + 1, count, stride=2), :]
        s = s.reshape(count // 16, 2, 8, 128)
        pair = [s[:, u].reshape(count // 2, 128) for u in range(2)]
        return mm(jnp.concatenate(pair, axis=1), m01[...])

    g1[3, 2:6, 0:8, :] = halved(384, 64).reshape(4, 8, 128)
    for p in range(4):
        t1[pl.ds(96 + 8 * p, 8), :] = g1[3, 2 + p, 0:8, :]

    theta0, steps0 = chebyshev(0)
    lane24 = iota((24, 128), 1)
    lane16 = iota((16, 128), 1)
    fields = [f0, d1, d2, d3]

    def sweep0(k, starts, count):
        d = fields[k]
        over = 1.0 / theta0 if k == 0 else 1.0
        scale, mass = over / 26.0, over * MASS
        rest = f0 if k == 0 else r0
        rows, lane = (24, lane24) if k < 3 else (16, lane16)
        for lo in starts:
            for i in range(lo, lo + count, 2):
                mids, boxes = [[], []], [[], []]
                for c in range(3):
                    a, b = d[c, i], d[c, i + 1]
                    both = a + b
                    for u, (mid, x) in enumerate(((a, d[c, i - 1]), (b, d[c, i + 2]))):
                        s = both + x
                        s = s + pltpu.roll(s, 1, 0) + pltpu.roll(s, 23, 0)
                        s = s[0:rows]
                        s = (
                            s
                            + jnp.where(lane == 0, 0.0, pltpu.roll(s, 1, 1))
                            + jnp.where(lane == 127, 0.0, pltpu.roll(s, 127, 1))
                        )
                        mids[u].append(mid[0:rows])
                        boxes[u].append(s)
                new = []
                for u in range(2):
                    us = [27.0 * mids[u][c] - boxes[u][c] for c in range(3)]
                    a = mix(coup, scale, mass, us, mids[u], k0[i + u, 0:rows])
                    new.append([rest[c, i + u, 0:rows] - a[c] for c in range(3)])
                    if k < 3:
                        ca, cb = steps0[k]
                        for c in range(3):
                            r0[c, i + u] = new[u][c]
                            fields[k + 1][c, i + u] = (ca * over) * mids[u][c] + cb * new[u][c]
                if k == 3:
                    for c in range(3):
                        t0[pl.ds(128 * c + 8 * (i - 4), 16), :] = new[0][c] + new[1][c]

    arrive(copies0, NEIGHBOURS, (6, 7))
    for k in range(4):
        sweep0(k, (5 + k,), 14 - 2 * k)
    arrive(copies0, NEIGHBOURS, (0, 1, 2, 3, 4, 5))
    start(copies1, NEIGHBOURS, None, slice(1, 2))
    for k in range(4):
        sweep0(k, (1 + k, 19 - k), 4)
    g1[0:3, 2:6, 0:8, :] = halved(0, 192).reshape(3, 4, 8, 128)
    start(copies1, NEIGHBOURS, None, slice(0, 1))
    sent(copies0, NEIGHBOURS)

    def sum0(i, carry):
        for c in range(3):
            acc[c][i] = (
                f0[c, 4 + i, 0:16, :] * (1.0 / theta0)
                + d1[c, 4 + i, 0:16, :]
                + d2[c, 4 + i, 0:16, :]
                + d3[c, 4 + i, 0:16, :]
            )
        return carry

    lax.fori_loop(0, 16, sum0, 0)

    arrive(copies1, NEIGHBOURS)

    theta1, steps1 = chebyshev(1)
    lower = lane16 < 64
    zpos1 = lane16 & 63

    def plane1(p, d, scale, mass):
        us, mids = [], []
        for c in range(3):
            mid = d[c, p]
            swap = mid + jnp.where(lower, d[c, min(p + 1, 7)], d[c, max(p - 1, 0)])
            up = pltpu.roll(mid, 1, 1) + pltpu.roll(swap, 65, 1)
            down = pltpu.roll(mid, 127, 1) + pltpu.roll(swap, 63, 1)
            s = mid + pltpu.roll(swap, 64, 1)
            s = s + jnp.where(zpos1 == 0, 0.0, up) + jnp.where(zpos1 == 63, 0.0, down)
            s = s + pltpu.roll(s, 1, 0) + pltpu.roll(s, 15, 0)
            us.append(27.0 * mid - s)
            mids.append(mid)
        return mids, mix(coup, scale, mass, us, mids, g1[3, p])

    x1 = {}
    fields1 = [g1, e1, e2, e1]
    for k, (lo, hi) in enumerate([(0, 8), (1, 7), (1, 7), (2, 6)]):
        d = fields1[k]
        over = 1.0 / theta1 if k == 0 else 1.0
        scale, mass = over / (4.0 * 26.0), over * MASS
        for p in range(lo, hi):
            mids, a = plane1(p, d, scale, mass)
            for c in range(3):
                new = (g1 if k == 0 else r1)[c, p] - a[c]
                if k < 3:
                    ca, cb = steps1[k]
                    r1[c, p] = new
                    fields1[k + 1][c, p] = (ca * over) * mids[c] + cb * new
                else:
                    t1[pl.ds(32 * c + 8 * (p - 2), 8), :] = new[0:8]
                if 2 <= p < 6:
                    part = (mids[c] * over)[0:8]
                    x1[c, p] = part if k == 0 else x1[c, p] + part

    ys = [t1[pl.ds(y, 16, stride=8), :] for y in range(8)]
    ys = jnp.concatenate([ys[2 * j] + ys[2 * j + 1] for j in range(4)], axis=1)
    blk = mm(ys, m12[...])
    for c in range(4):
        g2[c, 4:8, 128:256] = blk[4 * c : 4 * c + 4]
    start(copies2, NEIGHBOURS)
    sent(copies1, NEIGHBOURS)

    rows = jnp.concatenate([x1[c, p] for c in range(3) for p in range(2, 6)], axis=0)
    rep = mm(rows, p1[...])
    u_lo[pl.ds(0, 96, stride=2), :] = rep[:, 0:128]
    u_lo[pl.ds(1, 96, stride=2), :] = rep[:, 0:128]
    u_hi[pl.ds(0, 96, stride=2), :] = rep[:, 128:256]
    u_hi[pl.ds(1, 96, stride=2), :] = rep[:, 128:256]
    for c in range(3):
        for p in range(4):
            rows_cp = pl.ds(16 * (4 * c + p), 16)
            for j in range(4):
                acc[c][4 * p + j] += (u_lo if j < 2 else u_hi)[rows_cp, :]

    arrive(copies2, NEIGHBOURS)

    f2 = [[g2[c, :, 128 * j : 128 * j + 128] for j in range(3)] for c in range(4)]
    x2, r2 = flat_smooth(f2[:3], f2[3], coup, 2, 32, True)

    t2[...] = mm(
        jnp.concatenate([r2[0][1], r2[1][1], r2[2][1], f2[3][1]], axis=1), m23[...]
    )
    h3[10:12, :] = t2[pl.ds(4, 2, stride=2), :] + t2[pl.ds(5, 2, stride=2), :]
    start(copies3, along_wide)
    sent(copies2, NEIGHBOURS)

    for c in range(3):
        t3[4 * c : 4 * c + 4, 0:128] = x2[c][1][4:8]
    rep = mm(t3[0:16, 0:128], p2[...])
    for y in range(16):
        j = y // 4
        v2[pl.ds(y, 16, stride=16), :] = rep[:, 128 * j : 128 * j + 128]
    for c in range(3):
        for k in range(4):
            part = v2[pl.ds(16 * (4 * c + k), 16), :]
            for j in range(4):
                acc[c][4 * k + j] += part

    arrive(copies3, along_wide)
    start(copies4, along_narrow)
    sent(copies3, along_wide)
    arrive(copies4, along_narrow)
    sent(copies4, along_narrow)

    lane3 = iota((24, 128), 1)
    slots = [h3s[j] if j != 5 else h3[...] for j in range(11)]
    f3 = [[None] * 3 for _ in range(4)]
    for c in range(4):
        for v in range(3):
            out = jnp.zeros((24, 128), F32)
            for q in range(4):
                j = 4 * v + q
                if j < 11:
                    turn = 32 * ((q - c) % 4)
                    part = pltpu.roll(slots[j], turn, 1) if turn else slots[j]
                    out = jnp.where((lane3 >> 5) == q, part, out)
            f3[c][v] = out
    x3, r3 = flat_smooth(f3[:3], f3[3], coup, 3, 16, True)

    z4[...] = mm(
        jnp.concatenate(
            [jnp.concatenate(r3[c] if c < 3 else f3[3], axis=1) for c in range(4)],
            axis=0,
        ),
        m34[...],
    )
    f4 = []
    for c in range(4):
        even, odd = (z4[pl.ds(24 * c + 4 + u, 8, stride=2), :] for u in range(2))
        f4.append([even + odd])
    x4, _ = flat_smooth(f4[:3], f4[3], coup, 4, 8, False)

    for c in range(3):
        t3[2 * c : 2 * c + 2, 0:128] = x3[c][1][10:12]
        t3[2 * c : 2 * c + 2, 128:256] = jnp.broadcast_to(x4[c][0][3:4], (2, 128))
    tail_out[...] = mm(t3[0:16, 0:256], p34[...])[0:8]


def solution(mesh):
    nw, nn = mesh.shape["wide"], mesh.shape["narrow"]

    def vm(*shape):
        return pltpu.VMEM(shape, F32)

    def mat(*shape):
        return pltpu.VMEM(shape, BF16)

    dma = pltpu.SemaphoreType.DMA
    scratch = [
        vm(2, 3, 24, 24, 128),
        vm(2, 24, 24, 128),
        vm(3, 24, 24, 128),
        vm(3, 24, 24, 128),
        vm(3, 24, 24, 128),
        vm(3, 24, 24, 128),
        vm(512, 128),
        vm(2, 4, 8, 16, 128),
        vm(3, 8, 16, 128),
        vm(3, 8, 16, 128),
        vm(3, 8, 16, 128),
        vm(128, 128),
        vm(192, 128),
        vm(192, 128),
        vm(2, 4, 16, 384),
        vm(16, 128),
        vm(256, 128),
        vm(2, 24, 128),
        vm(2, 11, 24, 128),
        vm(16, 256),
        vm(96, 128),
        mat(256, 128),
        mat(512, 128),
        mat(512, 128),
        mat(384, 128),
        mat(128, 256),
        mat(128, 512),
        mat(256, 256),
        pltpu.SMEM((3, 3), F32),
        dma((3,)),
        pltpu.SemaphoreType.REGULAR,
        dma((16,)),
        dma((16,)),
        dma((16,)),
        dma((16,)),
        dma((8,)),
        dma((8,)),
        dma((10,)),
        dma((10,)),
        dma((10,)),
        dma((10,)),
    ]

    def per_device(residual, stiffness, coupling):
        hbm = pl.BlockSpec(memory_space=pltpu.HBM)
        vmem = pl.BlockSpec(memory_space=pltpu.VMEM)
        *acc, tail = pl.pallas_call(
            functools.partial(kernel, nw, nn),
            out_shape=(
                *[jax.ShapeDtypeStruct((16, 16, 128), F32)] * 3,
                jax.ShapeDtypeStruct((8, 256), F32),
            ),
            in_specs=[hbm, hbm, hbm],
            out_specs=(vmem,) * 4,
            scratch_shapes=scratch,
            compiler_params=pltpu.CompilerParams(
                collective_id=0,
                has_side_effects=True,
                vmem_limit_bytes=(53 * 1024 + 450) * 1024,
            ),
        )(residual, stiffness, coupling)
        tail = tail[0:6].reshape(3, 2, 1, 2, 1, 128)
        return (jnp.stack(acc).reshape(3, 2, 8, 2, 8, 128) + tail).reshape(3, 16, 16, 128)

    return jax.shard_map(
        per_device,
        mesh=mesh,
        in_specs=(P(None, "wide", "narrow", None), P("wide", "narrow", None), P()),
        out_specs=P(None, "wide", "narrow", None),
        check_vma=False,
    )
```

```python
import functools

import jax
import jax.numpy as jnp
from jax import lax
from jax.experimental import pallas as pl
from jax.experimental.pallas import tpu as pltpu
from jax.sharding import PartitionSpec as P

LEVELS = 4
MASS = 0.001
RATIO = 8.0
MESH = pl.DeviceIdType.MESH
NEIGHBOURS = [(1, 1), (1, -1), (-1, 1), (-1, -1), (1, 0), (-1, 0), (0, 1), (0, -1)]
NEAR = NEIGHBOURS + [(2, 0), (-2, 0), (0, 2), (0, -2)]
WINDOW = [o for k in range(5, 0, -1) for o in (k, -k)]
F32 = jnp.float32
BF16 = jnp.bfloat16


def chebyshev(level):
    top = 4.0 * (2.8 / 4.0**level + MASS)
    theta = (top + top / RATIO) / 2.0
    delta = (top - top / RATIO) / 2.0
    sigma = theta / delta
    rho = 1.0 / sigma
    steps = []
    for _ in range(3):
        nxt = 1.0 / (2.0 * sigma - rho)
        steps.append((nxt * rho, 2.0 * nxt / delta))
        rho = nxt
    return theta, steps


def iota(shape, dim):
    return lax.broadcasted_iota(jnp.int32, shape, dim)


def indicator(cond, value=1.0):
    return jnp.where(cond, value, 0.0).astype(BF16)


def mm(v, w):
    hi = v.astype(BF16)
    lo = (v - hi.astype(F32)).astype(BF16)
    return jnp.dot(hi, w, preferred_element_type=F32) + jnp.dot(
        lo, w, preferred_element_type=F32
    )


def mix(coup, scale, mass, u, d, k):
    out = []
    for c in range(3):
        a = (coup[c][0] * scale) * u[0]
        a = a + (coup[c][1] * scale) * u[1]
        a = a + (coup[c][2] * scale) * u[2]
        a = a + mass * d[c]
        out.append(k * a)
    return out


def flat_box(chunks, nz):
    rows = chunks[0].shape[0]
    lane = iota(chunks[0].shape, 1)
    zpos = lane & (nz - 1)
    s = []
    for v in chunks:
        v = v + pltpu.roll(v, 1, 0) + pltpu.roll(v, rows - 1, 0)
        s.append(
            v
            + jnp.where(zpos == 0, 0.0, pltpu.roll(v, 1, 1))
            + jnp.where(zpos == nz - 1, 0.0, pltpu.roll(v, 127, 1))
        )
    up = [pltpu.roll(v, nz, 1) for v in s]
    down = [pltpu.roll(v, 128 - nz, 1) for v in s]
    out = []
    for j, v in enumerate(s):
        before = up[j - 1] if j > 0 else 0.0
        after = down[j + 1] if j + 1 < len(s) else 0.0
        out.append(
            v
            + jnp.where(lane < nz, before, up[j])
            + jnp.where(lane >= 128 - nz, after, down[j])
        )
    return out


def flat_box_wide(chunks, nz):
    rows = chunks[0].shape[0]
    lane = iota(chunks[0].shape, 1)
    zpos = lane & (nz - 1)

    def shifted(v, y):
        mid = pltpu.roll(v, y % 128, 1) if y else v
        return (
            mid
            + jnp.where(zpos == 0, 0.0, pltpu.roll(v, (y + 1) % 128, 1))
            + jnp.where(zpos == nz - 1, 0.0, pltpu.roll(v, (y - 1) % 128, 1))
        )

    xs = [v + pltpu.roll(v, 1, 0) + pltpu.roll(v, rows - 1, 0) for v in chunks]
    up = [shifted(v, nz) for v in xs]
    down = [shifted(v, -nz) for v in xs]
    out = []
    for j, v in enumerate(xs):
        before = up[j - 1] if j > 0 else 0.0
        after = down[j + 1] if j + 1 < len(xs) else 0.0
        out.append(
            shifted(v, 0)
            + jnp.where(lane < nz, before, up[j])
            + jnp.where(lane >= 128 - nz, after, down[j])
        )
    return out


def flat_smooth(f, kappa, coup, level, nz, want_rest):
    theta, steps = chebyshev(level)
    scale = 4.0**-level / 26.0
    n = len(kappa)

    def apply(r, d):
        box = flat_box if n > 1 else flat_box_wide
        boxes = [box(d[c], nz) for c in range(3)]
        new = [[None] * n for _ in range(3)]
        for j in range(n):
            u = [27.0 * d[c][j] - boxes[c][j] for c in range(3)]
            a = mix(coup, scale, MASS, u, [d[c][j] for c in range(3)], kappa[j])
            for c in range(3):
                new[c][j] = r[c][j] - a[c]
        return new

    r = f
    d = [[v * (1.0 / theta) for v in f[c]] for c in range(3)]
    x = d
    for a, b in steps:
        r = apply(r, d)
        d = [[a * d[c][j] + b * r[c][j] for j in range(n)] for c in range(3)]
        x = [[x[c][j] + d[c][j] for j in range(n)] for c in range(3)]
    if want_rest:
        r = apply(r, d)
    return x, r


def kernel(
    nw,
    nn,
    res,
    stiff,
    coup_hbm,
    acc0,
    acc1,
    acc2,
    tail_out,
    f0b,
    k0b,
    r0,
    d1,
    d2,
    d3,
    t0,
    g1b,
    r1,
    e1,
    e2,
    t1,
    u_lo,
    u_hi,
    g2b,
    t2,
    v2,
    h3b,
    h3sb,
    t3,
    z4,
    m01,
    m12,
    m23,
    m34,
    p1,
    p2,
    p34,
    coup_ref,
    local_sem,
    s0,
    q0,
    s1,
    q1,
    s2,
    q2,
    s3,
    q3,
    s4,
    q4,
):
    w = lax.axis_index("wide")
    n = lax.axis_index("narrow")
    acc = [acc0, acc1, acc2]
    f0, k0, g1, g2, h3, h3s = (b.at[0] for b in (f0b, k0b, g1b, g2b, h3b, h3sb))

    def pair_of(i):
        return i + 1 - 2 * lax.rem(i, 2)

    def out_of(pos, off, size):
        if off == 0:
            return jnp.bool_(False)
        return pos + off >= size if off > 0 else pos + off < 0

    targets = {}

    def target(ow, on):
        if (ow, on) in targets:
            return targets[ow, on]
        w_out, n_out = out_of(w, ow, nw), out_of(n, on, nn)
        if on == 0:
            tw = jnp.where(w_out, w, w + ow)
            tn = jnp.where(w_out, pair_of(n), n)
            away = w_out
        elif ow == 0:
            tw = jnp.where(n_out, pair_of(w), w)
            tn = jnp.where(n_out, n, n + on)
            away = n_out
        else:
            w_end, n_end = (nw - 1 if ow > 0 else 0), (nn - 1 if on > 0 else 0)
            both = jnp.logical_and(w_out, n_out)
            away = jnp.logical_or(w_out, n_out)
            w_near, n_near = w == w_end - ow, n == n_end - on
            tw = jnp.where(
                both,
                w - ow,
                jnp.where(
                    w_out,
                    w,
                    jnp.where(n_out, jnp.where(w_near, w + ow, pair_of(w)), w + ow),
                ),
            )
            tn = jnp.where(
                both,
                n,
                jnp.where(
                    w_out,
                    jnp.where(n_near, n + on, pair_of(n)),
                    jnp.where(n_out, jnp.where(w_near, n - on, n), n + on),
                ),
            )
        targets[ow, on] = tw, tn, jnp.where(away, 1, 0)
        return targets[ow, on]

    def remote(src, dst, where, send, recv, sems, ow, on):
        tw, tn, away = target(ow, on)
        mine, other = sems
        return pltpu.make_async_remote_copy(
            src_ref=src,
            dst_ref=dst.at[(away,) + where],
            send_sem=send.at[mine],
            recv_sem=recv.at[mine + (other - mine) * away],
            device_id={"wide": tw, "narrow": tn},
            device_id_type=MESH,
        )

    def landed(buf, where, send, recv, mine):
        return pltpu.make_async_remote_copy(
            src_ref=buf.at[(0,) + where],
            dst_ref=buf.at[(0,) + where],
            send_sem=send.at[mine],
            recv_sem=recv.at[mine],
            device_id={"wide": w, "narrow": n},
            device_id_type=MESH,
        )

    own_f = pltpu.make_async_copy(res, f0.at[:, 4:20, 0:16, :], local_sem.at[0])
    own_k = pltpu.make_async_copy(stiff, k0.at[4:20, 0:16, :], local_sem.at[1])
    own_c = pltpu.make_async_copy(coup_hbm, coup_ref, local_sem.at[2])
    own_f.start()
    own_k.start()
    own_c.start()

    h3[...] = jnp.zeros_like(h3)
    h3s[...] = jnp.zeros_like(h3s)

    def tell(sem, offsets):
        for ow, on in offsets:
            tw, tn, _ = target(ow, on)
            pl.semaphore_signal(
                sem,
                inc=1,
                device_id={"wide": tw, "narrow": tn},
                device_id_type=MESH,
            )

    barrier = pltpu.get_barrier_semaphore()
    tell(barrier, NEAR)
    g1[...] = jnp.zeros_like(g1)
    g2[...] = jnp.zeros_like(g2)
    own_f.wait()
    own_k.wait()
    pl.semaphore_wait(barrier, len(NEAR))

    def copies0(i, ow, on):
        sx, dx = {0: (0, 4), 1: (12, 0), -1: (0, 20)}[ow]
        sy, dy = {0: (0, 0), 1: (12, 20), -1: (0, 16)}[on]
        nx, ny = (16 if ow == 0 else 4), (16 if on == 0 else 4)
        fs = (slice(None), slice(4 + sx, 4 + sx + nx), slice(sy, sy + ny))
        fd = (slice(None), slice(dx, dx + nx), slice(dy, dy + ny))
        if ow > 0:
            sx, dx = sx + 1, dx + 1
        if on > 0:
            sy, dy = sy + 1, dy + 1
        nx, ny = (16 if ow == 0 else 3), (16 if on == 0 else 3)
        ks = (slice(4 + sx, 4 + sx + nx), slice(sy, sy + ny))
        kd = (slice(dx, dx + nx), slice(dy, dy + ny))
        return [
            (f0.at[fs], f0b, fd, s0, q0, i),
            (k0.at[ks], k0b, kd, s0, q0, 8 + i),
        ]

    def copies1(i, ow, on):
        sx, dx = {0: ((2, 6), (2, 6)), 1: ((4, 6), (0, 2)), -1: ((2, 4), (6, 8))}[ow]
        sy, dy = {0: ((0, 8), (0, 8)), 1: ((4, 8), (12, 16)), -1: ((0, 4), (8, 12))}[on]
        sx, dx, sy, dy = slice(*sx), slice(*dx), slice(*sy), slice(*dy)
        return [
            (g1.at[0:3, sx, sy], g1b, (slice(0, 3), dx, dy), s1, q1, i),
            (g1.at[3, sx, sy], g1b, (3, dx, dy), s1, q1, 8 + i),
        ]

    def copies2(i, ow, on):
        dx = slice(4 - 4 * ow, 8 - 4 * ow)
        dy = slice(128 - 128 * on, 256 - 128 * on)
        return [(g2.at[:, 4:8, 128:256], g2b, (slice(None), dx, dy), s2, q2, i)]

    def copies3(i, ow, on):
        rows = slice(10 - 2 * ow, 12 - 2 * ow)
        return [(h3.at[10:12, :], h3b, (rows,), s3, q3, i)]

    def copies4(i, ow, on):
        rows = slice(0, 22)
        return [(h3.at[rows], h3sb, (5 - on, rows), s4, q4, i)]

    def start(copies, offsets, chosen=None, part=slice(None)):
        for i, (ow, on) in enumerate(offsets):
            if chosen is None or i in chosen:
                opposite = offsets.index((-ow, -on))
                for src, dst, where, send, recv, mine in copies(i, ow, on)[part]:
                    sems = mine, mine + opposite - i
                    remote(src, dst, where, send, recv, sems, ow, on).start()

    def arrive(copies, offsets, chosen=None):
        for i, (ow, on) in enumerate(offsets):
            if chosen is None or i in chosen:
                for src, dst, where, send, recv, mine in copies(i, ow, on):
                    landed(dst, where, send, recv, mine).wait_recv()

    def sent(copies, offsets):
        for i, (ow, on) in enumerate(offsets):
            for src, dst, where, send, recv, mine in copies(i, ow, on):
                landed(dst, where, send, recv, mine).wait_send()

    along_wide = [(o, 0) for o in WINDOW]
    along_narrow = [(0, o) for o in WINDOW]

    start(copies0, NEIGHBOURS, (6, 7))
    start(copies0, NEIGHBOURS, (0, 1, 2, 3))
    start(copies0, NEIGHBOURS, (4, 5))

    @pl.when(w == 0)
    def _():
        f0[:, 0:4] = jnp.zeros((3, 4, 24, 128), F32)
        k0[0:4] = jnp.zeros((4, 24, 128), F32)

    @pl.when(w == nw - 1)
    def _():
        f0[:, 20:24] = jnp.zeros((3, 4, 24, 128), F32)
        k0[20:24] = jnp.zeros((4, 24, 128), F32)

    @pl.when(n == 0)
    def _():
        f0[:, :, 20:24, :] = jnp.zeros((3, 24, 4, 128), F32)
        k0[:, 20:24, :] = jnp.zeros((24, 4, 128), F32)

    @pl.when(n == nn - 1)
    def _():
        f0[:, :, 16:20, :] = jnp.zeros((3, 24, 4, 128), F32)
        k0[:, 16:20, :] = jnp.zeros((24, 4, 128), F32)

    r, c = iota((256, 128), 0), iota((256, 128), 1)
    m01[...] = indicator(((r >> 7) == (c >> 6)) & (((r & 127) >> 1) == (c & 63)), 0.125)
    r, c = iota((512, 128), 0), iota((512, 128), 1)
    m12[...] = indicator(((r >> 7) == (c >> 5)) & (((r & 63) >> 1) == (c & 31)), 0.125)
    m23[...] = indicator(
        ((r >> 7) == (c >> 5))
        & (((r >> 6) & 1) == ((c >> 4) & 1))
        & (((r & 31) >> 1) == (c & 15)),
        0.125,
    )
    r, c = iota((384, 128), 0), iota((384, 128), 1)
    m34[...] = indicator(((r >> 5) == (c >> 3)) & (((r & 15) >> 1) == (c & 7)), 0.125)
    r, c = iota((128, 256), 0), iota((128, 256), 1)
    p1[...] = indicator(((r >> 6) == (c >> 7)) & ((r & 63) == ((c & 127) >> 1)))
    r, c = iota((128, 512), 0), iota((128, 512), 1)
    p2[...] = indicator(((r >> 5) == (c >> 7)) & ((r & 31) == ((c & 127) >> 2)))
    r, c = iota((256, 256), 0), iota((256, 256), 1)
    fine = ((r >> 4) == (2 + (c >> 7))) & ((r & 15) == ((c & 127) >> 3))
    coarse = (r >= 128 + 40) & (r < 128 + 48) & ((r & 7) == ((c & 127) >> 4))
    p34[...] = indicator(fine | coarse)

    own_c.wait()
    coup = [[coup_ref[i, j] for j in range(3)] for i in range(3)]

    for i in range(8):
        t0[pl.ds(384 + 16 * i, 16), :] = (
            k0[4 + 2 * i, 0:16, :] + k0[5 + 2 * i, 0:16, :]
        )

    def halved(first, count):
        s = t0[pl.ds(first, count, stride=2), :] + t0[pl.ds(first + 1, count, stride=2), :]
        s = s.reshape(count // 16, 2, 8, 128)
        pair = [s[:, u].reshape(count // 2, 128) for u in range(2)]
        return mm(jnp.concatenate(pair, axis=1), m01[...])

    g1[3, 2:6, 0:8, :] = halved(384, 64).reshape(4, 8, 128)
    for p in range(4):
        t1[pl.ds(96 + 8 * p, 8), :] = g1[3, 2 + p, 0:8, :]

    theta0, steps0 = chebyshev(0)
    lane24 = iota((24, 128), 1)
    lane16 = iota((16, 128), 1)
    fields = [f0, d1, d2, d3]

    def sweep0(k, starts, count):
        d = fields[k]
        over = 1.0 / theta0 if k == 0 else 1.0
        scale, mass = over / 26.0, over * MASS
        rest = f0 if k == 0 else r0
        rows, lane = (24, lane24) if k < 3 else (16, lane16)
        for lo in starts:
            for i in range(lo, lo + count, 2):
                mids, boxes = [[], []], [[], []]
                for c in range(3):
                    a, b = d[c, i], d[c, i + 1]
                    both = a + b
                    for u, (mid, x) in enumerate(((a, d[c, i - 1]), (b, d[c, i + 2]))):
                        s = both + x
                        s = s + pltpu.roll(s, 1, 0) + pltpu.roll(s, 23, 0)
                        s = s[0:rows]
                        s = (
                            s
                            + jnp.where(lane == 0, 0.0, pltpu.roll(s, 1, 1))
                            + jnp.where(lane == 127, 0.0, pltpu.roll(s, 127, 1))
                        )
                        mids[u].append(mid[0:rows])
                        boxes[u].append(s)
                new = []
                for u in range(2):
                    us = [27.0 * mids[u][c] - boxes[u][c] for c in range(3)]
                    a = mix(coup, scale, mass, us, mids[u], k0[i + u, 0:rows])
                    new.append([rest[c, i + u, 0:rows] - a[c] for c in range(3)])
                    if k < 3:
                        ca, cb = steps0[k]
                        for c in range(3):
                            r0[c, i + u] = new[u][c]
                            fields[k + 1][c, i + u] = (ca * over) * mids[u][c] + cb * new[u][c]
                if k == 3:
                    for c in range(3):
                        t0[pl.ds(128 * c + 8 * (i - 4), 16), :] = new[0][c] + new[1][c]

    arrive(copies0, NEIGHBOURS, (6, 7))
    for k in range(4):
        sweep0(k, (5 + k,), 14 - 2 * k)
    arrive(copies0, NEIGHBOURS, (0, 1, 2, 3, 4, 5))
    start(copies1, NEIGHBOURS, None, slice(1, 2))
    for k in range(4):
        sweep0(k, (1 + k, 19 - k), 4)
    g1[0:3, 2:6, 0:8, :] = halved(0, 192).reshape(3, 4, 8, 128)
    start(copies1, NEIGHBOURS, None, slice(0, 1))
    sent(copies0, NEIGHBOURS)

    def sum0(i, carry):
        for c in range(3):
            acc[c][i] = (
                f0[c, 4 + i, 0:16, :] * (1.0 / theta0)
                + d1[c, 4 + i, 0:16, :]
                + d2[c, 4 + i, 0:16, :]
                + d3[c, 4 + i, 0:16, :]
            )
        return carry

    lax.fori_loop(0, 16, sum0, 0)

    arrive(copies1, NEIGHBOURS)

    theta1, steps1 = chebyshev(1)
    lower = lane16 < 64
    zpos1 = lane16 & 63

    def plane1(p, d, scale, mass):
        us, mids = [], []
        for c in range(3):
            mid = d[c, p]
            swap = mid + jnp.where(lower, d[c, min(p + 1, 7)], d[c, max(p - 1, 0)])
            up = pltpu.roll(mid, 1, 1) + pltpu.roll(swap, 65, 1)
            down = pltpu.roll(mid, 127, 1) + pltpu.roll(swap, 63, 1)
            s = mid + pltpu.roll(swap, 64, 1)
            s = s + jnp.where(zpos1 == 0, 0.0, up) + jnp.where(zpos1 == 63, 0.0, down)
            s = s + pltpu.roll(s, 1, 0) + pltpu.roll(s, 15, 0)
            us.append(27.0 * mid - s)
            mids.append(mid)
        return mids, mix(coup, scale, mass, us, mids, g1[3, p])

    x1 = {}
    fields1 = [g1, e1, e2, e1]
    for k, (lo, hi) in enumerate([(0, 8), (1, 7), (1, 7), (2, 6)]):
        d = fields1[k]
        over = 1.0 / theta1 if k == 0 else 1.0
        scale, mass = over / (4.0 * 26.0), over * MASS
        for p in range(lo, hi):
            mids, a = plane1(p, d, scale, mass)
            for c in range(3):
                new = (g1 if k == 0 else r1)[c, p] - a[c]
                if k < 3:
                    ca, cb = steps1[k]
                    r1[c, p] = new
                    fields1[k + 1][c, p] = (ca * over) * mids[c] + cb * new
                else:
                    t1[pl.ds(32 * c + 8 * (p - 2), 8), :] = new[0:8]
                if 2 <= p < 6:
                    part = (mids[c] * over)[0:8]
                    x1[c, p] = part if k == 0 else x1[c, p] + part

    ys = [t1[pl.ds(y, 16, stride=8), :] for y in range(8)]
    ys = jnp.concatenate([ys[2 * j] + ys[2 * j + 1] for j in range(4)], axis=1)
    blk = mm(ys, m12[...])
    for c in range(4):
        g2[c, 4:8, 128:256] = blk[4 * c : 4 * c + 4]
    start(copies2, NEIGHBOURS)
    sent(copies1, NEIGHBOURS)

    rows = jnp.concatenate([x1[c, p] for c in range(3) for p in range(2, 6)], axis=0)
    rep = mm(rows, p1[...])
    u_lo[pl.ds(0, 96, stride=2), :] = rep[:, 0:128]
    u_lo[pl.ds(1, 96, stride=2), :] = rep[:, 0:128]
    u_hi[pl.ds(0, 96, stride=2), :] = rep[:, 128:256]
    u_hi[pl.ds(1, 96, stride=2), :] = rep[:, 128:256]
    for c in range(3):
        for p in range(4):
            rows_cp = pl.ds(16 * (4 * c + p), 16)
            for j in range(4):
                acc[c][4 * p + j] += (u_lo if j < 2 else u_hi)[rows_cp, :]

    arrive(copies2, NEIGHBOURS)

    f2 = [[g2[c, :, 128 * j : 128 * j + 128] for j in range(3)] for c in range(4)]
    x2, r2 = flat_smooth(f2[:3], f2[3], coup, 2, 32, True)

    t2[...] = mm(
        jnp.concatenate([r2[0][1], r2[1][1], r2[2][1], f2[3][1]], axis=1), m23[...]
    )
    h3[10:12, :] = t2[pl.ds(4, 2, stride=2), :] + t2[pl.ds(5, 2, stride=2), :]
    start(copies3, along_wide)
    sent(copies2, NEIGHBOURS)

    for c in range(3):
        t3[4 * c : 4 * c + 4, 0:128] = x2[c][1][4:8]
    rep = mm(t3[0:16, 0:128], p2[...])
    for y in range(16):
        j = y // 4
        v2[pl.ds(y, 16, stride=16), :] = rep[:, 128 * j : 128 * j + 128]
    for c in range(3):
        for k in range(4):
            part = v2[pl.ds(16 * (4 * c + k), 16), :]
            for j in range(4):
                acc[c][4 * k + j] += part

    arrive(copies3, along_wide)
    start(copies4, along_narrow)
    sent(copies3, along_wide)
    arrive(copies4, along_narrow)
    sent(copies4, along_narrow)

    lane3 = iota((24, 128), 1)
    slots = [h3s[j] if j != 5 else h3[...] for j in range(11)]
    f3 = [[None] * 3 for _ in range(4)]
    for c in range(4):
        for v in range(3):
            out = jnp.zeros((24, 128), F32)
            for q in range(4):
                j = 4 * v + q
                if j < 11:
                    turn = 32 * ((q - c) % 4)
                    part = pltpu.roll(slots[j], turn, 1) if turn else slots[j]
                    out = jnp.where((lane3 >> 5) == q, part, out)
            f3[c][v] = out
    x3, r3 = flat_smooth(f3[:3], f3[3], coup, 3, 16, True)

    z4[...] = mm(
        jnp.concatenate(
            [jnp.concatenate(r3[c] if c < 3 else f3[3], axis=1) for c in range(4)],
            axis=0,
        ),
        m34[...],
    )
    f4 = []
    for c in range(4):
        even, odd = (z4[pl.ds(24 * c + 4 + u, 8, stride=2), :] for u in range(2))
        f4.append([even + odd])
    x4, _ = flat_smooth(f4[:3], f4[3], coup, 4, 8, False)

    for c in range(3):
        t3[2 * c : 2 * c + 2, 0:128] = x3[c][1][10:12]
        t3[2 * c : 2 * c + 2, 128:256] = jnp.broadcast_to(x4[c][0][3:4], (2, 128))
    tail_out[...] = mm(t3[0:16, 0:256], p34[...])[0:8]


def solution(mesh):
    nw, nn = mesh.shape["wide"], mesh.shape["narrow"]

    def vm(*shape):
        return pltpu.VMEM(shape, F32)

    def mat(*shape):
        return pltpu.VMEM(shape, BF16)

    dma = pltpu.SemaphoreType.DMA
    scratch = [
        vm(2, 3, 24, 24, 128),
        vm(2, 24, 24, 128),
        vm(3, 24, 24, 128),
        vm(3, 24, 24, 128),
        vm(3, 24, 24, 128),
        vm(3, 24, 24, 128),
        vm(512, 128),
        vm(2, 4, 8, 16, 128),
        vm(3, 8, 16, 128),
        vm(3, 8, 16, 128),
        vm(3, 8, 16, 128),
        vm(128, 128),
        vm(192, 128),
        vm(192, 128),
        vm(2, 4, 16, 384),
        vm(16, 128),
        vm(256, 128),
        vm(2, 24, 128),
        vm(2, 11, 24, 128),
        vm(16, 256),
        vm(96, 128),
        mat(256, 128),
        mat(512, 128),
        mat(512, 128),
        mat(384, 128),
        mat(128, 256),
        mat(128, 512),
        mat(256, 256),
        pltpu.SMEM((3, 3), F32),
        dma((3,)),
        dma((16,)),
        dma((16,)),
        dma((16,)),
        dma((16,)),
        dma((8,)),
        dma((8,)),
        dma((10,)),
        dma((10,)),
        dma((10,)),
        dma((10,)),
    ]

    def per_device(residual, stiffness, coupling):
        hbm = pl.BlockSpec(memory_space=pltpu.HBM)
        vmem = pl.BlockSpec(memory_space=pltpu.VMEM)
        *acc, tail = pl.pallas_call(
            functools.partial(kernel, nw, nn),
            out_shape=(
                *[jax.ShapeDtypeStruct((16, 16, 128), F32)] * 3,
                jax.ShapeDtypeStruct((8, 256), F32),
            ),
            in_specs=[hbm, hbm, hbm],
            out_specs=(vmem,) * 4,
            scratch_shapes=scratch,
            compiler_params=pltpu.CompilerParams(
                collective_id=0,
                has_side_effects=True,
                vmem_limit_bytes=(53 * 1024 + 450) * 1024,
            ),
        )(residual, stiffness, coupling)
        tail = tail[0:6].reshape(3, 2, 1, 2, 1, 128)
        return (jnp.stack(acc).reshape(3, 2, 8, 2, 8, 128) + tail).reshape(3, 16, 16, 128)

    return jax.shard_map(
        per_device,
        mesh=mesh,
        in_specs=(P(None, "wide", "narrow", None), P("wide", "narrow", None), P()),
        out_specs=P(None, "wide", "narrow", None),
        check_vma=False,
    )
```

```python
import functools

import jax
import jax.numpy as jnp
from jax import lax
from jax.experimental import pallas as pl
from jax.experimental.pallas import tpu as pltpu
from jax.sharding import PartitionSpec as P

LEVELS = 4
MASS = 0.001
RATIO = 8.0
MESH = pl.DeviceIdType.MESH
NEIGHBOURS = [(1, 1), (1, -1), (-1, 1), (-1, -1), (1, 0), (-1, 0), (0, 1), (0, -1)]
AXIAL = NEIGHBOURS[4:]
WINDOW = [o for k in range(5, 0, -1) for o in (k, -k)]
F32 = jnp.float32
BF16 = jnp.bfloat16


def chebyshev(level):
    top = 4.0 * (2.8 / 4.0**level + MASS)
    theta = (top + top / RATIO) / 2.0
    delta = (top - top / RATIO) / 2.0
    sigma = theta / delta
    rho = 1.0 / sigma
    steps = []
    for _ in range(3):
        nxt = 1.0 / (2.0 * sigma - rho)
        steps.append((nxt * rho, 2.0 * nxt / delta))
        rho = nxt
    return theta, steps


def iota(shape, dim):
    return lax.broadcasted_iota(jnp.int32, shape, dim)


def indicator(cond, value=1.0):
    return jnp.where(cond, value, 0.0).astype(BF16)


def mm(v, w):
    hi = v.astype(BF16)
    lo = (v - hi.astype(F32)).astype(BF16)
    return jnp.dot(hi, w, preferred_element_type=F32) + jnp.dot(
        lo, w, preferred_element_type=F32
    )


def mix(coup, scale, mass, u, d, k):
    out = []
    for c in range(3):
        a = (coup[c][0] * scale) * u[0]
        a = a + (coup[c][1] * scale) * u[1]
        a = a + (coup[c][2] * scale) * u[2]
        a = a + mass * d[c]
        out.append(k * a)
    return out


def flat_box(chunks, nz):
    rows = chunks[0].shape[0]
    lane = iota(chunks[0].shape, 1)
    zpos = lane & (nz - 1)
    s = []
    for v in chunks:
        v = v + pltpu.roll(v, 1, 0) + pltpu.roll(v, rows - 1, 0)
        s.append(
            v
            + jnp.where(zpos == 0, 0.0, pltpu.roll(v, 1, 1))
            + jnp.where(zpos == nz - 1, 0.0, pltpu.roll(v, 127, 1))
        )
    up = [pltpu.roll(v, nz, 1) for v in s]
    down = [pltpu.roll(v, 128 - nz, 1) for v in s]
    out = []
    for j, v in enumerate(s):
        before = up[j - 1] if j > 0 else 0.0
        after = down[j + 1] if j + 1 < len(s) else 0.0
        out.append(
            v
            + jnp.where(lane < nz, before, up[j])
            + jnp.where(lane >= 128 - nz, after, down[j])
        )
    return out


def flat_box_wide(chunks, nz):
    rows = chunks[0].shape[0]
    lane = iota(chunks[0].shape, 1)
    zpos = lane & (nz - 1)

    def shifted(v, y):
        mid = pltpu.roll(v, y % 128, 1) if y else v
        return (
            mid
            + jnp.where(zpos == 0, 0.0, pltpu.roll(v, (y + 1) % 128, 1))
            + jnp.where(zpos == nz - 1, 0.0, pltpu.roll(v, (y - 1) % 128, 1))
        )

    xs = [v + pltpu.roll(v, 1, 0) + pltpu.roll(v, rows - 1, 0) for v in chunks]
    up = [shifted(v, nz) for v in xs]
    down = [shifted(v, -nz) for v in xs]
    out = []
    for j, v in enumerate(xs):
        before = up[j - 1] if j > 0 else 0.0
        after = down[j + 1] if j + 1 < len(xs) else 0.0
        out.append(
            shifted(v, 0)
            + jnp.where(lane < nz, before, up[j])
            + jnp.where(lane >= 128 - nz, after, down[j])
        )
    return out


def flat_smooth(f, kappa, coup, level, nz, want_rest):
    theta, steps = chebyshev(level)
    scale = 4.0**-level / 26.0
    n = len(kappa)

    def apply(r, d):
        box = flat_box if n > 1 else flat_box_wide
        boxes = [box(d[c], nz) for c in range(3)]
        new = [[None] * n for _ in range(3)]
        for j in range(n):
            u = [27.0 * d[c][j] - boxes[c][j] for c in range(3)]
            a = mix(coup, scale, MASS, u, [d[c][j] for c in range(3)], kappa[j])
            for c in range(3):
                new[c][j] = r[c][j] - a[c]
        return new

    r = f
    d = [[v * (1.0 / theta) for v in f[c]] for c in range(3)]
    x = d
    for a, b in steps:
        r = apply(r, d)
        d = [[a * d[c][j] + b * r[c][j] for j in range(n)] for c in range(3)]
        x = [[x[c][j] + d[c][j] for j in range(n)] for c in range(3)]
    if want_rest:
        r = apply(r, d)
    return x, r


def kernel(
    nw,
    nn,
    res,
    stiff,
    coup_hbm,
    acc0,
    acc1,
    acc2,
    tail_out,
    f0b,
    k0b,
    r0,
    d1,
    d2,
    d3,
    t0,
    g1b,
    r1,
    e1,
    e2,
    t1,
    u_lo,
    u_hi,
    g2b,
    t2,
    v2,
    h3b,
    h3sb,
    t3,
    z4,
    m01,
    m12,
    m23,
    m34,
    p1,
    p2,
    p34,
    coup_ref,
    local_sem,
    ready_sem,
    s0,
    q0,
    s1,
    q1,
    s2,
    q2,
    s3,
    q3,
    s4,
    q4,
):
    w = lax.axis_index("wide")
    n = lax.axis_index("narrow")
    acc = [acc0, acc1, acc2]
    f0, k0, g1, g2, h3, h3s = (b.at[0] for b in (f0b, k0b, g1b, g2b, h3b, h3sb))

    def pair_of(i):
        return i + 1 - 2 * lax.rem(i, 2)

    def out_of(pos, off, size):
        if off == 0:
            return jnp.bool_(False)
        return pos + off >= size if off > 0 else pos + off < 0

    targets = {}

    def target(ow, on):
        if (ow, on) in targets:
            return targets[ow, on]
        w_out, n_out = out_of(w, ow, nw), out_of(n, on, nn)
        if on == 0:
            tw = jnp.where(w_out, w, w + ow)
            tn = jnp.where(w_out, pair_of(n), n)
            away = w_out
        elif ow == 0:
            tw = jnp.where(n_out, pair_of(w), w)
            tn = jnp.where(n_out, n, n + on)
            away = n_out
        else:
            w_end, n_end = (nw - 1 if ow > 0 else 0), (nn - 1 if on > 0 else 0)
            both = jnp.logical_and(w_out, n_out)
            away = jnp.logical_or(w_out, n_out)
            w_near, n_near = w == w_end - ow, n == n_end - on
            tw = jnp.where(
                both,
                w - ow,
                jnp.where(
                    w_out,
                    w,
                    jnp.where(n_out, jnp.where(w_near, w + ow, pair_of(w)), w + ow),
                ),
            )
            tn = jnp.where(
                both,
                n,
                jnp.where(
                    w_out,
                    jnp.where(n_near, n + on, pair_of(n)),
                    jnp.where(n_out, jnp.where(w_near, n - on, n), n + on),
                ),
            )
        targets[ow, on] = tw, tn, jnp.where(away, 1, 0)
        return targets[ow, on]

    def remote(src, dst, where, send, recv, sems, ow, on):
        tw, tn, away = target(ow, on)
        mine, other = sems
        return pltpu.make_async_remote_copy(
            src_ref=src,
            dst_ref=dst.at[(away,) + where],
            send_sem=send.at[mine],
            recv_sem=recv.at[mine + (other - mine) * away],
            device_id={"wide": tw, "narrow": tn},
            device_id_type=MESH,
        )

    def landed(buf, where, send, recv, mine):
        return pltpu.make_async_remote_copy(
            src_ref=buf.at[(0,) + where],
            dst_ref=buf.at[(0,) + where],
            send_sem=send.at[mine],
            recv_sem=recv.at[mine],
            device_id={"wide": w, "narrow": n},
            device_id_type=MESH,
        )

    own_f = pltpu.make_async_copy(res, f0.at[:, 4:20, 0:16, :], local_sem.at[0])
    own_k = pltpu.make_async_copy(stiff, k0.at[4:20, 0:16, :], local_sem.at[1])
    own_c = pltpu.make_async_copy(coup_hbm, coup_ref, local_sem.at[2])
    own_f.start()
    own_k.start()
    own_c.start()

    h3[...] = jnp.zeros_like(h3)
    h3s[...] = jnp.zeros_like(h3s)

    def tell(sem, offsets):
        for ow, on in offsets:
            tw, tn, _ = target(ow, on)
            pl.semaphore_signal(
                sem,
                inc=1,
                device_id={"wide": tw, "narrow": tn},
                device_id_type=MESH,
            )

    barrier = pltpu.get_barrier_semaphore()
    tell(barrier, AXIAL)
    g1[...] = jnp.zeros_like(g1)
    g2[...] = jnp.zeros_like(g2)
    pl.semaphore_wait(barrier, len(AXIAL))

    def copies0(i, ow, on):
        sx, dx = {0: (0, 4), 1: (12, 0), -1: (0, 20)}[ow]
        sy, dy = {0: (0, 0), 1: (12, 20), -1: (0, 16)}[on]
        nx, ny = (16 if ow == 0 else 4), (16 if on == 0 else 4)
        fs = (slice(None), slice(sx, sx + nx), slice(sy, sy + ny))
        fd = (slice(None), slice(dx, dx + nx), slice(dy, dy + ny))
        if ow > 0:
            sx, dx = sx + 1, dx + 1
        if on > 0:
            sy, dy = sy + 1, dy + 1
        nx, ny = (16 if ow == 0 else 3), (16 if on == 0 else 3)
        ks = (slice(sx, sx + nx), slice(sy, sy + ny))
        kd = (slice(dx, dx + nx), slice(dy, dy + ny))
        return [
            (res.at[fs], f0b, fd, s0, q0, i),
            (stiff.at[ks], k0b, kd, s0, q0, 8 + i),
        ]

    def copies1(i, ow, on):
        sx, dx = {0: ((2, 6), (2, 6)), 1: ((4, 6), (0, 2)), -1: ((2, 4), (6, 8))}[ow]
        sy, dy = {0: ((0, 8), (0, 8)), 1: ((4, 8), (12, 16)), -1: ((0, 4), (8, 12))}[on]
        sx, dx, sy, dy = slice(*sx), slice(*dx), slice(*sy), slice(*dy)
        return [
            (g1.at[0:3, sx, sy], g1b, (slice(0, 3), dx, dy), s1, q1, i),
            (g1.at[3, sx, sy], g1b, (3, dx, dy), s1, q1, 8 + i),
        ]

    def copies2(i, ow, on):
        dx = slice(4 - 4 * ow, 8 - 4 * ow)
        dy = slice(128 - 128 * on, 256 - 128 * on)
        return [(g2.at[:, 4:8, 128:256], g2b, (slice(None), dx, dy), s2, q2, i)]

    def copies3(i, ow, on):
        rows = slice(10 - 2 * ow, 12 - 2 * ow)
        return [(h3.at[10:12, :], h3b, (rows,), s3, q3, i)]

    def copies4(i, ow, on):
        rows = slice(0, 22)
        return [(h3.at[rows], h3sb, (5 - on, rows), s4, q4, i)]

    def start(copies, offsets, chosen=None, part=slice(None)):
        for i, (ow, on) in enumerate(offsets):
            if chosen is None or i in chosen:
                opposite = offsets.index((-ow, -on))
                for src, dst, where, send, recv, mine in copies(i, ow, on)[part]:
                    sems = mine, mine + opposite - i
                    remote(src, dst, where, send, recv, sems, ow, on).start()

    def arrive(copies, offsets, chosen=None):
        for i, (ow, on) in enumerate(offsets):
            if chosen is None or i in chosen:
                for src, dst, where, send, recv, mine in copies(i, ow, on):
                    landed(dst, where, send, recv, mine).wait_recv()

    def sent(copies, offsets):
        for i, (ow, on) in enumerate(offsets):
            for src, dst, where, send, recv, mine in copies(i, ow, on):
                landed(dst, where, send, recv, mine).wait_send()

    along_wide = [(o, 0) for o in WINDOW]
    along_narrow = [(0, o) for o in WINDOW]

    start(copies0, NEIGHBOURS, (4, 5), slice(0, 1))
    start(copies0, NEIGHBOURS, (6, 7))
    tell(ready_sem, AXIAL)
    pl.semaphore_wait(ready_sem, len(AXIAL))
    start(copies0, NEIGHBOURS, (0, 1, 2, 3))
    start(copies0, NEIGHBOURS, (4, 5), slice(1, 2))

    @pl.when(w == 0)
    def _():
        f0[:, 0:4] = jnp.zeros((3, 4, 24, 128), F32)
        k0[0:4] = jnp.zeros((4, 24, 128), F32)

    @pl.when(w == nw - 1)
    def _():
        f0[:, 20:24] = jnp.zeros((3, 4, 24, 128), F32)
        k0[20:24] = jnp.zeros((4, 24, 128), F32)

    @pl.when(n == 0)
    def _():
        f0[:, :, 20:24, :] = jnp.zeros((3, 24, 4, 128), F32)
        k0[:, 20:24, :] = jnp.zeros((24, 4, 128), F32)

    @pl.when(n == nn - 1)
    def _():
        f0[:, :, 16:20, :] = jnp.zeros((3, 24, 4, 128), F32)
        k0[:, 16:20, :] = jnp.zeros((24, 4, 128), F32)

    r, c = iota((256, 128), 0), iota((256, 128), 1)
    m01[...] = indicator(((r >> 7) == (c >> 6)) & (((r & 127) >> 1) == (c & 63)), 0.125)
    r, c = iota((512, 128), 0), iota((512, 128), 1)
    m12[...] = indicator(((r >> 7) == (c >> 5)) & (((r & 63) >> 1) == (c & 31)), 0.125)
    m23[...] = indicator(
        ((r >> 7) == (c >> 5))
        & (((r >> 6) & 1) == ((c >> 4) & 1))
        & (((r & 31) >> 1) == (c & 15)),
        0.125,
    )
    r, c = iota((384, 128), 0), iota((384, 128), 1)
    m34[...] = indicator(((r >> 5) == (c >> 3)) & (((r & 15) >> 1) == (c & 7)), 0.125)
    r, c = iota((128, 256), 0), iota((128, 256), 1)
    p1[...] = indicator(((r >> 6) == (c >> 7)) & ((r & 63) == ((c & 127) >> 1)))
    r, c = iota((128, 512), 0), iota((128, 512), 1)
    p2[...] = indicator(((r >> 5) == (c >> 7)) & ((r & 31) == ((c & 127) >> 2)))
    r, c = iota((256, 256), 0), iota((256, 256), 1)
    fine = ((r >> 4) == (2 + (c >> 7))) & ((r & 15) == ((c & 127) >> 3))
    coarse = (r >= 128 + 40) & (r < 128 + 48) & ((r & 7) == ((c & 127) >> 4))
    p34[...] = indicator(fine | coarse)

    own_c.wait()
    coup = [[coup_ref[i, j] for j in range(3)] for i in range(3)]

    own_k.wait()
    for i in range(8):
        t0[pl.ds(384 + 16 * i, 16), :] = (
            k0[4 + 2 * i, 0:16, :] + k0[5 + 2 * i, 0:16, :]
        )

    def halved(first, count):
        s = t0[pl.ds(first, count, stride=2), :] + t0[pl.ds(first + 1, count, stride=2), :]
        s = s.reshape(count // 16, 2, 8, 128)
        pair = [s[:, u].reshape(count // 2, 128) for u in range(2)]
        return mm(jnp.concatenate(pair, axis=1), m01[...])

    g1[3, 2:6, 0:8, :] = halved(384, 64).reshape(4, 8, 128)
    for p in range(4):
        t1[pl.ds(96 + 8 * p, 8), :] = g1[3, 2 + p, 0:8, :]

    theta0, steps0 = chebyshev(0)
    lane24 = iota((24, 128), 1)
    lane16 = iota((16, 128), 1)
    fields = [f0, d1, d2, d3]

    def sweep0(k, starts, count):
        d = fields[k]
        over = 1.0 / theta0 if k == 0 else 1.0
        scale, mass = over / 26.0, over * MASS
        rest = f0 if k == 0 else r0
        rows, lane = (24, lane24) if k < 3 else (16, lane16)
        for lo in starts:
            for i in range(lo, lo + count, 2):
                mids, boxes = [[], []], [[], []]
                for c in range(3):
                    a, b = d[c, i], d[c, i + 1]
                    both = a + b
                    for u, (mid, x) in enumerate(((a, d[c, i - 1]), (b, d[c, i + 2]))):
                        s = both + x
                        s = s + pltpu.roll(s, 1, 0) + pltpu.roll(s, 23, 0)
                        s = s[0:rows]
                        s = (
                            s
                            + jnp.where(lane == 0, 0.0, pltpu.roll(s, 1, 1))
                            + jnp.where(lane == 127, 0.0, pltpu.roll(s, 127, 1))
                        )
                        mids[u].append(mid[0:rows])
                        boxes[u].append(s)
                new = []
                for u in range(2):
                    us = [27.0 * mids[u][c] - boxes[u][c] for c in range(3)]
                    a = mix(coup, scale, mass, us, mids[u], k0[i + u, 0:rows])
                    new.append([rest[c, i + u, 0:rows] - a[c] for c in range(3)])
                    if k < 3:
                        ca, cb = steps0[k]
                        for c in range(3):
                            r0[c, i + u] = new[u][c]
                            fields[k + 1][c, i + u] = (ca * over) * mids[u][c] + cb * new[u][c]
                if k == 3:
                    for c in range(3):
                        t0[pl.ds(128 * c + 8 * (i - 4), 16), :] = new[0][c] + new[1][c]

    own_f.wait()
    arrive(copies0, NEIGHBOURS, (6, 7))
    for k in range(4):
        sweep0(k, (5 + k,), 14 - 2 * k)
    arrive(copies0, NEIGHBOURS, (0, 1, 2, 3, 4, 5))
    start(copies1, NEIGHBOURS, None, slice(1, 2))
    for k in range(4):
        sweep0(k, (1 + k, 19 - k), 4)
    g1[0:3, 2:6, 0:8, :] = halved(0, 192).reshape(3, 4, 8, 128)
    start(copies1, NEIGHBOURS, None, slice(0, 1))
    sent(copies0, NEIGHBOURS)

    def sum0(i, carry):
        for c in range(3):
            acc[c][i] = (
                f0[c, 4 + i, 0:16, :] * (1.0 / theta0)
                + d1[c, 4 + i, 0:16, :]
                + d2[c, 4 + i, 0:16, :]
                + d3[c, 4 + i, 0:16, :]
            )
        return carry

    lax.fori_loop(0, 16, sum0, 0)

    arrive(copies1, NEIGHBOURS)

    theta1, steps1 = chebyshev(1)
    lower = lane16 < 64
    zpos1 = lane16 & 63

    def plane1(p, d, scale, mass):
        us, mids = [], []
        for c in range(3):
            mid = d[c, p]
            swap = mid + jnp.where(lower, d[c, min(p + 1, 7)], d[c, max(p - 1, 0)])
            up = pltpu.roll(mid, 1, 1) + pltpu.roll(swap, 65, 1)
            down = pltpu.roll(mid, 127, 1) + pltpu.roll(swap, 63, 1)
            s = mid + pltpu.roll(swap, 64, 1)
            s = s + jnp.where(zpos1 == 0, 0.0, up) + jnp.where(zpos1 == 63, 0.0, down)
            s = s + pltpu.roll(s, 1, 0) + pltpu.roll(s, 15, 0)
            us.append(27.0 * mid - s)
            mids.append(mid)
        return mids, mix(coup, scale, mass, us, mids, g1[3, p])

    x1 = {}
    fields1 = [g1, e1, e2, e1]
    for k, (lo, hi) in enumerate([(0, 8), (1, 7), (1, 7), (2, 6)]):
        d = fields1[k]
        over = 1.0 / theta1 if k == 0 else 1.0
        scale, mass = over / (4.0 * 26.0), over * MASS
        for p in range(lo, hi):
            mids, a = plane1(p, d, scale, mass)
            for c in range(3):
                new = (g1 if k == 0 else r1)[c, p] - a[c]
                if k < 3:
                    ca, cb = steps1[k]
                    r1[c, p] = new
                    fields1[k + 1][c, p] = (ca * over) * mids[c] + cb * new
                else:
                    t1[pl.ds(32 * c + 8 * (p - 2), 8), :] = new[0:8]
                if 2 <= p < 6:
                    part = (mids[c] * over)[0:8]
                    x1[c, p] = part if k == 0 else x1[c, p] + part

    ys = [t1[pl.ds(y, 16, stride=8), :] for y in range(8)]
    ys = jnp.concatenate([ys[2 * j] + ys[2 * j + 1] for j in range(4)], axis=1)
    blk = mm(ys, m12[...])
    for c in range(4):
        g2[c, 4:8, 128:256] = blk[4 * c : 4 * c + 4]
    start(copies2, NEIGHBOURS)
    sent(copies1, NEIGHBOURS)

    rows = jnp.concatenate([x1[c, p] for c in range(3) for p in range(2, 6)], axis=0)
    rep = mm(rows, p1[...])
    u_lo[pl.ds(0, 96, stride=2), :] = rep[:, 0:128]
    u_lo[pl.ds(1, 96, stride=2), :] = rep[:, 0:128]
    u_hi[pl.ds(0, 96, stride=2), :] = rep[:, 128:256]
    u_hi[pl.ds(1, 96, stride=2), :] = rep[:, 128:256]
    for c in range(3):
        for p in range(4):
            rows_cp = pl.ds(16 * (4 * c + p), 16)
            for j in range(4):
                acc[c][4 * p + j] += (u_lo if j < 2 else u_hi)[rows_cp, :]

    arrive(copies2, NEIGHBOURS)

    f2 = [[g2[c, :, 128 * j : 128 * j + 128] for j in range(3)] for c in range(4)]
    x2, r2 = flat_smooth(f2[:3], f2[3], coup, 2, 32, True)

    t2[...] = mm(
        jnp.concatenate([r2[0][1], r2[1][1], r2[2][1], f2[3][1]], axis=1), m23[...]
    )
    h3[10:12, :] = t2[pl.ds(4, 2, stride=2), :] + t2[pl.ds(5, 2, stride=2), :]
    start(copies3, along_wide)
    sent(copies2, NEIGHBOURS)

    for c in range(3):
        t3[4 * c : 4 * c + 4, 0:128] = x2[c][1][4:8]
    rep = mm(t3[0:16, 0:128], p2[...])
    for y in range(16):
        j = y // 4
        v2[pl.ds(y, 16, stride=16), :] = rep[:, 128 * j : 128 * j + 128]
    for c in range(3):
        for k in range(4):
            part = v2[pl.ds(16 * (4 * c + k), 16), :]
            for j in range(4):
                acc[c][4 * k + j] += part

    arrive(copies3, along_wide)
    start(copies4, along_narrow)
    sent(copies3, along_wide)
    arrive(copies4, along_narrow)
    sent(copies4, along_narrow)

    lane3 = iota((24, 128), 1)
    slots = [h3s[j] if j != 5 else h3[...] for j in range(11)]
    f3 = [[None] * 3 for _ in range(4)]
    for c in range(4):
        for v in range(3):
            out = jnp.zeros((24, 128), F32)
            for q in range(4):
                j = 4 * v + q
                if j < 11:
                    turn = 32 * ((q - c) % 4)
                    part = pltpu.roll(slots[j], turn, 1) if turn else slots[j]
                    out = jnp.where((lane3 >> 5) == q, part, out)
            f3[c][v] = out
    x3, r3 = flat_smooth(f3[:3], f3[3], coup, 3, 16, True)

    z4[...] = mm(
        jnp.concatenate(
            [jnp.concatenate(r3[c] if c < 3 else f3[3], axis=1) for c in range(4)],
            axis=0,
        ),
        m34[...],
    )
    f4 = []
    for c in range(4):
        even, odd = (z4[pl.ds(24 * c + 4 + u, 8, stride=2), :] for u in range(2))
        f4.append([even + odd])
    x4, _ = flat_smooth(f4[:3], f4[3], coup, 4, 8, False)

    for c in range(3):
        t3[2 * c : 2 * c + 2, 0:128] = x3[c][1][10:12]
        t3[2 * c : 2 * c + 2, 128:256] = jnp.broadcast_to(x4[c][0][3:4], (2, 128))
    tail_out[...] = mm(t3[0:16, 0:256], p34[...])[0:8]


def solution(mesh):
    nw, nn = mesh.shape["wide"], mesh.shape["narrow"]

    def vm(*shape):
        return pltpu.VMEM(shape, F32)

    def mat(*shape):
        return pltpu.VMEM(shape, BF16)

    dma = pltpu.SemaphoreType.DMA
    scratch = [
        vm(2, 3, 24, 24, 128),
        vm(2, 24, 24, 128),
        vm(3, 24, 24, 128),
        vm(3, 24, 24, 128),
        vm(3, 24, 24, 128),
        vm(3, 24, 24, 128),
        vm(512, 128),
        vm(2, 4, 8, 16, 128),
        vm(3, 8, 16, 128),
        vm(3, 8, 16, 128),
        vm(3, 8, 16, 128),
        vm(128, 128),
        vm(192, 128),
        vm(192, 128),
        vm(2, 4, 16, 384),
        vm(16, 128),
        vm(256, 128),
        vm(2, 24, 128),
        vm(2, 11, 24, 128),
        vm(16, 256),
        vm(96, 128),
        mat(256, 128),
        mat(512, 128),
        mat(512, 128),
        mat(384, 128),
        mat(128, 256),
        mat(128, 512),
        mat(256, 256),
        pltpu.SMEM((3, 3), F32),
        dma((3,)),
        pltpu.SemaphoreType.REGULAR,
        dma((16,)),
        dma((16,)),
        dma((16,)),
        dma((16,)),
        dma((8,)),
        dma((8,)),
        dma((10,)),
        dma((10,)),
        dma((10,)),
        dma((10,)),
    ]

    def per_device(residual, stiffness, coupling):
        hbm = pl.BlockSpec(memory_space=pltpu.HBM)
        vmem = pl.BlockSpec(memory_space=pltpu.VMEM)
        *acc, tail = pl.pallas_call(
            functools.partial(kernel, nw, nn),
            out_shape=(
                *[jax.ShapeDtypeStruct((16, 16, 128), F32)] * 3,
                jax.ShapeDtypeStruct((8, 256), F32),
            ),
            in_specs=[hbm, hbm, hbm],
            out_specs=(vmem,) * 4,
            scratch_shapes=scratch,
            compiler_params=pltpu.CompilerParams(
                collective_id=0,
                has_side_effects=True,
                vmem_limit_bytes=(53 * 1024 + 450) * 1024,
            ),
        )(residual, stiffness, coupling)
        tail = tail[0:6].reshape(3, 2, 1, 2, 1, 128)
        return (jnp.stack(acc).reshape(3, 2, 8, 2, 8, 128) + tail).reshape(3, 16, 16, 128)

    return jax.shard_map(
        per_device,
        mesh=mesh,
        in_specs=(P(None, "wide", "narrow", None), P("wide", "narrow", None), P()),
        out_specs=P(None, "wide", "narrow", None),
        check_vma=False,
    )
```

```python
import functools

import jax
import jax.numpy as jnp
from jax import lax
from jax.experimental import pallas as pl
from jax.experimental.pallas import tpu as pltpu
from jax.sharding import PartitionSpec as P

LEVELS = 4
MASS = 0.001
RATIO = 8.0
MESH = pl.DeviceIdType.MESH
NEIGHBOURS = [(1, 1), (1, -1), (-1, 1), (-1, -1), (1, 0), (-1, 0), (0, 1), (0, -1)]
AXIAL = NEIGHBOURS[4:]
WINDOW = [o for k in range(5, 0, -1) for o in (k, -k)]
F32 = jnp.float32
BF16 = jnp.bfloat16


def chebyshev(level):
    top = 4.0 * (2.8 / 4.0**level + MASS)
    theta = (top + top / RATIO) / 2.0
    delta = (top - top / RATIO) / 2.0
    sigma = theta / delta
    rho = 1.0 / sigma
    steps = []
    for _ in range(3):
        nxt = 1.0 / (2.0 * sigma - rho)
        steps.append((nxt * rho, 2.0 * nxt / delta))
        rho = nxt
    return theta, steps


def iota(shape, dim):
    return lax.broadcasted_iota(jnp.int32, shape, dim)


def indicator(cond, value=1.0):
    return jnp.where(cond, value, 0.0).astype(BF16)


def mm(v, w):
    hi = v.astype(BF16)
    lo = (v - hi.astype(F32)).astype(BF16)
    return jnp.dot(hi, w, preferred_element_type=F32) + jnp.dot(
        lo, w, preferred_element_type=F32
    )


def mix(coup, scale, mass, u, d, k):
    out = []
    for c in range(3):
        a = (coup[c][0] * scale) * u[0]
        a = a + (coup[c][1] * scale) * u[1]
        a = a + (coup[c][2] * scale) * u[2]
        a = a + mass * d[c]
        out.append(k * a)
    return out


def flat_box(chunks, nz):
    rows = chunks[0].shape[0]
    lane = iota(chunks[0].shape, 1)
    zpos = lane & (nz - 1)
    s = []
    for v in chunks:
        v = v + pltpu.roll(v, 1, 0) + pltpu.roll(v, rows - 1, 0)
        s.append(
            v
            + jnp.where(zpos == 0, 0.0, pltpu.roll(v, 1, 1))
            + jnp.where(zpos == nz - 1, 0.0, pltpu.roll(v, 127, 1))
        )
    up = [pltpu.roll(v, nz, 1) for v in s]
    down = [pltpu.roll(v, 128 - nz, 1) for v in s]
    out = []
    for j, v in enumerate(s):
        before = up[j - 1] if j > 0 else 0.0
        after = down[j + 1] if j + 1 < len(s) else 0.0
        out.append(
            v
            + jnp.where(lane < nz, before, up[j])
            + jnp.where(lane >= 128 - nz, after, down[j])
        )
    return out


def flat_box_wide(chunks, nz):
    rows = chunks[0].shape[0]
    lane = iota(chunks[0].shape, 1)
    zpos = lane & (nz - 1)

    def shifted(v, y):
        mid = pltpu.roll(v, y % 128, 1) if y else v
        return (
            mid
            + jnp.where(zpos == 0, 0.0, pltpu.roll(v, (y + 1) % 128, 1))
            + jnp.where(zpos == nz - 1, 0.0, pltpu.roll(v, (y - 1) % 128, 1))
        )

    xs = [v + pltpu.roll(v, 1, 0) + pltpu.roll(v, rows - 1, 0) for v in chunks]
    up = [shifted(v, nz) for v in xs]
    down = [shifted(v, -nz) for v in xs]
    out = []
    for j, v in enumerate(xs):
        before = up[j - 1] if j > 0 else 0.0
        after = down[j + 1] if j + 1 < len(xs) else 0.0
        out.append(
            shifted(v, 0)
            + jnp.where(lane < nz, before, up[j])
            + jnp.where(lane >= 128 - nz, after, down[j])
        )
    return out


def flat_smooth(f, kappa, coup, level, nz, want_rest):
    theta, steps = chebyshev(level)
    scale = 4.0**-level / 26.0
    n = len(kappa)

    def apply(r, d):
        box = flat_box if n > 1 else flat_box_wide
        boxes = [box(d[c], nz) for c in range(3)]
        new = [[None] * n for _ in range(3)]
        for j in range(n):
            u = [27.0 * d[c][j] - boxes[c][j] for c in range(3)]
            a = mix(coup, scale, MASS, u, [d[c][j] for c in range(3)], kappa[j])
            for c in range(3):
                new[c][j] = r[c][j] - a[c]
        return new

    r = f
    d = [[v * (1.0 / theta) for v in f[c]] for c in range(3)]
    x = d
    for a, b in steps:
        r = apply(r, d)
        d = [[a * d[c][j] + b * r[c][j] for j in range(n)] for c in range(3)]
        x = [[x[c][j] + d[c][j] for j in range(n)] for c in range(3)]
    if want_rest:
        r = apply(r, d)
    return x, r


def kernel(
    nw,
    nn,
    res,
    stiff,
    coup_hbm,
    acc0,
    acc1,
    acc2,
    tail_out,
    f0b,
    k0b,
    r0,
    d1,
    d2,
    d3,
    t0,
    g1b,
    r1,
    e1,
    e2,
    t1,
    u_lo,
    u_hi,
    g2b,
    t2,
    v2,
    h3b,
    h3sb,
    t3,
    z4,
    m01,
    m12,
    m23,
    m34,
    p1,
    p2,
    p34,
    coup_ref,
    local_sem,
    ready_sem,
    s0,
    q0,
    s1,
    q1,
    s2,
    q2,
    s3,
    q3,
    s4,
    q4,
):
    w = lax.axis_index("wide")
    n = lax.axis_index("narrow")
    acc = [acc0, acc1, acc2]
    f0, k0, g1, g2, h3, h3s = (b.at[0] for b in (f0b, k0b, g1b, g2b, h3b, h3sb))

    def pair_of(i):
        return i + 1 - 2 * lax.rem(i, 2)

    def out_of(pos, off, size):
        if off == 0:
            return jnp.bool_(False)
        return pos + off >= size if off > 0 else pos + off < 0

    targets = {}

    def target(ow, on):
        if (ow, on) in targets:
            return targets[ow, on]
        w_out, n_out = out_of(w, ow, nw), out_of(n, on, nn)
        if on == 0:
            tw = jnp.where(w_out, w, w + ow)
            tn = jnp.where(w_out, pair_of(n), n)
            away = w_out
        elif ow == 0:
            tw = jnp.where(n_out, pair_of(w), w)
            tn = jnp.where(n_out, n, n + on)
            away = n_out
        else:
            w_end, n_end = (nw - 1 if ow > 0 else 0), (nn - 1 if on > 0 else 0)
            both = jnp.logical_and(w_out, n_out)
            away = jnp.logical_or(w_out, n_out)
            w_near, n_near = w == w_end - ow, n == n_end - on
            tw = jnp.where(
                both,
                w - ow,
                jnp.where(
                    w_out,
                    w,
                    jnp.where(n_out, jnp.where(w_near, w + ow, pair_of(w)), w + ow),
                ),
            )
            tn = jnp.where(
                both,
                n,
                jnp.where(
                    w_out,
                    jnp.where(n_near, n + on, pair_of(n)),
                    jnp.where(n_out, jnp.where(w_near, n - on, n), n + on),
                ),
            )
        targets[ow, on] = tw, tn, jnp.where(away, 1, 0)
        return targets[ow, on]

    def remote(src, dst, where, send, recv, sems, ow, on):
        tw, tn, away = target(ow, on)
        mine, other = sems
        return pltpu.make_async_remote_copy(
            src_ref=src,
            dst_ref=dst.at[(away,) + where],
            send_sem=send.at[mine],
            recv_sem=recv.at[mine + (other - mine) * away],
            device_id={"wide": tw, "narrow": tn},
            device_id_type=MESH,
        )

    def landed(buf, where, send, recv, mine):
        return pltpu.make_async_remote_copy(
            src_ref=buf.at[(0,) + where],
            dst_ref=buf.at[(0,) + where],
            send_sem=send.at[mine],
            recv_sem=recv.at[mine],
            device_id={"wide": w, "narrow": n},
            device_id_type=MESH,
        )

    own_f = [
        pltpu.make_async_copy(res.at[c], f0.at[c, 4:20, 0:16, :], local_sem.at[2 + c])
        for c in range(3)
    ]
    own_k = pltpu.make_async_copy(stiff, k0.at[4:20, 0:16, :], local_sem.at[1])
    own_c = pltpu.make_async_copy(coup_hbm, coup_ref, local_sem.at[0])
    for c in own_f:
        c.start()

    h3[...] = jnp.zeros_like(h3)
    h3s[...] = jnp.zeros_like(h3s)

    def tell(sem, offsets):
        for ow, on in offsets:
            tw, tn, _ = target(ow, on)
            pl.semaphore_signal(
                sem,
                inc=1,
                device_id={"wide": tw, "narrow": tn},
                device_id_type=MESH,
            )

    barrier = pltpu.get_barrier_semaphore()
    tell(barrier, AXIAL)
    own_k.start()
    own_c.start()
    g1[...] = jnp.zeros_like(g1)
    g2[...] = jnp.zeros_like(g2)
    for c in own_f:
        c.wait()
    own_k.wait()
    pl.semaphore_wait(barrier, len(AXIAL))

    def copies0(i, ow, on):
        sx, dx = {0: (0, 4), 1: (12, 0), -1: (0, 20)}[ow]
        sy, dy = {0: (0, 0), 1: (12, 20), -1: (0, 16)}[on]
        nx, ny = (16 if ow == 0 else 4), (16 if on == 0 else 4)
        fs = (slice(None), slice(4 + sx, 4 + sx + nx), slice(sy, sy + ny))
        fd = (slice(None), slice(dx, dx + nx), slice(dy, dy + ny))
        if ow > 0:
            sx, dx = sx + 1, dx + 1
        if on > 0:
            sy, dy = sy + 1, dy + 1
        nx, ny = (16 if ow == 0 else 3), (16 if on == 0 else 3)
        ks = (slice(4 + sx, 4 + sx + nx), slice(sy, sy + ny))
        kd = (slice(dx, dx + nx), slice(dy, dy + ny))
        return [
            (f0.at[fs], f0b, fd, s0, q0, i),
            (k0.at[ks], k0b, kd, s0, q0, 8 + i),
        ]

    def copies1(i, ow, on):
        sx, dx = {0: ((2, 6), (2, 6)), 1: ((4, 6), (0, 2)), -1: ((2, 4), (6, 8))}[ow]
        sy, dy = {0: ((0, 8), (0, 8)), 1: ((4, 8), (12, 16)), -1: ((0, 4), (8, 12))}[on]
        sx, dx, sy, dy = slice(*sx), slice(*dx), slice(*sy), slice(*dy)
        return [
            (g1.at[0:3, sx, sy], g1b, (slice(0, 3), dx, dy), s1, q1, i),
            (g1.at[3, sx, sy], g1b, (3, dx, dy), s1, q1, 8 + i),
        ]

    def copies2(i, ow, on):
        dx = slice(4 - 4 * ow, 8 - 4 * ow)
        dy = slice(128 - 128 * on, 256 - 128 * on)
        return [(g2.at[:, 4:8, 128:256], g2b, (slice(None), dx, dy), s2, q2, i)]

    def copies3(i, ow, on):
        rows = slice(10 - 2 * ow, 12 - 2 * ow)
        return [(h3.at[10:12, :], h3b, (rows,), s3, q3, i)]

    def copies4(i, ow, on):
        rows = slice(0, 22)
        return [(h3.at[rows], h3sb, (5 - on, rows), s4, q4, i)]

    def start(copies, offsets, chosen=None, part=slice(None)):
        for i, (ow, on) in enumerate(offsets):
            if chosen is None or i in chosen:
                opposite = offsets.index((-ow, -on))
                for src, dst, where, send, recv, mine in copies(i, ow, on)[part]:
                    sems = mine, mine + opposite - i
                    remote(src, dst, where, send, recv, sems, ow, on).start()

    def arrive(copies, offsets, chosen=None):
        for i, (ow, on) in enumerate(offsets):
            if chosen is None or i in chosen:
                for src, dst, where, send, recv, mine in copies(i, ow, on):
                    landed(dst, where, send, recv, mine).wait_recv()

    def sent(copies, offsets):
        for i, (ow, on) in enumerate(offsets):
            for src, dst, where, send, recv, mine in copies(i, ow, on):
                landed(dst, where, send, recv, mine).wait_send()

    along_wide = [(o, 0) for o in WINDOW]
    along_narrow = [(0, o) for o in WINDOW]

    start(copies0, NEIGHBOURS, (4, 5), slice(0, 1))
    tell(ready_sem.at[0], AXIAL)
    start(copies0, NEIGHBOURS, (6, 7))
    start(copies0, NEIGHBOURS, (4, 5), slice(1, 2))
    pl.semaphore_wait(ready_sem.at[0], len(AXIAL))
    start(copies0, NEIGHBOURS, (0, 1, 2, 3))
    tell(ready_sem.at[1], AXIAL)

    @pl.when(w == 0)
    def _():
        f0[:, 0:4] = jnp.zeros((3, 4, 24, 128), F32)
        k0[0:4] = jnp.zeros((4, 24, 128), F32)

    @pl.when(w == nw - 1)
    def _():
        f0[:, 20:24] = jnp.zeros((3, 4, 24, 128), F32)
        k0[20:24] = jnp.zeros((4, 24, 128), F32)

    @pl.when(n == 0)
    def _():
        f0[:, :, 20:24, :] = jnp.zeros((3, 24, 4, 128), F32)
        k0[:, 20:24, :] = jnp.zeros((24, 4, 128), F32)

    @pl.when(n == nn - 1)
    def _():
        f0[:, :, 16:20, :] = jnp.zeros((3, 24, 4, 128), F32)
        k0[:, 16:20, :] = jnp.zeros((24, 4, 128), F32)

    r, c = iota((256, 128), 0), iota((256, 128), 1)
    m01[...] = indicator(((r >> 7) == (c >> 6)) & (((r & 127) >> 1) == (c & 63)), 0.125)
    r, c = iota((512, 128), 0), iota((512, 128), 1)
    m12[...] = indicator(((r >> 7) == (c >> 5)) & (((r & 63) >> 1) == (c & 31)), 0.125)
    m23[...] = indicator(
        ((r >> 7) == (c >> 5))
        & (((r >> 6) & 1) == ((c >> 4) & 1))
        & (((r & 31) >> 1) == (c & 15)),
        0.125,
    )
    r, c = iota((384, 128), 0), iota((384, 128), 1)
    m34[...] = indicator(((r >> 5) == (c >> 3)) & (((r & 15) >> 1) == (c & 7)), 0.125)
    r, c = iota((128, 256), 0), iota((128, 256), 1)
    p1[...] = indicator(((r >> 6) == (c >> 7)) & ((r & 63) == ((c & 127) >> 1)))
    r, c = iota((128, 512), 0), iota((128, 512), 1)
    p2[...] = indicator(((r >> 5) == (c >> 7)) & ((r & 31) == ((c & 127) >> 2)))
    r, c = iota((256, 256), 0), iota((256, 256), 1)
    fine = ((r >> 4) == (2 + (c >> 7))) & ((r & 15) == ((c & 127) >> 3))
    coarse = (r >= 128 + 40) & (r < 128 + 48) & ((r & 7) == ((c & 127) >> 4))
    p34[...] = indicator(fine | coarse)

    own_c.wait()
    coup = [[coup_ref[i, j] for j in range(3)] for i in range(3)]

    for i in range(8):
        t0[pl.ds(384 + 16 * i, 16), :] = (
            k0[4 + 2 * i, 0:16, :] + k0[5 + 2 * i, 0:16, :]
        )

    def halved(first, count):
        s = t0[pl.ds(first, count, stride=2), :] + t0[pl.ds(first + 1, count, stride=2), :]
        s = s.reshape(count // 16, 2, 8, 128)
        pair = [s[:, u].reshape(count // 2, 128) for u in range(2)]
        return mm(jnp.concatenate(pair, axis=1), m01[...])

    g1[3, 2:6, 0:8, :] = halved(384, 64).reshape(4, 8, 128)
    for p in range(4):
        t1[pl.ds(96 + 8 * p, 8), :] = g1[3, 2 + p, 0:8, :]

    theta0, steps0 = chebyshev(0)
    lane24 = iota((24, 128), 1)
    lane16 = iota((16, 128), 1)
    fields = [f0, d1, d2, d3]

    def sweep0(k, starts, count):
        d = fields[k]
        over = 1.0 / theta0 if k == 0 else 1.0
        scale, mass = over / 26.0, over * MASS
        rest = f0 if k == 0 else r0
        rows, lane = (24, lane24) if k < 3 else (16, lane16)
        for lo in starts:
            for i in range(lo, lo + count, 2):
                mids, boxes = [[], []], [[], []]
                for c in range(3):
                    a, b = d[c, i], d[c, i + 1]
                    both = a + b
                    for u, (mid, x) in enumerate(((a, d[c, i - 1]), (b, d[c, i + 2]))):
                        s = both + x
                        s = s + pltpu.roll(s, 1, 0) + pltpu.roll(s, 23, 0)
                        s = s[0:rows]
                        s = (
                            s
                            + jnp.where(lane == 0, 0.0, pltpu.roll(s, 1, 1))
                            + jnp.where(lane == 127, 0.0, pltpu.roll(s, 127, 1))
                        )
                        mids[u].append(mid[0:rows])
                        boxes[u].append(s)
                new = []
                for u in range(2):
                    us = [27.0 * mids[u][c] - boxes[u][c] for c in range(3)]
                    a = mix(coup, scale, mass, us, mids[u], k0[i + u, 0:rows])
                    new.append([rest[c, i + u, 0:rows] - a[c] for c in range(3)])
                    if k < 3:
                        ca, cb = steps0[k]
                        for c in range(3):
                            r0[c, i + u] = new[u][c]
                            fields[k + 1][c, i + u] = (ca * over) * mids[u][c] + cb * new[u][c]
                if k == 3:
                    for c in range(3):
                        t0[pl.ds(128 * c + 8 * (i - 4), 16), :] = new[0][c] + new[1][c]

    arrive(copies0, NEIGHBOURS, (6, 7))
    for k in range(4):
        sweep0(k, (5 + k,), 14 - 2 * k)
    arrive(copies0, NEIGHBOURS, (0, 1, 2, 3, 4, 5))
    pl.semaphore_wait(ready_sem.at[1], len(AXIAL))
    start(copies1, NEIGHBOURS, None, slice(1, 2))
    for k in range(4):
        sweep0(k, (1 + k, 19 - k), 4)
    g1[0:3, 2:6, 0:8, :] = halved(0, 192).reshape(3, 4, 8, 128)
    start(copies1, NEIGHBOURS, None, slice(0, 1))
    sent(copies0, NEIGHBOURS)

    def sum0(i, carry):
        for c in range(3):
            acc[c][i] = (
                f0[c, 4 + i, 0:16, :] * (1.0 / theta0)
                + d1[c, 4 + i, 0:16, :]
                + d2[c, 4 + i, 0:16, :]
                + d3[c, 4 + i, 0:16, :]
            )
        return carry

    lax.fori_loop(0, 16, sum0, 0)

    arrive(copies1, NEIGHBOURS)

    theta1, steps1 = chebyshev(1)
    lower = lane16 < 64
    zpos1 = lane16 & 63

    def plane1(p, d, scale, mass):
        us, mids = [], []
        for c in range(3):
            mid = d[c, p]
            swap = mid + jnp.where(lower, d[c, min(p + 1, 7)], d[c, max(p - 1, 0)])
            up = pltpu.roll(mid, 1, 1) + pltpu.roll(swap, 65, 1)
            down = pltpu.roll(mid, 127, 1) + pltpu.roll(swap, 63, 1)
            s = mid + pltpu.roll(swap, 64, 1)
            s = s + jnp.where(zpos1 == 0, 0.0, up) + jnp.where(zpos1 == 63, 0.0, down)
            s = s + pltpu.roll(s, 1, 0) + pltpu.roll(s, 15, 0)
            us.append(27.0 * mid - s)
            mids.append(mid)
        return mids, mix(coup, scale, mass, us, mids, g1[3, p])

    x1 = {}
    fields1 = [g1, e1, e2, e1]
    for k, (lo, hi) in enumerate([(0, 8), (1, 7), (1, 7), (2, 6)]):
        d = fields1[k]
        over = 1.0 / theta1 if k == 0 else 1.0
        scale, mass = over / (4.0 * 26.0), over * MASS
        for p in range(lo, hi):
            mids, a = plane1(p, d, scale, mass)
            for c in range(3):
                new = (g1 if k == 0 else r1)[c, p] - a[c]
                if k < 3:
                    ca, cb = steps1[k]
                    r1[c, p] = new
                    fields1[k + 1][c, p] = (ca * over) * mids[c] + cb * new
                else:
                    t1[pl.ds(32 * c + 8 * (p - 2), 8), :] = new[0:8]
                if 2 <= p < 6:
                    part = (mids[c] * over)[0:8]
                    x1[c, p] = part if k == 0 else x1[c, p] + part

    ys = [t1[pl.ds(y, 16, stride=8), :] for y in range(8)]
    ys = jnp.concatenate([ys[2 * j] + ys[2 * j + 1] for j in range(4)], axis=1)
    blk = mm(ys, m12[...])
    for c in range(4):
        g2[c, 4:8, 128:256] = blk[4 * c : 4 * c + 4]
    start(copies2, NEIGHBOURS)
    sent(copies1, NEIGHBOURS)

    rows = jnp.concatenate([x1[c, p] for c in range(3) for p in range(2, 6)], axis=0)
    rep = mm(rows, p1[...])
    u_lo[pl.ds(0, 96, stride=2), :] = rep[:, 0:128]
    u_lo[pl.ds(1, 96, stride=2), :] = rep[:, 0:128]
    u_hi[pl.ds(0, 96, stride=2), :] = rep[:, 128:256]
    u_hi[pl.ds(1, 96, stride=2), :] = rep[:, 128:256]
    for c in range(3):
        for p in range(4):
            rows_cp = pl.ds(16 * (4 * c + p), 16)
            for j in range(4):
                acc[c][4 * p + j] += (u_lo if j < 2 else u_hi)[rows_cp, :]

    arrive(copies2, NEIGHBOURS)

    f2 = [[g2[c, :, 128 * j : 128 * j + 128] for j in range(3)] for c in range(4)]
    x2, r2 = flat_smooth(f2[:3], f2[3], coup, 2, 32, True)

    t2[...] = mm(
        jnp.concatenate([r2[0][1], r2[1][1], r2[2][1], f2[3][1]], axis=1), m23[...]
    )
    h3[10:12, :] = t2[pl.ds(4, 2, stride=2), :] + t2[pl.ds(5, 2, stride=2), :]
    start(copies3, along_wide)
    sent(copies2, NEIGHBOURS)

    for c in range(3):
        t3[4 * c : 4 * c + 4, 0:128] = x2[c][1][4:8]
    rep = mm(t3[0:16, 0:128], p2[...])
    for y in range(16):
        j = y // 4
        v2[pl.ds(y, 16, stride=16), :] = rep[:, 128 * j : 128 * j + 128]
    for c in range(3):
        for k in range(4):
            part = v2[pl.ds(16 * (4 * c + k), 16), :]
            for j in range(4):
                acc[c][4 * k + j] += part

    arrive(copies3, along_wide)
    start(copies4, along_narrow)
    sent(copies3, along_wide)
    arrive(copies4, along_narrow)
    sent(copies4, along_narrow)

    lane3 = iota((24, 128), 1)
    slots = [h3s[j] if j != 5 else h3[...] for j in range(11)]
    f3 = [[None] * 3 for _ in range(4)]
    for c in range(4):
        for v in range(3):
            out = jnp.zeros((24, 128), F32)
            for q in range(4):
                j = 4 * v + q
                if j < 11:
                    turn = 32 * ((q - c) % 4)
                    part = pltpu.roll(slots[j], turn, 1) if turn else slots[j]
                    out = jnp.where((lane3 >> 5) == q, part, out)
            f3[c][v] = out
    x3, r3 = flat_smooth(f3[:3], f3[3], coup, 3, 16, True)

    z4[...] = mm(
        jnp.concatenate(
            [jnp.concatenate(r3[c] if c < 3 else f3[3], axis=1) for c in range(4)],
            axis=0,
        ),
        m34[...],
    )
    f4 = []
    for c in range(4):
        even, odd = (z4[pl.ds(24 * c + 4 + u, 8, stride=2), :] for u in range(2))
        f4.append([even + odd])
    x4, _ = flat_smooth(f4[:3], f4[3], coup, 4, 8, False)

    for c in range(3):
        t3[2 * c : 2 * c + 2, 0:128] = x3[c][1][10:12]
        t3[2 * c : 2 * c + 2, 128:256] = jnp.broadcast_to(x4[c][0][3:4], (2, 128))
    tail_out[...] = (
        mm(t3[0:16, 0:128], p34[0:128, :]) + mm(t3[0:16, 128:256], p34[128:256, :])
    )[0:8]


def solution(mesh):
    nw, nn = mesh.shape["wide"], mesh.shape["narrow"]

    def vm(*shape):
        return pltpu.VMEM(shape, F32)

    def mat(*shape):
        return pltpu.VMEM(shape, BF16)

    dma = pltpu.SemaphoreType.DMA
    scratch = [
        vm(2, 3, 24, 24, 128),
        vm(2, 24, 24, 128),
        vm(3, 24, 24, 128),
        vm(3, 24, 24, 128),
        vm(3, 24, 24, 128),
        vm(3, 24, 24, 128),
        vm(512, 128),
        vm(2, 4, 8, 16, 128),
        vm(3, 8, 16, 128),
        vm(3, 8, 16, 128),
        vm(3, 8, 16, 128),
        vm(128, 128),
        vm(192, 128),
        vm(192, 128),
        vm(2, 4, 16, 384),
        vm(16, 128),
        vm(256, 128),
        vm(2, 24, 128),
        vm(2, 11, 24, 128),
        vm(16, 256),
        vm(96, 128),
        mat(256, 128),
        mat(512, 128),
        mat(512, 128),
        mat(384, 128),
        mat(128, 256),
        mat(128, 512),
        mat(256, 256),
        pltpu.SMEM((3, 3), F32),
        dma((5,)),
        pltpu.SemaphoreType.REGULAR((2,)),
        dma((16,)),
        dma((16,)),
        dma((16,)),
        dma((16,)),
        dma((8,)),
        dma((8,)),
        dma((10,)),
        dma((10,)),
        dma((10,)),
        dma((10,)),
    ]

    def per_device(residual, stiffness, coupling):
        hbm = pl.BlockSpec(memory_space=pltpu.HBM)
        vmem = pl.BlockSpec(memory_space=pltpu.VMEM)
        *acc, tail = pl.pallas_call(
            functools.partial(kernel, nw, nn),
            out_shape=(
                *[jax.ShapeDtypeStruct((16, 16, 128), F32)] * 3,
                jax.ShapeDtypeStruct((8, 256), F32),
            ),
            in_specs=[hbm, hbm, hbm],
            out_specs=(vmem,) * 4,
            scratch_shapes=scratch,
            compiler_params=pltpu.CompilerParams(
                collective_id=0,
                has_side_effects=True,
                vmem_limit_bytes=(53 * 1024 + 450) * 1024,
            ),
        )(residual, stiffness, coupling)
        tail = tail[0:6].reshape(3, 2, 1, 2, 1, 128)
        return (jnp.stack(acc).reshape(3, 2, 8, 2, 8, 128) + tail).reshape(3, 16, 16, 128)

    return jax.shard_map(
        per_device,
        mesh=mesh,
        in_specs=(P(None, "wide", "narrow", None), P("wide", "narrow", None), P()),
        out_specs=P(None, "wide", "narrow", None),
        check_vma=False,
    )
```

```python
import functools

import jax
import jax.numpy as jnp
from jax import lax
from jax.experimental import pallas as pl
from jax.experimental.pallas import tpu as pltpu
from jax.sharding import PartitionSpec as P

LEVELS = 4
MASS = 0.001
RATIO = 8.0
MESH = pl.DeviceIdType.MESH
NEIGHBOURS = [(1, 1), (1, -1), (-1, 1), (-1, -1), (1, 0), (-1, 0), (0, 1), (0, -1)]
AXIAL = NEIGHBOURS[4:]
WINDOW = [o for k in range(5, 0, -1) for o in (k, -k)]
F32 = jnp.float32
BF16 = jnp.bfloat16


def chebyshev(level):
    top = 4.0 * (2.8 / 4.0**level + MASS)
    theta = (top + top / RATIO) / 2.0
    delta = (top - top / RATIO) / 2.0
    sigma = theta / delta
    rho = 1.0 / sigma
    steps = []
    for _ in range(3):
        nxt = 1.0 / (2.0 * sigma - rho)
        steps.append((nxt * rho, 2.0 * nxt / delta))
        rho = nxt
    return theta, steps


def iota(shape, dim):
    return lax.broadcasted_iota(jnp.int32, shape, dim)


def indicator(cond, value=1.0):
    return jnp.where(cond, value, 0.0).astype(BF16)


def mm(v, w):
    hi = v.astype(BF16)
    lo = (v - hi.astype(F32)).astype(BF16)
    return jnp.dot(hi, w, preferred_element_type=F32) + jnp.dot(
        lo, w, preferred_element_type=F32
    )


def mix(coup, scale, mass, u, d, k):
    out = []
    for c in range(3):
        a = (coup[c][0] * scale) * u[0]
        a = a + (coup[c][1] * scale) * u[1]
        a = a + (coup[c][2] * scale) * u[2]
        a = a + mass * d[c]
        out.append(k * a)
    return out


def flat_box(chunks, nz):
    rows = chunks[0].shape[0]
    lane = iota(chunks[0].shape, 1)
    zpos = lane & (nz - 1)
    s = []
    for v in chunks:
        v = v + pltpu.roll(v, 1, 0) + pltpu.roll(v, rows - 1, 0)
        s.append(
            v
            + jnp.where(zpos == 0, 0.0, pltpu.roll(v, 1, 1))
            + jnp.where(zpos == nz - 1, 0.0, pltpu.roll(v, 127, 1))
        )
    up = [pltpu.roll(v, nz, 1) for v in s]
    down = [pltpu.roll(v, 128 - nz, 1) for v in s]
    out = []
    for j, v in enumerate(s):
        before = up[j - 1] if j > 0 else 0.0
        after = down[j + 1] if j + 1 < len(s) else 0.0
        out.append(
            v
            + jnp.where(lane < nz, before, up[j])
            + jnp.where(lane >= 128 - nz, after, down[j])
        )
    return out


def flat_box_wide(chunks, nz):
    rows = chunks[0].shape[0]
    lane = iota(chunks[0].shape, 1)
    zpos = lane & (nz - 1)

    def shifted(v, y):
        mid = pltpu.roll(v, y % 128, 1) if y else v
        return (
            mid
            + jnp.where(zpos == 0, 0.0, pltpu.roll(v, (y + 1) % 128, 1))
            + jnp.where(zpos == nz - 1, 0.0, pltpu.roll(v, (y - 1) % 128, 1))
        )

    xs = [v + pltpu.roll(v, 1, 0) + pltpu.roll(v, rows - 1, 0) for v in chunks]
    up = [shifted(v, nz) for v in xs]
    down = [shifted(v, -nz) for v in xs]
    out = []
    for j, v in enumerate(xs):
        before = up[j - 1] if j > 0 else 0.0
        after = down[j + 1] if j + 1 < len(xs) else 0.0
        out.append(
            shifted(v, 0)
            + jnp.where(lane < nz, before, up[j])
            + jnp.where(lane >= 128 - nz, after, down[j])
        )
    return out


def flat_smooth(f, kappa, coup, level, nz, want_rest):
    theta, steps = chebyshev(level)
    scale = 4.0**-level / 26.0
    n = len(kappa)

    def apply(r, d):
        box = flat_box if n > 1 else flat_box_wide
        boxes = [box(d[c], nz) for c in range(3)]
        new = [[None] * n for _ in range(3)]
        for j in range(n):
            u = [27.0 * d[c][j] - boxes[c][j] for c in range(3)]
            a = mix(coup, scale, MASS, u, [d[c][j] for c in range(3)], kappa[j])
            for c in range(3):
                new[c][j] = r[c][j] - a[c]
        return new

    r = f
    d = [[v * (1.0 / theta) for v in f[c]] for c in range(3)]
    x = d
    for a, b in steps:
        r = apply(r, d)
        d = [[a * d[c][j] + b * r[c][j] for j in range(n)] for c in range(3)]
        x = [[x[c][j] + d[c][j] for j in range(n)] for c in range(3)]
    if want_rest:
        r = apply(r, d)
    return x, r


def kernel(
    nw,
    nn,
    res,
    stiff,
    coup_hbm,
    acc0,
    acc1,
    acc2,
    tail_out,
    f0b,
    k0b,
    r0,
    d1,
    d2,
    d3,
    t0,
    g1b,
    r1,
    e1,
    e2,
    t1,
    u_lo,
    u_hi,
    g2b,
    t2,
    v2,
    h3b,
    h3sb,
    t3,
    z4,
    m01,
    m12,
    m23,
    m34,
    p1,
    p2,
    p34,
    coup_ref,
    local_sem,
    ready_sem,
    s0,
    q0,
    s1,
    q1,
    s2,
    q2,
    s3,
    q3,
    s4,
    q4,
):
    w = lax.axis_index("wide")
    n = lax.axis_index("narrow")
    acc = [acc0, acc1, acc2]
    f0, k0, g1, g2, h3, h3s = (b.at[0] for b in (f0b, k0b, g1b, g2b, h3b, h3sb))

    def pair_of(i):
        return i + 1 - 2 * lax.rem(i, 2)

    def out_of(pos, off, size):
        if off == 0:
            return jnp.bool_(False)
        return pos + off >= size if off > 0 else pos + off < 0

    targets = {}

    def target(ow, on):
        if (ow, on) in targets:
            return targets[ow, on]
        w_out, n_out = out_of(w, ow, nw), out_of(n, on, nn)
        if on == 0:
            tw = jnp.where(w_out, w, w + ow)
            tn = jnp.where(w_out, pair_of(n), n)
            away = w_out
        elif ow == 0:
            tw = jnp.where(n_out, pair_of(w), w)
            tn = jnp.where(n_out, n, n + on)
            away = n_out
        else:
            w_end, n_end = (nw - 1 if ow > 0 else 0), (nn - 1 if on > 0 else 0)
            both = jnp.logical_and(w_out, n_out)
            away = jnp.logical_or(w_out, n_out)
            w_near, n_near = w == w_end - ow, n == n_end - on
            tw = jnp.where(
                both,
                w - ow,
                jnp.where(
                    w_out,
                    w,
                    jnp.where(n_out, jnp.where(w_near, w + ow, pair_of(w)), w + ow),
                ),
            )
            tn = jnp.where(
                both,
                n,
                jnp.where(
                    w_out,
                    jnp.where(n_near, n + on, pair_of(n)),
                    jnp.where(n_out, jnp.where(w_near, n - on, n), n + on),
                ),
            )
        targets[ow, on] = tw, tn, jnp.where(away, 1, 0)
        return targets[ow, on]

    def remote(src, dst, where, send, recv, sems, ow, on):
        tw, tn, away = target(ow, on)
        mine, other = sems
        return pltpu.make_async_remote_copy(
            src_ref=src,
            dst_ref=dst.at[(away,) + where],
            send_sem=send.at[mine],
            recv_sem=recv.at[mine + (other - mine) * away],
            device_id={"wide": tw, "narrow": tn},
            device_id_type=MESH,
        )

    def landed(buf, where, send, recv, mine):
        return pltpu.make_async_remote_copy(
            src_ref=buf.at[(0,) + where],
            dst_ref=buf.at[(0,) + where],
            send_sem=send.at[mine],
            recv_sem=recv.at[mine],
            device_id={"wide": w, "narrow": n},
            device_id_type=MESH,
        )

    own_f = [
        pltpu.make_async_copy(res.at[c], f0.at[c, 4:20, 0:16, :], local_sem.at[2 + c])
        for c in range(3)
    ]
    own_k = pltpu.make_async_copy(stiff, k0.at[4:20, 0:16, :], local_sem.at[1])
    own_c = pltpu.make_async_copy(coup_hbm, coup_ref, local_sem.at[0])
    for c in own_f:
        c.start()

    h3[...] = jnp.zeros_like(h3)
    h3s[...] = jnp.zeros_like(h3s)

    def tell(sem, offsets):
        for ow, on in offsets:
            tw, tn, _ = target(ow, on)
            pl.semaphore_signal(
                sem,
                inc=1,
                device_id={"wide": tw, "narrow": tn},
                device_id_type=MESH,
            )

    barrier = pltpu.get_barrier_semaphore()
    tell(barrier, AXIAL)
    own_k.start()
    own_c.start()
    g1[...] = jnp.zeros_like(g1)
    g2[...] = jnp.zeros_like(g2)
    for c in own_f:
        c.wait()
    own_k.wait()
    pl.semaphore_wait(barrier, len(AXIAL))

    def copies0(i, ow, on):
        sx, dx = {0: (0, 4), 1: (12, 0), -1: (0, 20)}[ow]
        sy, dy = {0: (0, 0), 1: (12, 20), -1: (0, 16)}[on]
        nx, ny = (16 if ow == 0 else 4), (16 if on == 0 else 4)
        fs = (slice(None), slice(4 + sx, 4 + sx + nx), slice(sy, sy + ny))
        fd = (slice(None), slice(dx, dx + nx), slice(dy, dy + ny))
        if ow > 0:
            sx, dx = sx + 1, dx + 1
        if on > 0:
            sy, dy = sy + 1, dy + 1
        nx, ny = (16 if ow == 0 else 3), (16 if on == 0 else 3)
        ks = (slice(4 + sx, 4 + sx + nx), slice(sy, sy + ny))
        kd = (slice(dx, dx + nx), slice(dy, dy + ny))
        return [
            (f0.at[fs], f0b, fd, s0, q0, i),
            (k0.at[ks], k0b, kd, s0, q0, 8 + i),
        ]

    def copies1(i, ow, on):
        sx, dx = {0: ((2, 6), (2, 6)), 1: ((4, 6), (0, 2)), -1: ((2, 4), (6, 8))}[ow]
        sy, dy = {0: ((0, 8), (0, 8)), 1: ((4, 8), (12, 16)), -1: ((0, 4), (8, 12))}[on]
        sx, dx, sy, dy = slice(*sx), slice(*dx), slice(*sy), slice(*dy)
        return [
            (g1.at[0:3, sx, sy], g1b, (slice(0, 3), dx, dy), s1, q1, i),
            (g1.at[3, sx, sy], g1b, (3, dx, dy), s1, q1, 8 + i),
        ]

    def copies2(i, ow, on):
        dx = slice(4 - 4 * ow, 8 - 4 * ow)
        dy = slice(128 - 128 * on, 256 - 128 * on)
        return [(g2.at[:, 4:8, 128:256], g2b, (slice(None), dx, dy), s2, q2, i)]

    def copies3(i, ow, on):
        row = (6 - 2 * ow) % 24
        return [(h3.at[6:8, :], h3b, (slice(row, row + 2),), s3, q3, i)]

    def copies4(i, ow, on):
        near, far = slice(0, 12), slice(12, 24)
        return [
            (h3.at[near], h3sb, (5 - on, near), s4, q4, i),
            (h3.at[far], h3sb, (5 - on, far), s4, q4, 10 + i),
        ]

    def start(copies, offsets, chosen=None, part=slice(None)):
        for i, (ow, on) in enumerate(offsets):
            if chosen is None or i in chosen:
                opposite = offsets.index((-ow, -on))
                for src, dst, where, send, recv, mine in copies(i, ow, on)[part]:
                    sems = mine, mine + opposite - i
                    remote(src, dst, where, send, recv, sems, ow, on).start()

    def arrive(copies, offsets, chosen=None):
        for i, (ow, on) in enumerate(offsets):
            if chosen is None or i in chosen:
                for src, dst, where, send, recv, mine in copies(i, ow, on):
                    landed(dst, where, send, recv, mine).wait_recv()

    def sent(copies, offsets):
        for i, (ow, on) in enumerate(offsets):
            for src, dst, where, send, recv, mine in copies(i, ow, on):
                landed(dst, where, send, recv, mine).wait_send()

    along_wide = [(o, 0) for o in WINDOW]
    along_narrow = [(0, o) for o in WINDOW]

    start(copies0, NEIGHBOURS, (4, 5), slice(0, 1))
    tell(ready_sem.at[0], AXIAL)
    start(copies0, NEIGHBOURS, (6, 7))
    start(copies0, NEIGHBOURS, (4, 5), slice(1, 2))
    pl.semaphore_wait(ready_sem.at[0], len(AXIAL))
    start(copies0, NEIGHBOURS, (0, 1, 2, 3))
    tell(ready_sem.at[1], AXIAL)

    @pl.when(w == 0)
    def _():
        f0[:, 0:4] = jnp.zeros((3, 4, 24, 128), F32)
        k0[0:4] = jnp.zeros((4, 24, 128), F32)

    @pl.when(w == nw - 1)
    def _():
        f0[:, 20:24] = jnp.zeros((3, 4, 24, 128), F32)
        k0[20:24] = jnp.zeros((4, 24, 128), F32)

    @pl.when(n == 0)
    def _():
        f0[:, :, 20:24, :] = jnp.zeros((3, 24, 4, 128), F32)
        k0[:, 20:24, :] = jnp.zeros((24, 4, 128), F32)

    @pl.when(n == nn - 1)
    def _():
        f0[:, :, 16:20, :] = jnp.zeros((3, 24, 4, 128), F32)
        k0[:, 16:20, :] = jnp.zeros((24, 4, 128), F32)

    r, c = iota((256, 128), 0), iota((256, 128), 1)
    m01[...] = indicator(((r >> 7) == (c >> 6)) & (((r & 127) >> 1) == (c & 63)), 0.125)
    r, c = iota((512, 128), 0), iota((512, 128), 1)
    m12[...] = indicator(((r >> 7) == (c >> 5)) & (((r & 63) >> 1) == (c & 31)), 0.125)
    m23[...] = indicator(
        ((r >> 7) == (c >> 5))
        & (((r >> 6) & 1) == ((c >> 4) & 1))
        & (((r & 31) >> 1) == (c & 15)),
        0.125,
    )
    r, c = iota((384, 128), 0), iota((384, 128), 1)
    m34[...] = indicator(((r >> 5) == (c >> 3)) & (((r & 15) >> 1) == (c & 7)), 0.125)
    r, c = iota((128, 256), 0), iota((128, 256), 1)
    p1[...] = indicator(((r >> 6) == (c >> 7)) & ((r & 63) == ((c & 127) >> 1)))
    r, c = iota((128, 512), 0), iota((128, 512), 1)
    p2[...] = indicator(((r >> 5) == (c >> 7)) & ((r & 31) == ((c & 127) >> 2)))
    r, c = iota((256, 256), 0), iota((256, 256), 1)
    fine = ((r >> 4) == (2 + (c >> 7))) & ((r & 15) == ((c & 127) >> 3))
    coarse = (r >= 128 + 40) & (r < 128 + 48) & ((r & 7) == ((c & 127) >> 4))
    p34[...] = indicator(fine | coarse)

    own_c.wait()
    coup = [[coup_ref[i, j] for j in range(3)] for i in range(3)]

    for i in range(8):
        t0[pl.ds(384 + 16 * i, 16), :] = (
            k0[4 + 2 * i, 0:16, :] + k0[5 + 2 * i, 0:16, :]
        )

    def halved(first, count):
        s = t0[pl.ds(first, count, stride=2), :] + t0[pl.ds(first + 1, count, stride=2), :]
        s = s.reshape(count // 16, 2, 8, 128)
        pair = [s[:, u].reshape(count // 2, 128) for u in range(2)]
        return mm(jnp.concatenate(pair, axis=1), m01[...])

    g1[3, 2:6, 0:8, :] = halved(384, 64).reshape(4, 8, 128)
    for p in range(4):
        t1[pl.ds(96 + 8 * p, 8), :] = g1[3, 2 + p, 0:8, :]

    theta0, steps0 = chebyshev(0)
    lane24 = iota((24, 128), 1)
    lane16 = iota((16, 128), 1)
    fields = [f0, d1, d2, d3]

    def sweep0(k, starts, count):
        d = fields[k]
        over = 1.0 / theta0 if k == 0 else 1.0
        scale, mass = over / 26.0, over * MASS
        rest = f0 if k == 0 else r0
        rows, lane = (24, lane24) if k < 3 else (16, lane16)
        for lo in starts:
            for i in range(lo, lo + count, 2):
                mids, boxes = [[], []], [[], []]
                for c in range(3):
                    a, b = d[c, i], d[c, i + 1]
                    both = a + b
                    for u, (mid, x) in enumerate(((a, d[c, i - 1]), (b, d[c, i + 2]))):
                        s = both + x
                        s = s + pltpu.roll(s, 1, 0) + pltpu.roll(s, 23, 0)
                        s = s[0:rows]
                        s = (
                            s
                            + jnp.where(lane == 0, 0.0, pltpu.roll(s, 1, 1))
                            + jnp.where(lane == 127, 0.0, pltpu.roll(s, 127, 1))
                        )
                        mids[u].append(mid[0:rows])
                        boxes[u].append(s)
                new = []
                for u in range(2):
                    us = [27.0 * mids[u][c] - boxes[u][c] for c in range(3)]
                    a = mix(coup, scale, mass, us, mids[u], k0[i + u, 0:rows])
                    new.append([rest[c, i + u, 0:rows] - a[c] for c in range(3)])
                    if k < 3:
                        ca, cb = steps0[k]
                        for c in range(3):
                            r0[c, i + u] = new[u][c]
                            fields[k + 1][c, i + u] = (ca * over) * mids[u][c] + cb * new[u][c]
                if k == 3:
                    for c in range(3):
                        t0[pl.ds(128 * c + 8 * (i - 4), 16), :] = new[0][c] + new[1][c]

    arrive(copies0, NEIGHBOURS, (6, 7))
    for k in range(4):
        sweep0(k, (5 + k,), 14 - 2 * k)
    arrive(copies0, NEIGHBOURS, (0, 1, 2, 3, 4, 5))
    pl.semaphore_wait(ready_sem.at[1], len(AXIAL))
    start(copies1, NEIGHBOURS, None, slice(1, 2))
    for k in range(4):
        sweep0(k, (1 + k, 19 - k), 4)
    g1[0:3, 2:6, 0:8, :] = halved(0, 192).reshape(3, 4, 8, 128)
    start(copies1, NEIGHBOURS, None, slice(0, 1))
    sent(copies0, NEIGHBOURS)

    def sum0(i, carry):
        for c in range(3):
            acc[c][i] = (
                f0[c, 4 + i, 0:16, :] * (1.0 / theta0)
                + d1[c, 4 + i, 0:16, :]
                + d2[c, 4 + i, 0:16, :]
                + d3[c, 4 + i, 0:16, :]
            )
        return carry

    lax.fori_loop(0, 16, sum0, 0)

    arrive(copies1, NEIGHBOURS)

    theta1, steps1 = chebyshev(1)
    lower = lane16 < 64
    zpos1 = lane16 & 63

    def plane1(p, d, scale, mass):
        us, mids = [], []
        for c in range(3):
            mid = d[c, p]
            swap = mid + jnp.where(lower, d[c, min(p + 1, 7)], d[c, max(p - 1, 0)])
            up = pltpu.roll(mid, 1, 1) + pltpu.roll(swap, 65, 1)
            down = pltpu.roll(mid, 127, 1) + pltpu.roll(swap, 63, 1)
            s = mid + pltpu.roll(swap, 64, 1)
            s = s + jnp.where(zpos1 == 0, 0.0, up) + jnp.where(zpos1 == 63, 0.0, down)
            s = s + pltpu.roll(s, 1, 0) + pltpu.roll(s, 15, 0)
            us.append(27.0 * mid - s)
            mids.append(mid)
        return mids, mix(coup, scale, mass, us, mids, g1[3, p])

    x1 = {}
    fields1 = [g1, e1, e2, e1]
    for k, (lo, hi) in enumerate([(0, 8), (1, 7), (1, 7), (2, 6)]):
        d = fields1[k]
        over = 1.0 / theta1 if k == 0 else 1.0
        scale, mass = over / (4.0 * 26.0), over * MASS
        for p in range(lo, hi):
            mids, a = plane1(p, d, scale, mass)
            for c in range(3):
                new = (g1 if k == 0 else r1)[c, p] - a[c]
                if k < 3:
                    ca, cb = steps1[k]
                    r1[c, p] = new
                    fields1[k + 1][c, p] = (ca * over) * mids[c] + cb * new
                else:
                    t1[pl.ds(32 * c + 8 * (p - 2), 8), :] = new[0:8]
                if 2 <= p < 6:
                    part = (mids[c] * over)[0:8]
                    x1[c, p] = part if k == 0 else x1[c, p] + part

    ys = [t1[pl.ds(y, 16, stride=8), :] for y in range(8)]
    ys = jnp.concatenate([ys[2 * j] + ys[2 * j + 1] for j in range(4)], axis=1)
    blk = mm(ys, m12[...])
    for c in range(4):
        g2[c, 4:8, 128:256] = blk[4 * c : 4 * c + 4]
    start(copies2, NEIGHBOURS)
    sent(copies1, NEIGHBOURS)

    rows = jnp.concatenate([x1[c, p] for c in range(3) for p in range(2, 6)], axis=0)
    rep = mm(rows, p1[...])
    u_lo[pl.ds(0, 96, stride=2), :] = rep[:, 0:128]
    u_lo[pl.ds(1, 96, stride=2), :] = rep[:, 0:128]
    u_hi[pl.ds(0, 96, stride=2), :] = rep[:, 128:256]
    u_hi[pl.ds(1, 96, stride=2), :] = rep[:, 128:256]
    for c in range(3):
        for p in range(4):
            rows_cp = pl.ds(16 * (4 * c + p), 16)
            for j in range(4):
                acc[c][4 * p + j] += (u_lo if j < 2 else u_hi)[rows_cp, :]

    arrive(copies2, NEIGHBOURS)

    f2 = [[g2[c, :, 128 * j : 128 * j + 128] for j in range(3)] for c in range(4)]
    x2, r2 = flat_smooth(f2[:3], f2[3], coup, 2, 32, True)

    t2[...] = mm(
        jnp.concatenate([r2[0][1], r2[1][1], r2[2][1], f2[3][1]], axis=1), m23[...]
    )
    h3[6:8, :] = t2[pl.ds(4, 2, stride=2), :] + t2[pl.ds(5, 2, stride=2), :]
    start(copies3, along_wide)
    sent(copies2, NEIGHBOURS)

    for c in range(3):
        t3[4 * c : 4 * c + 4, 0:128] = x2[c][1][4:8]
    rep = mm(t3[0:16, 0:128], p2[...])
    for y in range(16):
        j = y // 4
        v2[pl.ds(y, 16, stride=16), :] = rep[:, 128 * j : 128 * j + 128]
    for c in range(3):
        for k in range(4):
            part = v2[pl.ds(16 * (4 * c + k), 16), :]
            for j in range(4):
                acc[c][4 * k + j] += part

    close = [i for i, (ow, _) in enumerate(along_wide) if -2 <= ow <= 3]
    apart = [i for i in range(len(along_wide)) if i not in close]
    arrive(copies3, along_wide, close)
    start(copies4, along_narrow, None, slice(0, 1))
    arrive(copies3, along_wide, apart)
    start(copies4, along_narrow, None, slice(1, 2))
    sent(copies3, along_wide)
    arrive(copies4, along_narrow)
    sent(copies4, along_narrow)

    lane3 = iota((24, 128), 1)
    slots = [h3s[j] if j != 5 else h3[...] for j in range(11)]
    f3 = [[None] * 3 for _ in range(4)]
    for c in range(4):
        for v in range(3):
            out = jnp.zeros((24, 128), F32)
            for q in range(4):
                j = 4 * v + q
                if j < 11:
                    turn = 32 * ((q - c) % 4)
                    part = pltpu.roll(slots[j], turn, 1) if turn else slots[j]
                    out = jnp.where((lane3 >> 5) == q, part, out)
            f3[c][v] = out
    x3, r3 = flat_smooth(f3[:3], f3[3], coup, 3, 16, True)

    z4[...] = mm(
        jnp.concatenate(
            [jnp.concatenate(r3[c] if c < 3 else f3[3], axis=1) for c in range(4)],
            axis=0,
        ),
        m34[...],
    )
    f4 = []
    for c in range(4):
        even, odd = (z4[pl.ds(24 * c + u, 8, stride=2), :] for u in range(2))
        f4.append([even + odd])
    x4, _ = flat_smooth(f4[:3], f4[3], coup, 4, 8, False)

    for c in range(3):
        t3[2 * c : 2 * c + 2, 0:128] = x3[c][1][6:8]
        t3[2 * c : 2 * c + 2, 128:256] = jnp.broadcast_to(x4[c][0][3:4], (2, 128))
    tail_out[...] = (
        mm(t3[0:16, 0:128], p34[0:128, :]) + mm(t3[0:16, 128:256], p34[128:256, :])
    )[0:8]


def solution(mesh):
    nw, nn = mesh.shape["wide"], mesh.shape["narrow"]

    def vm(*shape):
        return pltpu.VMEM(shape, F32)

    def mat(*shape):
        return pltpu.VMEM(shape, BF16)

    dma = pltpu.SemaphoreType.DMA
    scratch = [
        vm(2, 3, 24, 24, 128),
        vm(2, 24, 24, 128),
        vm(3, 24, 24, 128),
        vm(3, 24, 24, 128),
        vm(3, 24, 24, 128),
        vm(3, 24, 24, 128),
        vm(512, 128),
        vm(2, 4, 8, 16, 128),
        vm(3, 8, 16, 128),
        vm(3, 8, 16, 128),
        vm(3, 8, 16, 128),
        vm(128, 128),
        vm(192, 128),
        vm(192, 128),
        vm(2, 4, 16, 384),
        vm(16, 128),
        vm(256, 128),
        vm(2, 24, 128),
        vm(2, 11, 24, 128),
        vm(16, 256),
        vm(96, 128),
        mat(256, 128),
        mat(512, 128),
        mat(512, 128),
        mat(384, 128),
        mat(128, 256),
        mat(128, 512),
        mat(256, 256),
        pltpu.SMEM((3, 3), F32),
        dma((5,)),
        pltpu.SemaphoreType.REGULAR((2,)),
        dma((16,)),
        dma((16,)),
        dma((16,)),
        dma((16,)),
        dma((8,)),
        dma((8,)),
        dma((10,)),
        dma((10,)),
        dma((20,)),
        dma((20,)),
    ]

    def per_device(residual, stiffness, coupling):
        hbm = pl.BlockSpec(memory_space=pltpu.HBM)
        vmem = pl.BlockSpec(memory_space=pltpu.VMEM)
        *acc, tail = pl.pallas_call(
            functools.partial(kernel, nw, nn),
            out_shape=(
                *[jax.ShapeDtypeStruct((16, 16, 128), F32)] * 3,
                jax.ShapeDtypeStruct((8, 256), F32),
            ),
            in_specs=[hbm, hbm, hbm],
            out_specs=(vmem,) * 4,
            scratch_shapes=scratch,
            compiler_params=pltpu.CompilerParams(
                collective_id=0,
                has_side_effects=True,
                vmem_limit_bytes=(53 * 1024 + 450) * 1024,
            ),
        )(residual, stiffness, coupling)
        tail = tail[0:6].reshape(3, 2, 1, 2, 1, 128)
        return (jnp.stack(acc).reshape(3, 2, 8, 2, 8, 128) + tail).reshape(3, 16, 16, 128)

    return jax.shard_map(
        per_device,
        mesh=mesh,
        in_specs=(P(None, "wide", "narrow", None), P("wide", "narrow", None), P()),
        out_specs=P(None, "wide", "narrow", None),
        check_vma=False,
    )
```

```python
import functools

import jax
import jax.numpy as jnp
from jax import lax
from jax.experimental import pallas as pl
from jax.experimental.pallas import tpu as pltpu
from jax.sharding import PartitionSpec as P

LEVELS = 4
MASS = 0.001
RATIO = 8.0
MESH = pl.DeviceIdType.MESH
NEIGHBOURS = [(1, 1), (1, -1), (-1, 1), (-1, -1), (1, 0), (-1, 0), (0, 1), (0, -1)]
AXIAL = NEIGHBOURS[4:]
WINDOW = [o for k in range(5, 0, -1) for o in (k, -k)]
F32 = jnp.float32
BF16 = jnp.bfloat16


def chebyshev(level):
    top = 4.0 * (2.8 / 4.0**level + MASS)
    theta = (top + top / RATIO) / 2.0
    delta = (top - top / RATIO) / 2.0
    sigma = theta / delta
    rho = 1.0 / sigma
    steps = []
    for _ in range(3):
        nxt = 1.0 / (2.0 * sigma - rho)
        steps.append((nxt * rho, 2.0 * nxt / delta))
        rho = nxt
    return theta, steps


def iota(shape, dim):
    return lax.broadcasted_iota(jnp.int32, shape, dim)


def indicator(cond, value=1.0):
    return jnp.where(cond, value, 0.0).astype(BF16)


def mm(v, w):
    hi = v.astype(BF16)
    lo = (v - hi.astype(F32)).astype(BF16)
    return jnp.dot(hi, w, preferred_element_type=F32) + jnp.dot(
        lo, w, preferred_element_type=F32
    )


def mix(coup, scale, mass, u, d, k):
    out = []
    for c in range(3):
        a = (coup[c][0] * scale) * u[0]
        a = a + (coup[c][1] * scale) * u[1]
        a = a + (coup[c][2] * scale) * u[2]
        a = a + mass * d[c]
        out.append(k * a)
    return out


def flat_box(chunks, nz):
    rows = chunks[0].shape[0]
    lane = iota(chunks[0].shape, 1)
    zpos = lane & (nz - 1)
    s = []
    for v in chunks:
        v = v + pltpu.roll(v, 1, 0) + pltpu.roll(v, rows - 1, 0)
        s.append(
            v
            + jnp.where(zpos == 0, 0.0, pltpu.roll(v, 1, 1))
            + jnp.where(zpos == nz - 1, 0.0, pltpu.roll(v, 127, 1))
        )
    up = [pltpu.roll(v, nz, 1) for v in s]
    down = [pltpu.roll(v, 128 - nz, 1) for v in s]
    out = []
    for j, v in enumerate(s):
        before = up[j - 1] if j > 0 else 0.0
        after = down[j + 1] if j + 1 < len(s) else 0.0
        out.append(
            v
            + jnp.where(lane < nz, before, up[j])
            + jnp.where(lane >= 128 - nz, after, down[j])
        )
    return out


def flat_box_wide(chunks, nz):
    rows = chunks[0].shape[0]
    lane = iota(chunks[0].shape, 1)
    zpos = lane & (nz - 1)

    def shifted(v, y):
        mid = pltpu.roll(v, y % 128, 1) if y else v
        return (
            mid
            + jnp.where(zpos == 0, 0.0, pltpu.roll(v, (y + 1) % 128, 1))
            + jnp.where(zpos == nz - 1, 0.0, pltpu.roll(v, (y - 1) % 128, 1))
        )

    xs = [v + pltpu.roll(v, 1, 0) + pltpu.roll(v, rows - 1, 0) for v in chunks]
    up = [shifted(v, nz) for v in xs]
    down = [shifted(v, -nz) for v in xs]
    out = []
    for j, v in enumerate(xs):
        before = up[j - 1] if j > 0 else 0.0
        after = down[j + 1] if j + 1 < len(xs) else 0.0
        out.append(
            shifted(v, 0)
            + jnp.where(lane < nz, before, up[j])
            + jnp.where(lane >= 128 - nz, after, down[j])
        )
    return out


def flat_smooth(f, kappa, coup, level, nz, want_rest):
    theta, steps = chebyshev(level)
    scale = 4.0**-level / 26.0
    n = len(kappa)

    def apply(r, d):
        box = flat_box if n > 1 else flat_box_wide
        boxes = [box(d[c], nz) for c in range(3)]
        new = [[None] * n for _ in range(3)]
        for j in range(n):
            u = [27.0 * d[c][j] - boxes[c][j] for c in range(3)]
            a = mix(coup, scale, MASS, u, [d[c][j] for c in range(3)], kappa[j])
            for c in range(3):
                new[c][j] = r[c][j] - a[c]
        return new

    r = f
    d = [[v * (1.0 / theta) for v in f[c]] for c in range(3)]
    x = d
    for a, b in steps:
        r = apply(r, d)
        d = [[a * d[c][j] + b * r[c][j] for j in range(n)] for c in range(3)]
        x = [[x[c][j] + d[c][j] for j in range(n)] for c in range(3)]
    if want_rest:
        r = apply(r, d)
    return x, r


def kernel(
    nw,
    nn,
    res,
    stiff,
    coup_hbm,
    acc0,
    acc1,
    acc2,
    tail_out,
    f0b,
    k0b,
    r0,
    d1,
    d2,
    d3,
    t0,
    g1b,
    r1,
    e1,
    e2,
    t1,
    u_lo,
    u_hi,
    g2b,
    t2,
    v2,
    h3b,
    h3sb,
    t3,
    z4,
    m01,
    m12,
    m23,
    m34,
    p1,
    p2,
    p34,
    coup_ref,
    local_sem,
    ready_sem,
    s0,
    q0,
    s1,
    q1,
    s2,
    q2,
    s3,
    q3,
    s4,
    q4,
):
    w = lax.axis_index("wide")
    n = lax.axis_index("narrow")
    acc = [acc0, acc1, acc2]
    f0, k0, g1, g2, h3, h3s = (b.at[0] for b in (f0b, k0b, g1b, g2b, h3b, h3sb))

    def pair_of(i):
        return i + 1 - 2 * lax.rem(i, 2)

    def out_of(pos, off, size):
        if off == 0:
            return jnp.bool_(False)
        return pos + off >= size if off > 0 else pos + off < 0

    targets = {}

    def target(ow, on):
        if (ow, on) in targets:
            return targets[ow, on]
        w_out, n_out = out_of(w, ow, nw), out_of(n, on, nn)
        if on == 0:
            tw = jnp.where(w_out, w, w + ow)
            tn = jnp.where(w_out, pair_of(n), n)
            away = w_out
        elif ow == 0:
            tw = jnp.where(n_out, pair_of(w), w)
            tn = jnp.where(n_out, n, n + on)
            away = n_out
        else:
            w_end, n_end = (nw - 1 if ow > 0 else 0), (nn - 1 if on > 0 else 0)
            both = jnp.logical_and(w_out, n_out)
            away = jnp.logical_or(w_out, n_out)
            w_near, n_near = w == w_end - ow, n == n_end - on
            tw = jnp.where(
                both,
                w - ow,
                jnp.where(
                    w_out,
                    w,
                    jnp.where(n_out, jnp.where(w_near, w + ow, pair_of(w)), w + ow),
                ),
            )
            tn = jnp.where(
                both,
                n,
                jnp.where(
                    w_out,
                    jnp.where(n_near, n + on, pair_of(n)),
                    jnp.where(n_out, jnp.where(w_near, n - on, n), n + on),
                ),
            )
        targets[ow, on] = tw, tn, jnp.where(away, 1, 0)
        return targets[ow, on]

    def remote(src, dst, where, send, recv, sems, ow, on):
        tw, tn, away = target(ow, on)
        mine, other = sems
        return pltpu.make_async_remote_copy(
            src_ref=src,
            dst_ref=dst.at[(away,) + where],
            send_sem=send.at[mine],
            recv_sem=recv.at[mine + (other - mine) * away],
            device_id={"wide": tw, "narrow": tn},
            device_id_type=MESH,
        )

    def landed(buf, where, send, recv, mine):
        return pltpu.make_async_remote_copy(
            src_ref=buf.at[(0,) + where],
            dst_ref=buf.at[(0,) + where],
            send_sem=send.at[mine],
            recv_sem=recv.at[mine],
            device_id={"wide": w, "narrow": n},
            device_id_type=MESH,
        )

    own_f = pltpu.make_async_copy(res, f0.at[:, 4:20, 0:16, :], local_sem.at[0])
    own_k = pltpu.make_async_copy(stiff, k0.at[4:20, 0:16, :], local_sem.at[1])
    own_c = pltpu.make_async_copy(coup_hbm, coup_ref, local_sem.at[2])
    own_f.start()
    own_k.start()
    own_c.start()

    g1[...] = jnp.zeros_like(g1)
    h3[...] = jnp.zeros_like(h3)
    h3s[...] = jnp.zeros_like(h3s)

    def tell(sem, offsets):
        for ow, on in offsets:
            tw, tn, _ = target(ow, on)
            pl.semaphore_signal(
                sem,
                inc=1,
                device_id={"wide": tw, "narrow": tn},
                device_id_type=MESH,
            )

    barrier = pltpu.get_barrier_semaphore()
    tell(barrier, AXIAL)
    g2[...] = jnp.zeros_like(g2)
    own_f.wait()
    own_k.wait()
    pl.semaphore_wait(barrier, len(AXIAL))

    def copies0(i, ow, on):
        sx, dx = {0: (0, 4), 1: (12, 0), -1: (0, 20)}[ow]
        sy, dy = {0: (0, 0), 1: (12, 20), -1: (0, 16)}[on]
        nx, ny = (16 if ow == 0 else 4), (16 if on == 0 else 4)
        fs = (slice(None), slice(4 + sx, 4 + sx + nx), slice(sy, sy + ny))
        fd = (slice(None), slice(dx, dx + nx), slice(dy, dy + ny))
        if ow > 0:
            sx, dx = sx + 1, dx + 1
        if on > 0:
            sy, dy = sy + 1, dy + 1
        nx, ny = (16 if ow == 0 else 3), (16 if on == 0 else 3)
        ks = (slice(4 + sx, 4 + sx + nx), slice(sy, sy + ny))
        kd = (slice(dx, dx + nx), slice(dy, dy + ny))
        return [
            (f0.at[fs], f0b, fd, s0, q0, i),
            (k0.at[ks], k0b, kd, s0, q0, 8 + i),
        ]

    def copies1(i, ow, on):
        sx, dx = {0: ((2, 6), (2, 6)), 1: ((4, 6), (0, 2)), -1: ((2, 4), (6, 8))}[ow]
        sy, dy = {0: ((0, 8), (0, 8)), 1: ((4, 8), (12, 16)), -1: ((0, 4), (8, 12))}[on]
        sx, dx, sy, dy = slice(*sx), slice(*dx), slice(*sy), slice(*dy)
        return [
            (g1.at[0:3, sx, sy], g1b, (slice(0, 3), dx, dy), s1, q1, i),
            (g1.at[3, sx, sy], g1b, (3, dx, dy), s1, q1, 8 + i),
        ]

    def copies2(i, ow, on):
        dx = slice(4 - 4 * ow, 8 - 4 * ow)
        dy = slice(128 - 128 * on, 256 - 128 * on)
        return [(g2.at[:, 4:8, 128:256], g2b, (slice(None), dx, dy), s2, q2, i)]

    def copies3(i, ow, on):
        rows = slice(10 - 2 * ow, 12 - 2 * ow)
        return [(h3.at[10:12, :], h3b, (rows,), s3, q3, i)]

    def copies4(i, ow, on):
        rows = slice(0, 22)
        return [(h3.at[rows], h3sb, (5 - on, rows), s4, q4, i)]

    def start(copies, offsets, chosen=None, part=slice(None)):
        for i, (ow, on) in enumerate(offsets):
            if chosen is None or i in chosen:
                opposite = offsets.index((-ow, -on))
                for src, dst, where, send, recv, mine in copies(i, ow, on)[part]:
                    sems = mine, mine + opposite - i
                    remote(src, dst, where, send, recv, sems, ow, on).start()

    def arrive(copies, offsets, chosen=None):
        for i, (ow, on) in enumerate(offsets):
            if chosen is None or i in chosen:
                for src, dst, where, send, recv, mine in copies(i, ow, on):
                    landed(dst, where, send, recv, mine).wait_recv()

    def sent(copies, offsets):
        for i, (ow, on) in enumerate(offsets):
            for src, dst, where, send, recv, mine in copies(i, ow, on):
                landed(dst, where, send, recv, mine).wait_send()

    along_wide = [(o, 0) for o in WINDOW]
    along_narrow = [(0, o) for o in WINDOW]
    for ow, on in along_wide + along_narrow:
        target(ow, on)

    start(copies0, NEIGHBOURS, (4, 5), slice(0, 1))
    start(copies0, NEIGHBOURS, (6, 7))
    tell(ready_sem, AXIAL)
    pl.semaphore_wait(ready_sem, len(AXIAL))
    start(copies0, NEIGHBOURS, (0, 1, 2, 3))
    start(copies0, NEIGHBOURS, (4, 5), slice(1, 2))

    @pl.when(w == 0)
    def _():
        f0[:, 0:4] = jnp.zeros((3, 4, 24, 128), F32)
        k0[0:4] = jnp.zeros((4, 24, 128), F32)

    @pl.when(w == nw - 1)
    def _():
        f0[:, 20:24] = jnp.zeros((3, 4, 24, 128), F32)
        k0[20:24] = jnp.zeros((4, 24, 128), F32)

    @pl.when(n == 0)
    def _():
        f0[:, :, 20:24, :] = jnp.zeros((3, 24, 4, 128), F32)
        k0[:, 20:24, :] = jnp.zeros((24, 4, 128), F32)

    @pl.when(n == nn - 1)
    def _():
        f0[:, :, 16:20, :] = jnp.zeros((3, 24, 4, 128), F32)
        k0[:, 16:20, :] = jnp.zeros((24, 4, 128), F32)

    r, c = iota((256, 128), 0), iota((256, 128), 1)
    m01[...] = indicator(((r >> 7) == (c >> 6)) & (((r & 127) >> 1) == (c & 63)), 0.125)
    r, c = iota((512, 128), 0), iota((512, 128), 1)
    m12[...] = indicator(((r >> 7) == (c >> 5)) & (((r & 63) >> 1) == (c & 31)), 0.125)
    m23[...] = indicator(
        ((r >> 7) == (c >> 5))
        & (((r >> 6) & 1) == ((c >> 4) & 1))
        & (((r & 31) >> 1) == (c & 15)),
        0.125,
    )
    r, c = iota((384, 128), 0), iota((384, 128), 1)
    m34[...] = indicator(((r >> 5) == (c >> 3)) & (((r & 15) >> 1) == (c & 7)), 0.125)
    r, c = iota((128, 256), 0), iota((128, 256), 1)
    p1[...] = indicator(((r >> 6) == (c >> 7)) & ((r & 63) == ((c & 127) >> 1)))
    r, c = iota((128, 512), 0), iota((128, 512), 1)
    p2[...] = indicator(((r >> 5) == (c >> 7)) & ((r & 31) == ((c & 127) >> 2)))
    r, c = iota((256, 256), 0), iota((256, 256), 1)
    fine = ((r >> 4) == (2 + (c >> 7))) & ((r & 15) == ((c & 127) >> 3))
    coarse = (r >= 128 + 40) & (r < 128 + 48) & ((r & 7) == ((c & 127) >> 4))
    p34[...] = indicator(fine | coarse)

    own_c.wait()
    coup = [[coup_ref[i, j] for j in range(3)] for i in range(3)]

    for i in range(8):
        t0[pl.ds(384 + 16 * i, 16), :] = (
            k0[4 + 2 * i, 0:16, :] + k0[5 + 2 * i, 0:16, :]
        )

    def halved(first, count):
        s = t0[pl.ds(first, count, stride=2), :] + t0[pl.ds(first + 1, count, stride=2), :]
        s = s.reshape(count // 16, 2, 8, 128)
        pair = [s[:, u].reshape(count // 2, 128) for u in range(2)]
        return mm(jnp.concatenate(pair, axis=1), m01[...])

    g1[3, 2:6, 0:8, :] = halved(384, 64).reshape(4, 8, 128)
    for p in range(4):
        t1[pl.ds(96 + 8 * p, 8), :] = g1[3, 2 + p, 0:8, :]

    theta0, steps0 = chebyshev(0)
    lane24 = iota((24, 128), 1)
    lane16 = iota((16, 128), 1)
    fields = [f0, d1, d2, d3]

    def sweep0(k, starts, count):
        d = fields[k]
        over = 1.0 / theta0 if k == 0 else 1.0
        scale, mass = over / 26.0, over * MASS
        rest = f0 if k == 0 else r0
        rows, lane = (24, lane24) if k < 3 else (16, lane16)
        for lo in starts:
            for i in range(lo, lo + count, 2):
                mids, boxes = [[], []], [[], []]
                for c in range(3):
                    a, b = d[c, i], d[c, i + 1]
                    both = a + b
                    for u, (mid, x) in enumerate(((a, d[c, i - 1]), (b, d[c, i + 2]))):
                        s = both + x
                        s = s + pltpu.roll(s, 1, 0) + pltpu.roll(s, 23, 0)
                        s = s[0:rows]
                        s = (
                            s
                            + jnp.where(lane == 0, 0.0, pltpu.roll(s, 1, 1))
                            + jnp.where(lane == 127, 0.0, pltpu.roll(s, 127, 1))
                        )
                        mids[u].append(mid[0:rows])
                        boxes[u].append(s)
                new = []
                for u in range(2):
                    us = [27.0 * mids[u][c] - boxes[u][c] for c in range(3)]
                    a = mix(coup, scale, mass, us, mids[u], k0[i + u, 0:rows])
                    new.append([rest[c, i + u, 0:rows] - a[c] for c in range(3)])
                    if k < 3:
                        ca, cb = steps0[k]
                        for c in range(3):
                            r0[c, i + u] = new[u][c]
                            fields[k + 1][c, i + u] = (ca * over) * mids[u][c] + cb * new[u][c]
                if k == 3:
                    for c in range(3):
                        t0[pl.ds(128 * c + 8 * (i - 4), 16), :] = new[0][c] + new[1][c]

    arrive(copies0, NEIGHBOURS, (6, 7))
    for k in range(4):
        sweep0(k, (5 + k,), 14 - 2 * k)
    start(copies1, NEIGHBOURS, None, slice(1, 2))
    arrive(copies0, NEIGHBOURS, (0, 1, 2, 3, 4, 5))
    for k in range(4):
        sweep0(k, (1 + k, 19 - k), 4)
    g1[0:3, 2:6, 0:8, :] = halved(0, 192).reshape(3, 4, 8, 128)
    start(copies1, NEIGHBOURS, None, slice(0, 1))
    sent(copies0, NEIGHBOURS)

    def sum0(i, carry):
        for c in range(3):
            acc[c][i] = (
                f0[c, 4 + i, 0:16, :] * (1.0 / theta0)
                + d1[c, 4 + i, 0:16, :]
                + d2[c, 4 + i, 0:16, :]
                + d3[c, 4 + i, 0:16, :]
            )
        return carry

    lax.fori_loop(0, 16, sum0, 0)

    arrive(copies1, NEIGHBOURS)

    theta1, steps1 = chebyshev(1)
    lower = lane16 < 64
    zpos1 = lane16 & 63

    def plane1(p, d, scale, mass):
        us, mids = [], []
        for c in range(3):
            mid = d[c, p]
            swap = mid + jnp.where(lower, d[c, min(p + 1, 7)], d[c, max(p - 1, 0)])
            up = pltpu.roll(mid, 1, 1) + pltpu.roll(swap, 65, 1)
            down = pltpu.roll(mid, 127, 1) + pltpu.roll(swap, 63, 1)
            s = mid + pltpu.roll(swap, 64, 1)
            s = s + jnp.where(zpos1 == 0, 0.0, up) + jnp.where(zpos1 == 63, 0.0, down)
            s = s + pltpu.roll(s, 1, 0) + pltpu.roll(s, 15, 0)
            us.append(27.0 * mid - s)
            mids.append(mid)
        return mids, mix(coup, scale, mass, us, mids, g1[3, p])

    x1 = {}
    fields1 = [g1, e1, e2, e1]
    for k, (lo, hi) in enumerate([(0, 8), (1, 7), (1, 7), (2, 6)]):
        d = fields1[k]
        over = 1.0 / theta1 if k == 0 else 1.0
        scale, mass = over / (4.0 * 26.0), over * MASS
        for p in range(lo, hi):
            mids, a = plane1(p, d, scale, mass)
            for c in range(3):
                new = (g1 if k == 0 else r1)[c, p] - a[c]
                if k < 3:
                    ca, cb = steps1[k]
                    r1[c, p] = new
                    fields1[k + 1][c, p] = (ca * over) * mids[c] + cb * new
                else:
                    t1[pl.ds(32 * c + 8 * (p - 2), 8), :] = new[0:8]
                if 2 <= p < 6:
                    part = (mids[c] * over)[0:8]
                    x1[c, p] = part if k == 0 else x1[c, p] + part

    ys = [t1[pl.ds(y, 16, stride=8), :] for y in range(8)]
    ys = jnp.concatenate([ys[2 * j] + ys[2 * j + 1] for j in range(4)], axis=1)
    blk = mm(ys, m12[...])
    for c in range(4):
        g2[c, 4:8, 128:256] = blk[4 * c : 4 * c + 4]
    start(copies2, NEIGHBOURS)
    sent(copies1, NEIGHBOURS)

    rows = jnp.concatenate([x1[c, p] for c in range(3) for p in range(2, 6)], axis=0)
    rep = mm(rows, p1[...])
    u_lo[pl.ds(0, 96, stride=2), :] = rep[:, 0:128]
    u_lo[pl.ds(1, 96, stride=2), :] = rep[:, 0:128]
    u_hi[pl.ds(0, 96, stride=2), :] = rep[:, 128:256]
    u_hi[pl.ds(1, 96, stride=2), :] = rep[:, 128:256]
    for c in range(3):
        for p in range(4):
            rows_cp = pl.ds(16 * (4 * c + p), 16)
            for j in range(4):
                acc[c][4 * p + j] += (u_lo if j < 2 else u_hi)[rows_cp, :]

    arrive(copies2, NEIGHBOURS)

    f2 = [[g2[c, :, 128 * j : 128 * j + 128] for j in range(3)] for c in range(4)]
    x2, r2 = flat_smooth(f2[:3], f2[3], coup, 2, 32, True)

    t2[...] = mm(
        jnp.concatenate([r2[0][1], r2[1][1], r2[2][1], f2[3][1]], axis=1), m23[...]
    )
    h3[10:12, :] = t2[pl.ds(4, 2, stride=2), :] + t2[pl.ds(5, 2, stride=2), :]
    start(copies3, along_wide)
    sent(copies2, NEIGHBOURS)

    for c in range(3):
        t3[4 * c : 4 * c + 4, 0:128] = x2[c][1][4:8]
    rep = mm(t3[0:16, 0:128], p2[...])
    for y in range(16):
        j = y // 4
        v2[pl.ds(y, 16, stride=16), :] = rep[:, 128 * j : 128 * j + 128]
    for c in range(3):
        for k in range(4):
            part = v2[pl.ds(16 * (4 * c + k), 16), :]
            for j in range(4):
                acc[c][4 * k + j] += part

    arrive(copies3, along_wide)
    start(copies4, along_narrow)
    sent(copies3, along_wide)
    arrive(copies4, along_narrow)
    sent(copies4, along_narrow)

    lane3 = iota((24, 128), 1)
    slots = [h3s[j] if j != 5 else h3[...] for j in range(11)]
    f3 = [[None] * 3 for _ in range(4)]
    for c in range(4):
        for v in range(3):
            out = jnp.zeros((24, 128), F32)
            for q in range(4):
                j = 4 * v + q
                if j < 11:
                    turn = 32 * ((q - c) % 4)
                    part = pltpu.roll(slots[j], turn, 1) if turn else slots[j]
                    out = jnp.where((lane3 >> 5) == q, part, out)
            f3[c][v] = out
    x3, r3 = flat_smooth(f3[:3], f3[3], coup, 3, 16, True)

    z4[...] = mm(
        jnp.concatenate(
            [jnp.concatenate(r3[c] if c < 3 else f3[3], axis=1) for c in range(4)],
            axis=0,
        ),
        m34[...],
    )
    f4 = []
    for c in range(4):
        even, odd = (z4[pl.ds(24 * c + 4 + u, 8, stride=2), :] for u in range(2))
        f4.append([even + odd])
    x4, _ = flat_smooth(f4[:3], f4[3], coup, 4, 8, False)

    for c in range(3):
        t3[2 * c : 2 * c + 2, 0:128] = x3[c][1][10:12]
        t3[2 * c : 2 * c + 2, 128:256] = jnp.broadcast_to(x4[c][0][3:4], (2, 128))
    tail_out[...] = mm(t3[0:16, 0:256], p34[...])[0:8]


def solution(mesh):
    nw, nn = mesh.shape["wide"], mesh.shape["narrow"]

    def vm(*shape):
        return pltpu.VMEM(shape, F32)

    def mat(*shape):
        return pltpu.VMEM(shape, BF16)

    dma = pltpu.SemaphoreType.DMA
    scratch = [
        vm(2, 3, 24, 24, 128),
        vm(2, 24, 24, 128),
        vm(3, 24, 24, 128),
        vm(3, 24, 24, 128),
        vm(3, 24, 24, 128),
        vm(3, 24, 24, 128),
        vm(512, 128),
        vm(2, 4, 8, 16, 128),
        vm(3, 8, 16, 128),
        vm(3, 8, 16, 128),
        vm(3, 8, 16, 128),
        vm(128, 128),
        vm(192, 128),
        vm(192, 128),
        vm(2, 4, 16, 384),
        vm(16, 128),
        vm(256, 128),
        vm(2, 24, 128),
        vm(2, 11, 24, 128),
        vm(16, 256),
        vm(96, 128),
        mat(256, 128),
        mat(512, 128),
        mat(512, 128),
        mat(384, 128),
        mat(128, 256),
        mat(128, 512),
        mat(256, 256),
        pltpu.SMEM((3, 3), F32),
        dma((3,)),
        pltpu.SemaphoreType.REGULAR,
        dma((16,)),
        dma((16,)),
        dma((16,)),
        dma((16,)),
        dma((8,)),
        dma((8,)),
        dma((10,)),
        dma((10,)),
        dma((10,)),
        dma((10,)),
    ]

    def per_device(residual, stiffness, coupling):
        hbm = pl.BlockSpec(memory_space=pltpu.HBM)
        vmem = pl.BlockSpec(memory_space=pltpu.VMEM)
        *acc, tail = pl.pallas_call(
            functools.partial(kernel, nw, nn),
            out_shape=(
                *[jax.ShapeDtypeStruct((16, 16, 128), F32)] * 3,
                jax.ShapeDtypeStruct((8, 256), F32),
            ),
            in_specs=[hbm, hbm, hbm],
            out_specs=(vmem,) * 4,
            scratch_shapes=scratch,
            compiler_params=pltpu.CompilerParams(
                collective_id=0,
                has_side_effects=True,
                vmem_limit_bytes=(53 * 1024 + 450) * 1024,
            ),
        )(residual, stiffness, coupling)
        tail = tail[0:6].reshape(3, 2, 1, 2, 1, 128)
        return (jnp.stack(acc).reshape(3, 2, 8, 2, 8, 128) + tail).reshape(3, 16, 16, 128)

    return jax.shard_map(
        per_device,
        mesh=mesh,
        in_specs=(P(None, "wide", "narrow", None), P("wide", "narrow", None), P()),
        out_specs=P(None, "wide", "narrow", None),
        check_vma=False,
    )
```

```python
import functools

import jax
import jax.numpy as jnp
from jax import lax
from jax.experimental import pallas as pl
from jax.experimental.pallas import tpu as pltpu
from jax.sharding import PartitionSpec as P

LEVELS = 4
MASS = 0.001
RATIO = 8.0
MESH = pl.DeviceIdType.MESH
NEIGHBOURS = [(1, 1), (1, -1), (-1, 1), (-1, -1), (1, 0), (-1, 0), (0, 1), (0, -1)]
AXIAL = NEIGHBOURS[4:]
WINDOW = [o for k in range(5, 0, -1) for o in (k, -k)]
F32 = jnp.float32
BF16 = jnp.bfloat16


def chebyshev(level):
    top = 4.0 * (2.8 / 4.0**level + MASS)
    theta = (top + top / RATIO) / 2.0
    delta = (top - top / RATIO) / 2.0
    sigma = theta / delta
    rho = 1.0 / sigma
    steps = []
    for _ in range(3):
        nxt = 1.0 / (2.0 * sigma - rho)
        steps.append((nxt * rho, 2.0 * nxt / delta))
        rho = nxt
    return theta, steps


def iota(shape, dim):
    return lax.broadcasted_iota(jnp.int32, shape, dim)


def indicator(cond, value=1.0):
    return jnp.where(cond, value, 0.0).astype(BF16)


def mm(v, w):
    hi = v.astype(BF16)
    lo = (v - hi.astype(F32)).astype(BF16)
    return jnp.dot(hi, w, preferred_element_type=F32) + jnp.dot(
        lo, w, preferred_element_type=F32
    )


def mix(coup, scale, mass, u, d, k):
    out = []
    for c in range(3):
        a = (coup[c][0] * scale) * u[0]
        a = a + (coup[c][1] * scale) * u[1]
        a = a + (coup[c][2] * scale) * u[2]
        a = a + mass * d[c]
        out.append(k * a)
    return out


def flat_box(chunks, nz):
    rows = chunks[0].shape[0]
    lane = iota(chunks[0].shape, 1)
    zpos = lane & (nz - 1)
    s = []
    for v in chunks:
        v = v + pltpu.roll(v, 1, 0) + pltpu.roll(v, rows - 1, 0)
        s.append(
            v
            + jnp.where(zpos == 0, 0.0, pltpu.roll(v, 1, 1))
            + jnp.where(zpos == nz - 1, 0.0, pltpu.roll(v, 127, 1))
        )
    up = [pltpu.roll(v, nz, 1) for v in s]
    down = [pltpu.roll(v, 128 - nz, 1) for v in s]
    out = []
    for j, v in enumerate(s):
        before = up[j - 1] if j > 0 else 0.0
        after = down[j + 1] if j + 1 < len(s) else 0.0
        out.append(
            v
            + jnp.where(lane < nz, before, up[j])
            + jnp.where(lane >= 128 - nz, after, down[j])
        )
    return out


def flat_box_wide(chunks, nz):
    rows = chunks[0].shape[0]
    lane = iota(chunks[0].shape, 1)
    zpos = lane & (nz - 1)

    def shifted(v, y):
        mid = pltpu.roll(v, y % 128, 1) if y else v
        return (
            mid
            + jnp.where(zpos == 0, 0.0, pltpu.roll(v, (y + 1) % 128, 1))
            + jnp.where(zpos == nz - 1, 0.0, pltpu.roll(v, (y - 1) % 128, 1))
        )

    xs = [v + pltpu.roll(v, 1, 0) + pltpu.roll(v, rows - 1, 0) for v in chunks]
    up = [shifted(v, nz) for v in xs]
    down = [shifted(v, -nz) for v in xs]
    out = []
    for j, v in enumerate(xs):
        before = up[j - 1] if j > 0 else 0.0
        after = down[j + 1] if j + 1 < len(xs) else 0.0
        out.append(
            shifted(v, 0)
            + jnp.where(lane < nz, before, up[j])
            + jnp.where(lane >= 128 - nz, after, down[j])
        )
    return out


def flat_smooth(f, kappa, coup, level, nz, want_rest):
    theta, steps = chebyshev(level)
    scale = 4.0**-level / 26.0
    n = len(kappa)

    def apply(r, d):
        box = flat_box if n > 1 else flat_box_wide
        boxes = [box(d[c], nz) for c in range(3)]
        new = [[None] * n for _ in range(3)]
        for j in range(n):
            u = [27.0 * d[c][j] - boxes[c][j] for c in range(3)]
            a = mix(coup, scale, MASS, u, [d[c][j] for c in range(3)], kappa[j])
            for c in range(3):
                new[c][j] = r[c][j] - a[c]
        return new

    r = f
    d = [[v * (1.0 / theta) for v in f[c]] for c in range(3)]
    x = d
    for a, b in steps:
        r = apply(r, d)
        d = [[a * d[c][j] + b * r[c][j] for j in range(n)] for c in range(3)]
        x = [[x[c][j] + d[c][j] for j in range(n)] for c in range(3)]
    if want_rest:
        r = apply(r, d)
    return x, r


def kernel(
    nw,
    nn,
    res,
    stiff,
    coup_hbm,
    acc0,
    acc1,
    acc2,
    tail_out,
    f0b,
    k0b,
    r0,
    d1,
    d2,
    d3,
    t0,
    g1b,
    r1,
    e1,
    e2,
    t1,
    u_lo,
    u_hi,
    g2b,
    t2,
    v2,
    h3b,
    h3sb,
    t3,
    z4,
    m01,
    m12,
    m23,
    m34,
    p1,
    p2,
    p34,
    coup_ref,
    local_sem,
    ready_sem,
    s0,
    q0,
    s1,
    q1,
    s2,
    q2,
    s3,
    q3,
    s4,
    q4,
):
    w = lax.axis_index("wide")
    n = lax.axis_index("narrow")
    acc = [acc0, acc1, acc2]
    f0, k0, g1, g2, h3, h3s = (b.at[0] for b in (f0b, k0b, g1b, g2b, h3b, h3sb))

    def pair_of(i):
        return i + 1 - 2 * lax.rem(i, 2)

    def out_of(pos, off, size):
        if off == 0:
            return jnp.bool_(False)
        return pos + off >= size if off > 0 else pos + off < 0

    targets = {}

    def target(ow, on):
        if (ow, on) in targets:
            return targets[ow, on]
        w_out, n_out = out_of(w, ow, nw), out_of(n, on, nn)
        if on == 0:
            tw = jnp.where(w_out, w, w + ow)
            tn = jnp.where(w_out, pair_of(n), n)
            away = w_out
        elif ow == 0:
            tw = jnp.where(n_out, pair_of(w), w)
            tn = jnp.where(n_out, n, n + on)
            away = n_out
        else:
            w_end, n_end = (nw - 1 if ow > 0 else 0), (nn - 1 if on > 0 else 0)
            both = jnp.logical_and(w_out, n_out)
            away = jnp.logical_or(w_out, n_out)
            w_near, n_near = w == w_end - ow, n == n_end - on
            tw = jnp.where(
                both,
                w - ow,
                jnp.where(
                    w_out,
                    w,
                    jnp.where(n_out, jnp.where(w_near, w + ow, pair_of(w)), w + ow),
                ),
            )
            tn = jnp.where(
                both,
                n,
                jnp.where(
                    w_out,
                    jnp.where(n_near, n + on, pair_of(n)),
                    jnp.where(n_out, jnp.where(w_near, n - on, n), n + on),
                ),
            )
        targets[ow, on] = tw, tn, jnp.where(away, 1, 0)
        return targets[ow, on]

    def remote(src, dst, where, send, recv, sems, ow, on):
        tw, tn, away = target(ow, on)
        mine, other = sems
        return pltpu.make_async_remote_copy(
            src_ref=src,
            dst_ref=dst.at[(away,) + where],
            send_sem=send.at[mine],
            recv_sem=recv.at[mine + (other - mine) * away],
            device_id={"wide": tw, "narrow": tn},
            device_id_type=MESH,
        )

    def landed(buf, where, send, recv, mine):
        return pltpu.make_async_remote_copy(
            src_ref=buf.at[(0,) + where],
            dst_ref=buf.at[(0,) + where],
            send_sem=send.at[mine],
            recv_sem=recv.at[mine],
            device_id={"wide": w, "narrow": n},
            device_id_type=MESH,
        )

    own_f = pltpu.make_async_copy(res, f0.at[:, 4:20, 0:16, :], local_sem.at[0])
    own_k = pltpu.make_async_copy(stiff, k0.at[4:20, 0:16, :], local_sem.at[1])
    own_c = pltpu.make_async_copy(coup_hbm, coup_ref, local_sem.at[2])
    own_f.start()
    own_k.start()
    own_c.start()

    h3[...] = jnp.zeros_like(h3)
    h3s[...] = jnp.zeros_like(h3s)

    def tell(sem, offsets):
        for ow, on in offsets:
            tw, tn, _ = target(ow, on)
            pl.semaphore_signal(
                sem,
                inc=1,
                device_id={"wide": tw, "narrow": tn},
                device_id_type=MESH,
            )

    barrier = pltpu.get_barrier_semaphore()
    tell(barrier, AXIAL)
    g1[...] = jnp.zeros_like(g1)
    g2[...] = jnp.zeros_like(g2)
    own_f.wait()
    own_k.wait()
    pl.semaphore_wait(barrier, len(AXIAL))

    def copies0(i, ow, on):
        sx, dx = {0: (0, 4), 1: (12, 0), -1: (0, 20)}[ow]
        sy, dy = {0: (0, 0), 1: (12, 20), -1: (0, 16)}[on]
        nx, ny = (16 if ow == 0 else 4), (16 if on == 0 else 4)
        fs = (slice(None), slice(4 + sx, 4 + sx + nx), slice(sy, sy + ny))
        fd = (slice(None), slice(dx, dx + nx), slice(dy, dy + ny))
        if ow > 0:
            sx, dx = sx + 1, dx + 1
        if on > 0:
            sy, dy = sy + 1, dy + 1
        nx, ny = (16 if ow == 0 else 3), (16 if on == 0 else 3)
        ks = (slice(4 + sx, 4 + sx + nx), slice(sy, sy + ny))
        kd = (slice(dx, dx + nx), slice(dy, dy + ny))
        return [
            (f0.at[fs], f0b, fd, s0, q0, i),
            (k0.at[ks], k0b, kd, s0, q0, 8 + i),
        ]

    def copies1(i, ow, on):
        sx, dx = {0: ((2, 6), (2, 6)), 1: ((4, 6), (0, 2)), -1: ((2, 4), (6, 8))}[ow]
        sy, dy = {0: ((0, 8), (0, 8)), 1: ((4, 8), (12, 16)), -1: ((0, 4), (8, 12))}[on]
        sx, dx, sy, dy = slice(*sx), slice(*dx), slice(*sy), slice(*dy)
        return [
            (g1.at[0:3, sx, sy], g1b, (slice(0, 3), dx, dy), s1, q1, i),
            (g1.at[3, sx, sy], g1b, (3, dx, dy), s1, q1, 8 + i),
        ]

    def copies2(i, ow, on):
        dx = slice(4 - 4 * ow, 8 - 4 * ow)
        dy = slice(128 - 128 * on, 256 - 128 * on)
        return [(g2.at[:, 4:8, 128:256], g2b, (slice(None), dx, dy), s2, q2, i)]

    def copies3(i, ow, on):
        rows = slice(10 - 2 * ow, 12 - 2 * ow)
        return [(h3.at[10:12, :], h3b, (rows,), s3, q3, i)]

    def copies4(i, ow, on):
        rows = slice(0, 22)
        return [(h3.at[rows], h3sb, (5 - on, rows), s4, q4, i)]

    def start(copies, offsets, chosen=None, part=slice(None)):
        for i, (ow, on) in enumerate(offsets):
            if chosen is None or i in chosen:
                opposite = offsets.index((-ow, -on))
                for src, dst, where, send, recv, mine in copies(i, ow, on)[part]:
                    sems = mine, mine + opposite - i
                    remote(src, dst, where, send, recv, sems, ow, on).start()

    def arrive(copies, offsets, chosen=None):
        for i, (ow, on) in enumerate(offsets):
            if chosen is None or i in chosen:
                for src, dst, where, send, recv, mine in copies(i, ow, on):
                    landed(dst, where, send, recv, mine).wait_recv()

    def sent(copies, offsets):
        for i, (ow, on) in enumerate(offsets):
            for src, dst, where, send, recv, mine in copies(i, ow, on):
                landed(dst, where, send, recv, mine).wait_send()

    along_wide = [(o, 0) for o in WINDOW]
    along_narrow = [(0, o) for o in WINDOW]

    start(copies0, NEIGHBOURS, (4, 5), slice(0, 1))
    start(copies0, NEIGHBOURS, (6, 7))
    tell(ready_sem, AXIAL)
    pl.semaphore_wait(ready_sem, len(AXIAL))
    start(copies0, NEIGHBOURS, (0, 1, 2, 3))
    start(copies0, NEIGHBOURS, (4, 5), slice(1, 2))

    @pl.when(w == 0)
    def _():
        f0[:, 0:4] = jnp.zeros((3, 4, 24, 128), F32)
        k0[0:4] = jnp.zeros((4, 24, 128), F32)

    @pl.when(w == nw - 1)
    def _():
        f0[:, 20:24] = jnp.zeros((3, 4, 24, 128), F32)
        k0[20:24] = jnp.zeros((4, 24, 128), F32)

    @pl.when(n == 0)
    def _():
        f0[:, :, 20:24, :] = jnp.zeros((3, 24, 4, 128), F32)
        k0[:, 20:24, :] = jnp.zeros((24, 4, 128), F32)

    @pl.when(n == nn - 1)
    def _():
        f0[:, :, 16:20, :] = jnp.zeros((3, 24, 4, 128), F32)
        k0[:, 16:20, :] = jnp.zeros((24, 4, 128), F32)

    r, c = iota((256, 128), 0), iota((256, 128), 1)
    m01[...] = indicator(((r >> 7) == (c >> 6)) & (((r & 127) >> 1) == (c & 63)), 0.125)
    r, c = iota((512, 128), 0), iota((512, 128), 1)
    m12[...] = indicator(((r >> 7) == (c >> 5)) & (((r & 63) >> 1) == (c & 31)), 0.125)
    m23[...] = indicator(
        ((r >> 7) == (c >> 5))
        & (((r >> 6) & 1) == ((c >> 4) & 1))
        & (((r & 31) >> 1) == (c & 15)),
        0.125,
    )
    r, c = iota((384, 128), 0), iota((384, 128), 1)
    m34[...] = indicator(((r >> 5) == (c >> 3)) & (((r & 15) >> 1) == (c & 7)), 0.125)
    r, c = iota((128, 256), 0), iota((128, 256), 1)
    p1[...] = indicator(((r >> 6) == (c >> 7)) & ((r & 63) == ((c & 127) >> 1)))
    r, c = iota((128, 512), 0), iota((128, 512), 1)
    p2[...] = indicator(((r >> 5) == (c >> 7)) & ((r & 31) == ((c & 127) >> 2)))
    r, c = iota((256, 256), 0), iota((256, 256), 1)
    fine = ((r >> 4) == (2 + (c >> 7))) & ((r & 15) == ((c & 127) >> 3))
    coarse = (r >= 128 + 40) & (r < 128 + 48) & ((r & 7) == ((c & 127) >> 4))
    p34[...] = indicator(fine | coarse)

    own_c.wait()
    coup = [[coup_ref[i, j] for j in range(3)] for i in range(3)]

    for i in range(8):
        t0[pl.ds(384 + 16 * i, 16), :] = (
            k0[4 + 2 * i, 0:16, :] + k0[5 + 2 * i, 0:16, :]
        )

    def halved(first, count):
        s = t0[pl.ds(first, count, stride=2), :] + t0[pl.ds(first + 1, count, stride=2), :]
        s = s.reshape(count // 16, 2, 8, 128)
        pair = [s[:, u].reshape(count // 2, 128) for u in range(2)]
        return mm(jnp.concatenate(pair, axis=1), m01[...])

    g1[3, 2:6, 0:8, :] = halved(384, 64).reshape(4, 8, 128)
    for p in range(4):
        t1[pl.ds(96 + 8 * p, 8), :] = g1[3, 2 + p, 0:8, :]

    theta0, steps0 = chebyshev(0)
    lane24 = iota((24, 128), 1)
    lane16 = iota((16, 128), 1)
    fields = [f0, d1, d2, d3]

    def sweep0(k, starts, count):
        d = fields[k]
        over = 1.0 / theta0 if k == 0 else 1.0
        scale, mass = over / 26.0, over * MASS
        rest = f0 if k == 0 else r0
        rows, lane = (24, lane24) if k < 3 else (16, lane16)
        for lo in starts:
            for i in range(lo, lo + count, 2):
                mids, boxes = [[], []], [[], []]
                for c in range(3):
                    a, b = d[c, i], d[c, i + 1]
                    both = a + b
                    for u, (mid, x) in enumerate(((a, d[c, i - 1]), (b, d[c, i + 2]))):
                        s = both + x
                        s = s + pltpu.roll(s, 1, 0) + pltpu.roll(s, 23, 0)
                        s = s[0:rows]
                        s = (
                            s
                            + jnp.where(lane == 0, 0.0, pltpu.roll(s, 1, 1))
                            + jnp.where(lane == 127, 0.0, pltpu.roll(s, 127, 1))
                        )
                        mids[u].append(mid[0:rows])
                        boxes[u].append(s)
                new = []
                for u in range(2):
                    us = [27.0 * mids[u][c] - boxes[u][c] for c in range(3)]
                    a = mix(coup, scale, mass, us, mids[u], k0[i + u, 0:rows])
                    new.append([rest[c, i + u, 0:rows] - a[c] for c in range(3)])
                    if k < 3:
                        ca, cb = steps0[k]
                        for c in range(3):
                            r0[c, i + u] = new[u][c]
                            fields[k + 1][c, i + u] = (ca * over) * mids[u][c] + cb * new[u][c]
                if k == 3:
                    for c in range(3):
                        t0[pl.ds(128 * c + 8 * (i - 4), 16), :] = new[0][c] + new[1][c]

    arrive(copies0, NEIGHBOURS, (6, 7))
    for k in range(4):
        sweep0(k, (5 + k,), 14 - 2 * k)
    arrive(copies0, NEIGHBOURS, (0, 1, 2, 3, 4, 5))
    start(copies1, NEIGHBOURS, None, slice(1, 2))
    for k in range(4):
        sweep0(k, (1 + k, 19 - k), 4)
    g1[0:3, 2:6, 0:8, :] = halved(0, 192).reshape(3, 4, 8, 128)
    start(copies1, NEIGHBOURS, None, slice(0, 1))
    sent(copies0, NEIGHBOURS)

    def sum0(i, carry):
        for c in range(3):
            acc[c][i] = (
                f0[c, 4 + i, 0:16, :] * (1.0 / theta0)
                + d1[c, 4 + i, 0:16, :]
                + d2[c, 4 + i, 0:16, :]
                + d3[c, 4 + i, 0:16, :]
            )
        return carry

    lax.fori_loop(0, 16, sum0, 0)

    arrive(copies1, NEIGHBOURS)

    theta1, steps1 = chebyshev(1)
    lower = lane16 < 64
    zpos1 = lane16 & 63

    def plane1(p, d, scale, mass):
        us, mids = [], []
        for c in range(3):
            mid = d[c, p]
            swap = mid + jnp.where(lower, d[c, min(p + 1, 7)], d[c, max(p - 1, 0)])
            up = pltpu.roll(mid, 1, 1) + pltpu.roll(swap, 65, 1)
            down = pltpu.roll(mid, 127, 1) + pltpu.roll(swap, 63, 1)
            s = mid + pltpu.roll(swap, 64, 1)
            s = s + jnp.where(zpos1 == 0, 0.0, up) + jnp.where(zpos1 == 63, 0.0, down)
            s = s + pltpu.roll(s, 1, 0) + pltpu.roll(s, 15, 0)
            us.append(27.0 * mid - s)
            mids.append(mid)
        return mids, mix(coup, scale, mass, us, mids, g1[3, p])

    x1 = {}
    fields1 = [g1, e1, e2, e1]
    for k, (lo, hi) in enumerate([(0, 8), (1, 7), (1, 7), (2, 6)]):
        d = fields1[k]
        over = 1.0 / theta1 if k == 0 else 1.0
        scale, mass = over / (4.0 * 26.0), over * MASS
        for p in range(lo, hi):
            mids, a = plane1(p, d, scale, mass)
            for c in range(3):
                new = (g1 if k == 0 else r1)[c, p] - a[c]
                if k < 3:
                    ca, cb = steps1[k]
                    r1[c, p] = new
                    fields1[k + 1][c, p] = (ca * over) * mids[c] + cb * new
                else:
                    t1[pl.ds(32 * c + 8 * (p - 2), 8), :] = new[0:8]
                if 2 <= p < 6:
                    part = (mids[c] * over)[0:8]
                    x1[c, p] = part if k == 0 else x1[c, p] + part

    ys = [t1[pl.ds(y, 16, stride=8), :] for y in range(8)]
    ys = jnp.concatenate([ys[2 * j] + ys[2 * j + 1] for j in range(4)], axis=1)
    blk = mm(ys, m12[...])
    for c in range(4):
        g2[c, 4:8, 128:256] = blk[4 * c : 4 * c + 4]
    start(copies2, NEIGHBOURS)
    sent(copies1, NEIGHBOURS)

    rows = jnp.concatenate([x1[c, p] for c in range(3) for p in range(2, 6)], axis=0)
    rep = mm(rows, p1[...])
    u_lo[pl.ds(0, 96, stride=2), :] = rep[:, 0:128]
    u_lo[pl.ds(1, 96, stride=2), :] = rep[:, 0:128]
    u_hi[pl.ds(0, 96, stride=2), :] = rep[:, 128:256]
    u_hi[pl.ds(1, 96, stride=2), :] = rep[:, 128:256]
    for c in range(3):
        for p in range(4):
            rows_cp = pl.ds(16 * (4 * c + p), 16)
            for j in range(4):
                acc[c][4 * p + j] += (u_lo if j < 2 else u_hi)[rows_cp, :]

    arrive(copies2, NEIGHBOURS)

    f2 = [[g2[c, :, 128 * j : 128 * j + 128] for j in range(3)] for c in range(4)]
    x2, r2 = flat_smooth(f2[:3], f2[3], coup, 2, 32, True)

    t2[0:16, :] = mm(
        jnp.concatenate([r2[0][1], r2[1][1], r2[2][1], f2[3][1]], axis=1), m23[...]
    )
    h3[10:12, :] = t2[pl.ds(4, 2, stride=2), :] + t2[pl.ds(5, 2, stride=2), :]
    start(copies3, along_wide)
    sent(copies2, NEIGHBOURS)

    for c in range(3):
        t3[4 * c : 4 * c + 4, 0:128] = x2[c][1][4:8]
    rep = mm(t3[0:16, 0:128], p2[...])
    for y in range(16):
        j = y // 4
        v2[pl.ds(y, 16, stride=16), :] = rep[:, 128 * j : 128 * j + 128]
    for c in range(3):
        for k in range(4):
            part = v2[pl.ds(16 * (4 * c + k), 16), :]
            for j in range(4):
                acc[c][4 * k + j] += part

    arrive(copies3, along_wide)
    start(copies4, along_narrow)
    sent(copies3, along_wide)
    arrive(copies4, along_narrow)
    sent(copies4, along_narrow)

    lane3 = iota((24, 128), 1)
    slots = [h3s[j] if j != 5 else h3[...] for j in range(11)]
    f3 = [[None] * 3 for _ in range(4)]
    for c in range(4):
        for v in range(3):
            out = jnp.zeros((24, 128), F32)
            for q in range(4):
                j = 4 * v + q
                if j < 11:
                    turn = 32 * ((q - c) % 4)
                    part = pltpu.roll(slots[j], turn, 1) if turn else slots[j]
                    out = jnp.where((lane3 >> 5) == q, part, out)
            f3[c][v] = out
    x3, r3 = flat_smooth(f3[:3], f3[3], coup, 3, 16, True)

    z4[0:96, :] = mm(
        jnp.concatenate(
            [jnp.concatenate(r3[c] if c < 3 else f3[3], axis=1) for c in range(4)],
            axis=0,
        ),
        m34[...],
    )
    f4 = []
    for c in range(4):
        even, odd = (z4[pl.ds(24 * c + 4 + u, 8, stride=2), :] for u in range(2))
        f4.append([even + odd])
    x4, _ = flat_smooth(f4[:3], f4[3], coup, 4, 8, False)

    for c in range(3):
        t3[2 * c : 2 * c + 2, 0:128] = x3[c][1][10:12]
        t3[2 * c : 2 * c + 2, 128:256] = jnp.broadcast_to(x4[c][0][3:4], (2, 128))
    tail_out[...] = mm(t3[0:16, 0:256], p34[...])[0:8]


def solution(mesh):
    nw, nn = mesh.shape["wide"], mesh.shape["narrow"]

    def vm(*shape):
        return pltpu.VMEM(shape, F32)

    def mat(*shape):
        return pltpu.VMEM(shape, BF16)

    dma = pltpu.SemaphoreType.DMA
    scratch = [
        vm(2, 3, 24, 24, 128),
        vm(2, 24, 24, 128),
        vm(3, 24, 24, 128),
        vm(3, 24, 24, 128),
        vm(3, 24, 24, 128),
        vm(3, 24, 24, 128),
        vm(528, 128),
        vm(2, 4, 8, 16, 128),
        vm(3, 8, 16, 128),
        vm(3, 8, 16, 128),
        vm(3, 8, 16, 128),
        vm(144, 128),
        vm(208, 128),
        vm(208, 128),
        vm(2, 4, 16, 384),
        vm(32, 128),
        vm(288, 128),
        vm(2, 24, 128),
        vm(2, 11, 24, 128),
        vm(16, 256),
        vm(128, 128),
        mat(256, 128),
        mat(512, 128),
        mat(512, 128),
        mat(384, 128),
        mat(128, 256),
        mat(128, 512),
        mat(256, 256),
        pltpu.SMEM((3, 3), F32),
        dma((3,)),
        pltpu.SemaphoreType.REGULAR,
        dma((16,)),
        dma((16,)),
        dma((16,)),
        dma((16,)),
        dma((8,)),
        dma((8,)),
        dma((10,)),
        dma((10,)),
        dma((10,)),
        dma((10,)),
    ]

    def per_device(residual, stiffness, coupling):
        hbm = pl.BlockSpec(memory_space=pltpu.HBM)
        vmem = pl.BlockSpec(memory_space=pltpu.VMEM)
        *acc, tail = pl.pallas_call(
            functools.partial(kernel, nw, nn),
            out_shape=(
                *[jax.ShapeDtypeStruct((16, 16, 128), F32)] * 3,
                jax.ShapeDtypeStruct((8, 256), F32),
            ),
            in_specs=[hbm, hbm, hbm],
            out_specs=(vmem,) * 4,
            scratch_shapes=scratch,
            compiler_params=pltpu.CompilerParams(
                collective_id=0,
                has_side_effects=True,
                vmem_limit_bytes=(53 * 1024 + 450) * 1024,
            ),
        )(residual, stiffness, coupling)
        tail = tail[0:6].reshape(3, 2, 1, 2, 1, 128)
        return (jnp.stack(acc).reshape(3, 2, 8, 2, 8, 128) + tail).reshape(3, 16, 16, 128)

    return jax.shard_map(
        per_device,
        mesh=mesh,
        in_specs=(P(None, "wide", "narrow", None), P("wide", "narrow", None), P()),
        out_specs=P(None, "wide", "narrow", None),
        check_vma=False,
    )
```
